32 devices in a mesh: group: 2 (over y), tile: 4 (over x, core), seq: 4 (over z).
Axes of the slice: x: 2, y: 2, z: 4, core: 2. Of those that a mesh axis runs over, the one named last changes fastest.
Arguments:
- hidden: bfloat16 [8, 1024, 3072], P(('group', 'tile'), 'seq'), parts along dimension 0
- modulation: float32 [10, 3072], P('group'), parts along dimension 0, may hold values from -3 to 3
- w_qkv: bfloat16 [3072, 9216], P('tile', 'seq')
- w_out: bfloat16 [3072, 3072], P('seq', 'tile'), may hold values from -0.109375 to 0.109375
- w_head: bfloat16 [3072, 64], replicated, may hold values from -0.109375 to 0.109375
- latent: float32 [8, 1024, 64], P(('group', 'tile'), 'seq'), parts along dimension 0, may hold values from -6 to 6
- weights_int: int32 [8, 1024], P(('group', 'tile'), 'seq'), parts along dimension 0, may hold values from 1 to 8
- step_index: int32 [2], P('group'), parts along dimension 0, may hold values from 0 to 13
Outputs:
- stepped: float32 [8, 1024, 64], P(('group', 'tile'), 'seq'), parts along dimension 0
- clean: float32 [8, 1024, 64], P(('group', 'tile'), 'seq'), parts along dimension 0
The draws below stay inside these ranges and needn't reach their ends.
There are 2 independent parts, one for each index of `group`. The reference program is written for one: setup_inputs(seed, part) draws one part's arguments, and reference() takes and returns one part's arrays. A program takes and returns all parts, laid end to end along the dimension named above; an argument that names none is the same for every part. Nothing has to cross between parts.
All inputs are finite; a program needn't handle non-finite values.
Results may differ from the reference program's by a relative error of at most 0.0055.
Values may be sent and summed in bfloat16 or wider, within the bound.
No kernel may reach another device: no remote copies, remote signals or barrier semaphores. Data moves between devices by JAX's collectives and lax.ppermute only.
A program may use at most 64 MiB of HBM per device.

```python
import math
import jax
import jax.numpy as jnp
from jax import lax

D = 3072
HEADS = 24
HD = 128
C = 64
TILE_LEN = 1024
NSTEPS = 28
TILES = 4
STRIDE = 512
N_SEQ = 4


def draw_hidden(key, part):
    first = jax.random.fold_in(key, 0)
    second = jax.random.fold_in(key, 1)
    third = jax.random.fold_in(key, 2)
    fifth = jax.random.fold_in(key, 4)
    sixth = jax.random.fold_in(key, 5)
    clusters = 16
    rows = jnp.exp(jax.random.uniform(second, (TILES, TILE_LEN, 1), jnp.float32, math.log(0.3), math.log(3.0)))
    cols = jnp.exp(jax.random.uniform(third, (1, 1, D), jnp.float32, math.log(0.3), math.log(3.0)))
    labels = jax.random.randint(fifth, (TILES, TILE_LEN, 1), 0, clusters)
    centres = jax.random.normal(sixth, (TILES, clusters, D), jnp.float32)
    noise = jax.random.normal(first, (TILES, TILE_LEN, D), jnp.float32)
    picked = jnp.take_along_axis(centres, labels, axis=1)
    base = 0.9 * picked + 0.45 * noise
    base = jnp.clip(base, -5.0, 5.0)
    return (base * rows * cols).astype(jnp.bfloat16)


def draw_w_qkv(key, part):
    first, second = jax.random.split(jax.random.fold_in(key, 17), 2)
    scale = 1.0 / math.sqrt(D)
    base = jax.random.normal(first, (D, HEADS, 3, HD), jnp.float32) * scale
    extra = jax.random.normal(second, (D, HEADS, HD), jnp.float32) * scale
    keys = 0.6 * base[:, :, 0] + 0.8 * extra
    stacked = jnp.stack([base[:, :, 0], keys, base[:, :, 2]], axis=2)
    return stacked.reshape(D, 3 * D).astype(jnp.bfloat16)


def set_ends(values, stream_key, least, top_value):
    dims = values.shape
    index_at = [jax.random.randint(jax.random.fold_in(stream_key, axis), (), 0, dims[axis]) for axis in range(len(dims))]
    values = values.at[tuple(index_at)].set(least)
    longest = dims.index(max(dims))
    index_at[longest] = (index_at[longest] + 1) % dims[longest]
    return values.at[tuple(index_at)].set(top_value)


def level_of(key, extent, cuts, least, top_value):
    def one(axis_at, blocks):
        steps = jax.random.uniform(jax.random.fold_in(jax.random.fold_in(key, 6), axis_at), (blocks,), jnp.float32, least / len(cuts), top_value / len(cuts))
        return jnp.repeat(jnp.exp(steps), extent[axis_at] // blocks).reshape((-1,) + (1,) * (len(extent) - axis_at - 1))

    gain = one(*cuts[0])
    for cut in cuts[1:]:
        gain = gain * one(*cut)
    return gain


def normal_values(own_key, dims, width, most, pieces=(), held_as=jnp.bfloat16):
    result = width * jax.random.normal(own_key, dims, jnp.float32)
    if pieces:
        result = result * level_of(own_key, dims, pieces, -0.22, 0.18)
    return jnp.clip(result, -most, most).astype(held_as)


def setup_inputs(seed: int = 0, part: int = 0) -> dict:
    streams_of = jax.random.split(jax.random.key(seed), 9)
    part_splits = jax.random.split(jax.random.fold_in(streams_of[8], part), 9)
    return {
        "hidden": draw_hidden(jax.random.fold_in(jax.random.fold_in(streams_of[8], part), 71), part),
        "modulation": normal_values(part_splits[1], (5, D), 0.5, 3.0, (), jnp.float32),
        "w_qkv": draw_w_qkv(jax.random.fold_in(streams_of[8], 71), part),
        "w_out": normal_values(streams_of[3], (D, D), D ** -0.5, 0.109375, ((0, 4), (1, 4))),
        "w_head": normal_values(streams_of[4], (D, C), D ** -0.5, 0.109375),
        "latent": normal_values(part_splits[5], (TILES, TILE_LEN, C), 1.0, 6.0, ((0, 4), (1, 4)), jnp.float32),
        "weights_int": set_ends(jax.random.randint(part_splits[6], (TILES, TILE_LEN), 1, 9), jax.random.fold_in(part_splits[6], 1), 1, 8).astype(jnp.int32),
        "step_index": jax.random.randint(part_splits[7], (1,), 0, NSTEPS // 2).astype(jnp.int32),
    }


def layer_norm(values):
    mean = lax.optimization_barrier(jnp.mean(values, axis=-1, keepdims=True))
    centred = values - mean
    spread = lax.optimization_barrier(jnp.mean(centred * centred, axis=-1, keepdims=True))
    return centred * lax.rsqrt(spread + 1e-06)

def root_norm(values):
    return values * lax.rsqrt(lax.optimization_barrier(jnp.mean(values * values, axis=-1, keepdims=True)) + 1e-06)

def noise_level(index, steps):
    level = 1.0 - index / steps
    return 3.0 * level / (1.0 + 2.0 * level)

def reference(hidden, modulation, w_qkv, w_out, w_head, latent, weights_int, step_index):
    qkv_full = w_qkv.astype(jnp.float32)
    out_groups = w_out.astype(jnp.float32).reshape(N_SEQ, D // N_SEQ, D)
    head_full = w_head.astype(jnp.float32)

    def one_tile(tokens):
        local = tokens.astype(jnp.float32)
        norm_in = (layer_norm(local) * (1.0 + modulation[1]) + modulation[0]).astype(jnp.bfloat16)
        proj = jnp.dot(norm_in.astype(jnp.float32), qkv_full)
        proj = proj.reshape(TILE_LEN, HEADS, 3, HD)
        queries = root_norm(proj[:, :, 0]).astype(jnp.bfloat16).astype(jnp.float32)
        keys = root_norm(proj[:, :, 1]).astype(jnp.bfloat16).astype(jnp.float32)
        values = proj[:, :, 2].astype(jnp.bfloat16).astype(jnp.float32)
        scores = jnp.einsum('qhe,khe->hqk', queries, keys) / math.sqrt(HD)
        expo = jnp.exp(scores)
        probs = (expo / lax.optimization_barrier(jnp.sum(expo, axis=-1, keepdims=True))).astype(jnp.bfloat16).astype(jnp.float32)
        attended = jnp.einsum('hqk,khe->qhe', probs, values).astype(jnp.bfloat16)
        attended = attended.astype(jnp.float32).reshape(TILE_LEN, N_SEQ, D // N_SEQ)
        parts = jnp.einsum('lgd,gdo->glo', attended, out_groups).astype(jnp.bfloat16)
        summed = lax.optimization_barrier(jnp.sum(parts.astype(jnp.float32), axis=0))
        mixed = local + modulation[2] * summed
        norm_out = (layer_norm(mixed) * (1.0 + modulation[4]) + modulation[3]).astype(jnp.bfloat16)
        return jnp.dot(norm_out.astype(jnp.float32), head_full)
    velocity = lax.map(one_tile, hidden)
    index = step_index[0].astype(jnp.float32)
    now = noise_level(index, NSTEPS)
    after = noise_level(index + 1.0, NSTEPS)
    moved = latent + (after - now) * velocity
    guess = latent - now * velocity
    weight = weights_int.astype(jnp.float32)
    band = (TILES - 1) * STRIDE + TILE_LEN
    places = (jnp.arange(TILES, dtype=jnp.int32)[:, None] * STRIDE + jnp.arange(TILE_LEN, dtype=jnp.int32)[None, :]).reshape(-1)
    stacked = jnp.concatenate([moved, guess], axis=2) * weight[:, :, None]
    totals = jnp.zeros((band, 2 * C), jnp.float32).at[places].add(stacked.reshape(-1, 2 * C))
    norms = jnp.zeros((band,), jnp.float32).at[places].add(weight.reshape(-1))
    joined = (totals[places] / norms[places][:, None]).reshape(TILES, TILE_LEN, 2 * C)
    return (joined[:, :, :C], joined[:, :, C:])
```

```python
import functools
import math

import jax
import jax.numpy as jnp
from jax import lax
from jax.experimental import pallas as pl
from jax.experimental.pallas import tpu as pltpu
from jax.sharding import PartitionSpec as P

HD = 128
NSTEPS = 28
CHUNKS = 2
MIB = 1 << 20


def swap(value, axis, bit):
    count = lax.axis_size(axis)
    return lax.ppermute(value, axis, [(i, i ^ bit) for i in range(count)])


def bits_of(count):
    far = [1 << n for n in range(1, count.bit_length() - 1)]
    return far + [1]


def noise_level(index, steps):
    level = 1.0 - index / steps
    return 3.0 * level / (1.0 + 2.0 * level)


def layer_norm(values):
    mean = jnp.mean(values, axis=-1, keepdims=True)
    centred = values - mean
    spread = jnp.mean(centred * centred, axis=-1, keepdims=True)
    return centred * lax.rsqrt(spread + 1e-06)


def norm_kernel(blocks, starts_ref, hidden_ref, mod_ref, out_ref):
    local = hidden_ref[...].astype(jnp.float32)
    mean = jnp.mean(local, axis=-1, keepdims=True)
    centred = local - mean
    spread = jnp.mean(centred * centred, axis=-1, keepdims=True)
    scaling = lax.rsqrt(spread + 1e-06)
    width = hidden_ref.shape[1] // blocks
    for n in range(blocks):
        taken = pl.ds(pl.multiple_of(starts_ref[n], HD), width)
        values = (hidden_ref[:, taken].astype(jnp.float32) - mean) * scaling
        values = values * (1.0 + mod_ref[1:2, taken]) + mod_ref[0:1, taken]
        out_ref[:, n * width : (n + 1) * width] = values.astype(jnp.bfloat16)


def norm_rows(hidden, modulation, starts, chunk, rows):
    width = hidden.shape[1]
    block = math.gcd(rows, 64)
    steps = rows // block
    return pl.pallas_call(
        functools.partial(norm_kernel, starts.shape[0]),
        grid=(steps,),
        in_specs=[
            pl.BlockSpec(memory_space=pltpu.SMEM),
            pl.BlockSpec((block, width), lambda i: (chunk * steps + i, 0)),
            pl.BlockSpec(modulation.shape, lambda i: (0, 0)),
        ],
        out_specs=pl.BlockSpec((block, width), lambda i: (i, 0)),
        out_shape=jax.ShapeDtypeStruct((rows, width), jnp.bfloat16),
        name="norm_in",
    )(starts, hidden, modulation)


def qkv_kernel(blocks, x_ref, *refs):
    q_ref, k_ref, v_ref = refs[-3:]
    height = x_ref.shape[1] // blocks
    proj = 0.0
    for n in range(blocks):
        proj += jnp.dot(
            x_ref[:, n * height : (n + 1) * height],
            refs[n][...],
            preferred_element_type=jnp.float32,
        )
    shape = q_ref.shape

    def rooted(part):
        spread = jnp.mean(part * part, axis=-1, keepdims=True)
        return (part * lax.rsqrt(spread + 1e-06)).astype(jnp.bfloat16)

    q_ref[...] = rooted(proj[:, :HD]).reshape(shape)
    k_ref[...] = rooted(proj[:, HD : 2 * HD]).reshape(shape)
    v_ref[...] = proj[:, 2 * HD :].astype(jnp.bfloat16).reshape(shape)


def project(x, blocks, chunk, devices, before):
    length, width = x.shape
    rows = length // devices
    count = len(blocks)
    total = blocks[0].shape[1]
    heads = total // (3 * HD)
    out = jax.ShapeDtypeStruct((heads, devices, CHUNKS, rows, HD), jnp.bfloat16)
    spec = pl.BlockSpec((1, devices, 1, rows, HD), lambda h: (h, 0, chunk, 0, 0))
    return pl.pallas_call(
        functools.partial(qkv_kernel, count),
        grid=(heads,),
        in_specs=[pl.BlockSpec((length, width), lambda h: (0, 0))]
        + [pl.BlockSpec((width // count, 3 * HD), lambda h: (0, h))] * count
        + [pl.BlockSpec(memory_space=pl.ANY)] * len(before),
        out_specs=[spec] * 3,
        out_shape=[out] * 3,
        input_output_aliases={1 + count + i: i for i in range(len(before))},
        compiler_params=pltpu.CompilerParams(vmem_limit_bytes=40 * MIB),
        cost_estimate=pl.CostEstimate(
            flops=2 * length * width * total,
            bytes_accessed=2 * (length * width + width * total * 2),
            transcendentals=0,
        ),
        name="project",
    )(x, *blocks, *before)


def attend_kernel(dest_ref, q_ref, k_ref, v_ref, out_ref):
    scores = lax.dot_general(
        q_ref[0, 0], k_ref[0], (((1,), (1,)), ((), ())), preferred_element_type=jnp.float32
    )
    expo = jnp.exp(scores * (1.0 / math.sqrt(HD)))
    total = jnp.sum(expo, axis=-1, keepdims=True)
    mixed = jnp.dot(expo.astype(jnp.bfloat16), v_ref[0], preferred_element_type=jnp.float32)
    out_ref[...] = (mixed / total).astype(jnp.bfloat16)


def attend(dest, queries, keys, values):
    heads, devices, rows, _ = queries.shape
    length = devices * rows
    whole = pl.BlockSpec((1, length, HD), lambda h, dest: (h, 0, 0))
    return pl.pallas_call(
        attend_kernel,
        grid_spec=pltpu.PrefetchScalarGridSpec(
            num_scalar_prefetch=1,
            grid=(heads,),
            in_specs=[
                pl.BlockSpec((1, 1, rows, HD), lambda h, dest: (h, dest[0], 0, 0)),
                whole,
                whole,
            ],
            out_specs=pl.BlockSpec((rows, HD), lambda h, dest: (0, h)),
        ),
        out_shape=jax.ShapeDtypeStruct((rows, heads * HD), jnp.bfloat16),
        compiler_params=pltpu.CompilerParams(vmem_limit_bytes=40 * MIB),
        cost_estimate=pl.CostEstimate(
            flops=4 * rows * length * heads * HD,
            bytes_accessed=2 * heads * HD * 2 * (rows + length),
            transcendentals=rows * length * heads,
        ),
        name="attend",
    )(
        dest.reshape(1),
        queries,
        keys.reshape(heads, length, HD),
        values.reshape(heads, length, HD),
    )


def finish_kernel(devices, pieces, place_ref, coef_ref, *refs):
    parts = refs[:devices]
    sources = refs[devices : devices + pieces]
    hidden_ref, mod_ref, head_ref, latent_ref, weight_ref = refs[
        devices + pieces : devices + pieces + 5
    ]
    out_ref, sent_ref, weights, attended, mixed, sems = refs[devices + pieces + 5 :]
    copies = [
        pltpu.make_async_copy(sources[p], weights.at[p], sems.at[p]) for p in range(pieces)
    ]
    for copy in copies:
        copy.start()
    features = parts[0].shape[1]
    place = place_ref[0]
    for k in range(devices):
        origin = lax.rem(place - k + devices, devices)
        attended[:, pl.ds(pl.multiple_of(origin * features, HD), features)] = parts[k][...]
    width = weights.shape[2]
    for p in range(pieces):
        copies[p].wait()
        summed = jnp.dot(attended[...], weights[p], preferred_element_type=jnp.float32)
        cols = slice(p * width, (p + 1) * width)
        mixed[:, cols] = hidden_ref[:, cols].astype(jnp.float32) + mod_ref[2:3, cols] * summed
    normed = layer_norm(mixed[...]) * (1.0 + mod_ref[4:5, :]) + mod_ref[3:4, :]
    velocity = lax.dot_general(
        head_ref[...],
        normed.astype(jnp.bfloat16),
        (((1,), (1,)), ((), ())),
        preferred_element_type=jnp.float32,
    )
    channels = velocity.shape[0]
    base, weight = latent_ref[...], weight_ref[...]
    moved = (base + coef_ref[1] * velocity) * weight
    guess = (base - coef_ref[0] * velocity) * weight
    out_ref[:channels, :] = moved
    out_ref[channels:, :] = guess
    sent_ref[:channels, :] = moved.astype(jnp.bfloat16)
    sent_ref[channels:, :] = guess.astype(jnp.bfloat16)


def finish(place, coef, parts, pieces, hidden, modulation, head, latent, weight):
    devices, count = len(parts), len(pieces)
    rows, width = hidden.shape
    channels = head.shape[0]
    smem = pl.BlockSpec(memory_space=pltpu.SMEM)
    vmem = pl.BlockSpec(memory_space=pltpu.VMEM)
    hbm = pl.BlockSpec(memory_space=pl.ANY)
    return pl.pallas_call(
        functools.partial(finish_kernel, devices, count),
        in_specs=[smem, smem] + [vmem] * devices + [hbm] * count + [vmem] * 5,
        out_specs=[vmem, vmem],
        out_shape=[
            jax.ShapeDtypeStruct((2 * channels, rows), jnp.float32),
            jax.ShapeDtypeStruct((2 * channels, rows), jnp.bfloat16),
        ],
        scratch_shapes=[
            pltpu.VMEM((count,) + pieces[0].shape, jnp.bfloat16),
            pltpu.VMEM((rows, width), jnp.bfloat16),
            pltpu.VMEM((rows, width), jnp.float32),
            pltpu.SemaphoreType.DMA((count,)),
        ],
        compiler_params=pltpu.CompilerParams(vmem_limit_bytes=56 * MIB),
        cost_estimate=pl.CostEstimate(
            flops=2 * rows * width * width,
            bytes_accessed=2 * width * width,
            transcendentals=0,
        ),
        name="finish",
    )(place.reshape(1), coef, *parts, *pieces, hidden, modulation, head, latent, weight)


def shards(hidden, modulation, w_qkv, w_out, w_head, latent, weights_int, step_index):
    local = hidden[0]
    rows = local.shape[0]
    devices = lax.axis_size("seq")
    tiles = lax.axis_size("tile")
    groups = lax.axis_size("group")
    place, tile, group = lax.axis_index("seq"), lax.axis_index("tile"), lax.axis_index("group")

    weight = weights_int.astype(jnp.float32)
    joins = [
        (t * devices + s, (t + 1) * devices + s - (devices - 2))
        for t in range(tiles - 1)
        for s in range(devices - 2, devices)
    ]
    joins += [
        (t * devices + s, (t - 1) * devices + s + (devices - 2))
        for t in range(1, tiles)
        for s in range(2)
    ]
    norms = weight + lax.ppermute(
        weight.astype(jnp.bfloat16), ("tile", "seq"), joins
    ).astype(jnp.float32)

    part = w_out.shape[1] // groups
    share = lax.dynamic_slice_in_dim(w_out, group * part, part, axis=1)
    columns = {(0, 0): lax.all_gather(share, "seq", axis=0, tiled=True)}

    height = w_qkv.shape[0]
    blocks = {0: w_qkv}
    for bit in bits_of(tiles):
        blocks.update({d ^ bit: swap(blocks[d], "tile", bit) for d in list(blocks)})
    starts = jnp.stack([(tile ^ d) * height for d in range(tiles)]).astype(jnp.int32)
    if height % HD:
        full = jnp.zeros((tiles * height, w_qkv.shape[1]), w_qkv.dtype)
        for d in range(tiles):
            full = lax.dynamic_update_slice_in_dim(full, blocks[d], starts[d], axis=0)
        blocks = {0: full}
        starts = jnp.zeros((1,), jnp.int32)
    blocks = [blocks[d] for d in range(len(blocks))]

    count = rows // CHUNKS
    gathered = [
        lax.all_gather(norm_rows(local, modulation, starts, c, count), "seq", axis=0, tiled=True)
        for c in range(CHUNKS)
    ]

    far, near = bits_of(tiles)[:-1], bits_of(tiles)[-1]
    for bit in far:
        columns.update({(d ^ bit, g): swap(columns[d, g], "tile", bit) for d, g in list(columns)})
    if groups > 1:
        for turn in range(1, groups):
            pairs = [(g, (g + turn) % groups) for g in range(groups)]
            columns.update(
                {
                    (d, turn): lax.ppermute(columns[d, 0], "group", pairs)
                    for d, g in list(columns)
                    if g == 0
                }
            )
    columns.update({(d ^ near, g): swap(columns[d, g], "tile", near) for d, g in list(columns)})
    order = sorted(columns)

    def reorder(value, axis):
        return jnp.concatenate(
            [
                lax.dynamic_slice_in_dim(
                    value,
                    (tile ^ d) * (part * groups) + lax.rem(group - g + groups, groups) * part,
                    part,
                    axis=axis,
                )
                for d, g in order
            ],
            axis=axis,
        )

    hidden_by = reorder(local, 1)
    modulation_by = reorder(modulation, 1)
    head_by = reorder(w_head.T, 1)
    pieces = [columns[key] for key in order]
    if part % HD:
        pieces = [jnp.concatenate(pieces, axis=1)]

    state = ()
    for c in range(CHUNKS):
        state = project(gathered[c], blocks, c, devices, state)
    heads = w_qkv.shape[1] // (3 * HD)
    queries, keys, values = [value.reshape(heads, devices, rows, HD) for value in state]

    parts = {}
    for turn in list(range(1, devices)) + [0]:
        done = attend(lax.rem(place + turn, devices), queries, keys, values)
        if turn:
            done = lax.ppermute(done, "seq", [(s, (s + turn) % devices) for s in range(devices)])
        parts[turn] = done

    index = step_index[0].astype(jnp.float32)
    now = noise_level(index, NSTEPS)
    after = noise_level(index + 1.0, NSTEPS)
    weighted, sent = finish(
        place,
        jnp.stack([now, after - now]),
        [parts[turn] for turn in range(devices)],
        pieces,
        hidden_by,
        modulation_by,
        head_by,
        latent[0].T,
        weight,
    )
    other = lax.ppermute(sent, ("tile", "seq"), joins).astype(jnp.float32)
    joined = (weighted + other) / norms
    channels = w_head.shape[1]
    return (joined[:channels].T[None], joined[channels:].T[None])


def solution(mesh):
    in_specs = (
        P(("group", "tile"), "seq", None),
        P("group", None),
        P("tile", "seq"),
        P("seq", "tile"),
        P(),
        P(("group", "tile"), "seq", None),
        P(("group", "tile"), "seq"),
        P("group"),
    )
    out_specs = (P(("group", "tile"), "seq", None), P(("group", "tile"), "seq", None))
    return jax.shard_map(shards, mesh=mesh, in_specs=in_specs, out_specs=out_specs, check_vma=False)
```

```python
import functools
import math

import jax
import jax.numpy as jnp
from jax import lax
from jax.experimental import pallas as pl
from jax.experimental.pallas import tpu as pltpu
from jax.sharding import PartitionSpec as P

HD = 128
NSTEPS = 28
CHUNKS = 2
MIB = 1 << 20


def swap(value, axis, bit):
    count = lax.axis_size(axis)
    return lax.ppermute(value, axis, [(i, i ^ bit) for i in range(count)])


def bits_of(count):
    far = [1 << n for n in range(1, count.bit_length() - 1)]
    return far + [1]


def along(value, axis):
    count = lax.axis_size(axis)
    ups, downs = [value], [value]
    for step in range(1, count):
        ups.append(
            lax.ppermute(ups[-1], axis, [(s, s + 1) for s in range(step - 1, count - 1)])
        )
        downs.append(
            lax.ppermute(downs[-1], axis, [(s, s - 1) for s in range(1, count - step + 1)])
        )
    return [value] + [ups[m] + downs[count - m] for m in range(1, count)]


def after(value, *others):
    return lax.optimization_barrier((value,) + others)[0]


def noise_level(index, steps):
    level = 1.0 - index / steps
    return 3.0 * level / (1.0 + 2.0 * level)


def layer_norm(values):
    mean = jnp.mean(values, axis=-1, keepdims=True)
    centred = values - mean
    spread = jnp.mean(centred * centred, axis=-1, keepdims=True)
    return centred * lax.rsqrt(spread + 1e-06)


def norm_kernel(blocks, starts_ref, hidden_ref, mod_ref, out_ref):
    local = hidden_ref[...].astype(jnp.float32)
    mean = jnp.mean(local, axis=-1, keepdims=True)
    centred = local - mean
    spread = jnp.mean(centred * centred, axis=-1, keepdims=True)
    scaling = lax.rsqrt(spread + 1e-06)
    width = hidden_ref.shape[1] // blocks
    for n in range(blocks):
        taken = pl.ds(pl.multiple_of(starts_ref[n], HD), width)
        values = (hidden_ref[:, taken].astype(jnp.float32) - mean) * scaling
        values = values * (1.0 + mod_ref[1:2, taken]) + mod_ref[0:1, taken]
        out_ref[:, n * width : (n + 1) * width] = values.astype(jnp.bfloat16)


def norm_rows(hidden, modulation, starts, chunk, rows):
    width = hidden.shape[1]
    block = math.gcd(rows, 64)
    steps = rows // block
    return pl.pallas_call(
        functools.partial(norm_kernel, starts.shape[0]),
        grid=(steps,),
        in_specs=[
            pl.BlockSpec(memory_space=pltpu.SMEM),
            pl.BlockSpec((block, width), lambda i: (chunk * steps + i, 0)),
            pl.BlockSpec(modulation.shape, lambda i: (0, 0)),
        ],
        out_specs=pl.BlockSpec((block, width), lambda i: (i, 0)),
        out_shape=jax.ShapeDtypeStruct((rows, width), jnp.bfloat16),
        name="norm_in",
    )(starts, hidden, modulation)


def qkv_kernel(blocks, x_ref, *refs):
    q_ref, k_ref, v_ref = refs[-3:]
    height = x_ref.shape[1] // blocks
    proj = 0.0
    for n in range(blocks):
        proj += jnp.dot(
            x_ref[:, n * height : (n + 1) * height],
            refs[n][...],
            preferred_element_type=jnp.float32,
        )
    shape = q_ref.shape[1:]

    def rooted(part):
        spread = jnp.mean(part * part, axis=-1, keepdims=True)
        return (part * lax.rsqrt(spread + 1e-06)).astype(jnp.bfloat16)

    for h in range(q_ref.shape[0]):
        query, key, value = (proj[:, (3 * h + i) * HD : (3 * h + i + 1) * HD] for i in range(3))
        q_ref[h] = rooted(query).reshape(shape)
        k_ref[h] = rooted(key).reshape(shape)
        v_ref[h] = value.astype(jnp.bfloat16).reshape(shape)


def project(x, blocks, chunk, devices, before):
    length, width = x.shape
    rows = length // devices
    count = len(blocks)
    total = blocks[0].shape[1]
    heads = total // (3 * HD)
    many = 2 if heads % 2 == 0 else 1
    out = jax.ShapeDtypeStruct((heads, devices, CHUNKS, rows, HD), jnp.bfloat16)
    spec = pl.BlockSpec((many, devices, 1, rows, HD), lambda h: (h, 0, chunk, 0, 0))
    return pl.pallas_call(
        functools.partial(qkv_kernel, count),
        grid=(heads // many,),
        in_specs=[pl.BlockSpec((length, width), lambda h: (0, 0))]
        + [pl.BlockSpec((width // count, many * 3 * HD), lambda h: (0, h))] * count
        + [pl.BlockSpec(memory_space=pl.ANY)] * len(before),
        out_specs=[spec] * 3,
        out_shape=[out] * 3,
        input_output_aliases={1 + count + i: i for i in range(len(before))},
        compiler_params=pltpu.CompilerParams(vmem_limit_bytes=60 * MIB),
        cost_estimate=pl.CostEstimate(
            flops=2 * length * width * total,
            bytes_accessed=2 * (length * width + width * total * 2),
            transcendentals=0,
        ),
        name="project",
    )(x, *blocks, *before)


def attend_kernel(dest_ref, q_ref, k_ref, v_ref, out_ref):
    scores = lax.dot_general(
        q_ref[0, 0], k_ref[0], (((1,), (1,)), ((), ())), preferred_element_type=jnp.float32
    )
    expo = jnp.exp(scores * (1.0 / math.sqrt(HD)))
    total = jnp.sum(expo, axis=-1, keepdims=True)
    mixed = jnp.dot(expo.astype(jnp.bfloat16), v_ref[0], preferred_element_type=jnp.float32)
    out_ref[...] = (mixed / total).astype(jnp.bfloat16)


def attend(dest, queries, keys, values):
    heads, devices, rows, _ = queries.shape
    length = devices * rows
    whole = pl.BlockSpec((1, length, HD), lambda h, dest: (h, 0, 0))
    return pl.pallas_call(
        attend_kernel,
        grid_spec=pltpu.PrefetchScalarGridSpec(
            num_scalar_prefetch=1,
            grid=(heads,),
            in_specs=[
                pl.BlockSpec((1, 1, rows, HD), lambda h, dest: (h, dest[0], 0, 0)),
                whole,
                whole,
            ],
            out_specs=pl.BlockSpec((rows, HD), lambda h, dest: (0, h)),
        ),
        out_shape=jax.ShapeDtypeStruct((rows, heads * HD), jnp.bfloat16),
        compiler_params=pltpu.CompilerParams(vmem_limit_bytes=60 * MIB),
        cost_estimate=pl.CostEstimate(
            flops=4 * rows * length * heads * HD,
            bytes_accessed=2 * heads * HD * 2 * (rows + length),
            transcendentals=rows * length * heads,
        ),
        name="attend",
    )(
        dest.reshape(1),
        queries,
        keys.reshape(heads, length, HD),
        values.reshape(heads, length, HD),
    )


def add_kernel(count, part_ref, *refs):
    pieces = refs[:count]
    before_ref, mod_ref, out_ref = refs[count:]
    width = pieces[0].shape[1]
    for p in range(count):
        cols = slice(p * width, (p + 1) * width)
        summed = jnp.dot(part_ref[...], pieces[p][...], preferred_element_type=jnp.float32)
        out_ref[:, cols] = before_ref[:, cols].astype(jnp.float32) + mod_ref[2:3, cols] * summed


def add_part(part, turn, pieces, before, modulation):
    rows, features = part.shape
    width = before.shape[1]
    count = len(pieces)
    aliased = before.dtype == jnp.float32
    return pl.pallas_call(
        functools.partial(add_kernel, count),
        grid=(1,),
        in_specs=[pl.BlockSpec(part.shape, lambda i: (0, 0))]
        + [pl.BlockSpec((features, pieces[0].shape[1]), lambda i: (turn, 0))] * count
        + [
            pl.BlockSpec(before.shape, lambda i: (0, 0)),
            pl.BlockSpec(modulation.shape, lambda i: (0, 0)),
        ],
        out_specs=pl.BlockSpec((rows, width), lambda i: (0, 0)),
        out_shape=jax.ShapeDtypeStruct((rows, width), jnp.float32),
        input_output_aliases={1 + count: 0} if aliased else {},
        compiler_params=pltpu.CompilerParams(vmem_limit_bytes=60 * MIB),
        cost_estimate=pl.CostEstimate(
            flops=2 * rows * width * features,
            bytes_accessed=2 * width * features + 8 * rows * width,
            transcendentals=0,
        ),
        name="add_part",
    )(part, *pieces, before, modulation)


def finish_kernel(turn, count, coef_ref, part_ref, *refs):
    sources = refs[:count]
    before_ref, mod_ref, head_ref, latent_ref, weight_ref = refs[count : count + 5]
    out_ref, sent_ref, weights, mixed, sems = refs[count + 5 :]
    features = part_ref.shape[1]
    width = weights.shape[2]
    copies = []
    for p in range(count):
        cols = pl.ds(p * width, width)
        copies.append(
            (
                pltpu.make_async_copy(
                    sources[p].at[pl.ds(turn * features, features)], weights.at[p], sems.at[0, p]
                ),
                pltpu.make_async_copy(before_ref.at[:, cols], mixed.at[:, cols], sems.at[1, p]),
            )
        )
        copies[p][0].start()
        copies[p][1].start()
    for p in range(count):
        copies[p][0].wait()
        summed = jnp.dot(part_ref[...], weights[p], preferred_element_type=jnp.float32)
        cols = slice(p * width, (p + 1) * width)
        copies[p][1].wait()
        mixed[:, cols] += mod_ref[2:3, cols] * summed
    normed = layer_norm(mixed[...]) * (1.0 + mod_ref[4:5, :]) + mod_ref[3:4, :]
    velocity = lax.dot_general(
        head_ref[...],
        normed.astype(jnp.bfloat16),
        (((1,), (1,)), ((), ())),
        preferred_element_type=jnp.float32,
    )
    channels = velocity.shape[0]
    base, weight = latent_ref[...], weight_ref[...]
    moved = (base + coef_ref[1] * velocity) * weight
    guess = (base - coef_ref[0] * velocity) * weight
    out_ref[:channels, :] = moved
    out_ref[channels:, :] = guess
    sent_ref[:channels, :] = moved.astype(jnp.bfloat16)
    sent_ref[channels:, :] = guess.astype(jnp.bfloat16)


def finish(coef, part, turn, pieces, before, modulation, head, latent, weight):
    rows, width = before.shape
    features = part.shape[1]
    count = len(pieces)
    channels = head.shape[0]
    smem = pl.BlockSpec(memory_space=pltpu.SMEM)
    vmem = pl.BlockSpec(memory_space=pltpu.VMEM)
    hbm = pl.BlockSpec(memory_space=pl.ANY)
    return pl.pallas_call(
        functools.partial(finish_kernel, turn, count),
        in_specs=[smem, vmem] + [hbm] * count + [hbm] + [vmem] * 4,
        out_specs=[vmem, vmem],
        out_shape=[
            jax.ShapeDtypeStruct((2 * channels, rows), jnp.float32),
            jax.ShapeDtypeStruct((2 * channels, rows), jnp.bfloat16),
        ],
        scratch_shapes=[
            pltpu.VMEM((count, features, pieces[0].shape[1]), jnp.bfloat16),
            pltpu.VMEM((rows, width), jnp.float32),
            pltpu.SemaphoreType.DMA((2, count)),
        ],
        compiler_params=pltpu.CompilerParams(vmem_limit_bytes=60 * MIB),
        cost_estimate=pl.CostEstimate(
            flops=2 * rows * width * features,
            bytes_accessed=2 * width * features + 4 * rows * width,
            transcendentals=0,
        ),
        name="finish",
    )(coef, part, *pieces, before, modulation, head, latent, weight)


def shards(hidden, modulation, w_qkv, w_out, w_head, latent, weights_int, step_index):
    local = hidden[0]
    rows = local.shape[0]
    devices = lax.axis_size("seq")
    tiles = lax.axis_size("tile")
    groups = lax.axis_size("group")
    place, tile, group = lax.axis_index("seq"), lax.axis_index("tile"), lax.axis_index("group")

    weight = weights_int.astype(jnp.float32)
    joins = [
        (t * devices + s, (t + 1) * devices + s - (devices - 2))
        for t in range(tiles - 1)
        for s in range(devices - 2, devices)
    ]
    joins += [
        (t * devices + s, (t - 1) * devices + s + (devices - 2))
        for t in range(1, tiles)
        for s in range(2)
    ]
    norms = weight + lax.ppermute(
        weight.astype(jnp.bfloat16), ("tile", "seq"), joins
    ).astype(jnp.float32)

    part = w_out.shape[1] // groups
    share = lax.dynamic_slice_in_dim(w_out, group * part, part, axis=1)
    columns = {(0, 0): jnp.concatenate(along(share, "seq"), axis=0)}

    height = w_qkv.shape[0]
    blocks = {0: w_qkv}
    for bit in bits_of(tiles):
        blocks.update({d ^ bit: swap(blocks[d], "tile", bit) for d in list(blocks)})
    starts = jnp.stack([(tile ^ d) * height for d in range(tiles)]).astype(jnp.int32)
    arrived = dict(blocks)
    if height % HD:
        full = jnp.zeros((tiles * height, w_qkv.shape[1]), w_qkv.dtype)
        for d in range(tiles):
            full = lax.dynamic_update_slice_in_dim(full, blocks[d], starts[d], axis=0)
        blocks = {0: full}
        starts = jnp.zeros((1,), jnp.int32)
    blocks = [blocks[d] for d in range(len(blocks))]

    count = rows // CHUNKS
    gathered = [
        lax.all_gather(norm_rows(local, modulation, starts, c, count), "seq", axis=0, tiled=True)
        for c in range(CHUNKS)
    ]

    state = ()
    for c in range(CHUNKS):
        state = project(gathered[c], blocks, c, devices, state)

    far, near = bits_of(tiles)[:-1], bits_of(tiles)[-1]
    if far:
        first = far[0]
        columns[first, 0] = swap(after(columns[0, 0], arrived[first]), "tile", first)
    for bit in far[1:]:
        columns.update({(d ^ bit, g): swap(columns[d, g], "tile", bit) for d, g in list(columns)})
    for turn in range(1, groups):
        pairs = [(g, (g + turn) % groups) for g in range(groups)]
        columns.update(
            {
                (d, turn): lax.ppermute(columns[d, 0], "group", pairs)
                for d, g in list(columns)
                if g == 0
            }
        )
    columns.update(
        {
            (d ^ near, g): swap(after(columns[d, g], state[0]) if g else columns[d, g], "tile", near)
            for d, g in list(columns)
        }
    )
    order = sorted(columns)

    def reorder(value, axis):
        return jnp.concatenate(
            [
                lax.dynamic_slice_in_dim(
                    value,
                    (tile ^ d) * (part * groups) + lax.rem(group - g + groups, groups) * part,
                    part,
                    axis=axis,
                )
                for d, g in order
            ],
            axis=axis,
        )

    hidden_by = reorder(local, 1)
    modulation_by = reorder(modulation, 1)
    head_by = reorder(w_head.T, 1)
    pieces = [columns[key] for key in order]
    if part % HD:
        pieces = [jnp.concatenate(pieces, axis=1)]

    heads = w_qkv.shape[1] // (3 * HD)
    queries, keys, values = [value.reshape(heads, devices, rows, HD) for value in state]

    turns = sorted(range(1, devices), key=lambda turn: -min(turn, devices - turn))
    parts = {}
    for turn in turns + [0]:
        done = attend(lax.rem(place + turn, devices), queries, keys, values)
        if turn:
            done = lax.ppermute(done, "seq", [(s, (s + turn) % devices) for s in range(devices)])
        parts[turn] = done

    mixed = hidden_by
    for turn in [0] + turns[:-1]:
        mixed = add_part(parts[turn], turn, pieces, mixed, modulation_by)
    index = step_index[0].astype(jnp.float32)
    now = noise_level(index, NSTEPS)
    later = noise_level(index + 1.0, NSTEPS)
    weighted, sent = finish(
        jnp.stack([now, later - now]),
        parts[turns[-1]],
        turns[-1],
        pieces,
        mixed,
        modulation_by,
        head_by,
        latent[0].T,
        weight,
    )
    other = lax.ppermute(sent, ("tile", "seq"), joins).astype(jnp.float32)
    joined = (weighted + other) / norms
    channels = w_head.shape[1]
    return (joined[:channels].T[None], joined[channels:].T[None])


def solution(mesh):
    in_specs = (
        P(("group", "tile"), "seq", None),
        P("group", None),
        P("tile", "seq"),
        P("seq", "tile"),
        P(),
        P(("group", "tile"), "seq", None),
        P(("group", "tile"), "seq"),
        P("group"),
    )
    out_specs = (P(("group", "tile"), "seq", None), P(("group", "tile"), "seq", None))
    return jax.shard_map(shards, mesh=mesh, in_specs=in_specs, out_specs=out_specs, check_vma=False)
```

```python
import functools
import math

import jax
import jax.numpy as jnp
from jax import lax
from jax.experimental import pallas as pl
from jax.experimental.pallas import tpu as pltpu
from jax.sharding import PartitionSpec as P

HD = 128
NSTEPS = 28
MIB = 1 << 20


def swap(value, axis, bit):
    count = lax.axis_size(axis)
    return lax.ppermute(value, axis, [(i, i ^ bit) for i in range(count)])


def bits_of(count):
    far = [1 << n for n in range(1, count.bit_length() - 1)]
    return far + [1]


def after(value, *others):
    return lax.optimization_barrier((value,) + others)[0]


def noise_level(index, steps):
    level = 1.0 - index / steps
    return 3.0 * level / (1.0 + 2.0 * level)


def turned(value, axis, turn):
    count = lax.axis_size(axis)
    return lax.ppermute(value, axis, [(i, (i + turn) % count) for i in range(count)])


def layer_norm(values):
    mean = jnp.mean(values, axis=-1, keepdims=True)
    centred = values - mean
    spread = jnp.mean(centred * centred, axis=-1, keepdims=True)
    return centred * lax.rsqrt(spread + 1e-06)


def root_norm(values):
    spread = jnp.mean(values * values, axis=-1, keepdims=True)
    return (values * lax.rsqrt(spread + 1e-06)).astype(jnp.bfloat16)


def norm_kernel(blocks, starts_ref, hidden_ref, mod_ref, out_ref):
    local = hidden_ref[...].astype(jnp.float32)
    mean = jnp.mean(local, axis=-1, keepdims=True)
    centred = local - mean
    spread = jnp.mean(centred * centred, axis=-1, keepdims=True)
    scaling = lax.rsqrt(spread + 1e-06)
    width = hidden_ref.shape[1] // blocks
    for n in range(blocks):
        taken = pl.ds(pl.multiple_of(starts_ref[n], HD), width)
        values = (hidden_ref[:, taken].astype(jnp.float32) - mean) * scaling
        values = values * (1.0 + mod_ref[1:2, taken]) + mod_ref[0:1, taken]
        out_ref[:, n * width : (n + 1) * width] = values.astype(jnp.bfloat16)


def norm_rows(hidden, modulation, starts, first, rows):
    width = hidden.shape[1]
    block = math.gcd(math.gcd(first, rows), 64)
    return pl.pallas_call(
        functools.partial(norm_kernel, starts.shape[0]),
        grid=(rows // block,),
        in_specs=[
            pl.BlockSpec(memory_space=pltpu.SMEM),
            pl.BlockSpec((block, width), lambda i: (first // block + i, 0)),
            pl.BlockSpec(modulation.shape, lambda i: (0, 0)),
        ],
        out_specs=pl.BlockSpec((block, width), lambda i: (i, 0)),
        out_shape=jax.ShapeDtypeStruct((rows, width), jnp.bfloat16),
        name="norm_in",
    )(starts, hidden, modulation)


def product(x_ref, blocks):
    height = x_ref.shape[1] // len(blocks)
    total = 0.0
    for n, block in enumerate(blocks):
        total += jnp.dot(
            x_ref[:, n * height : (n + 1) * height],
            block[...],
            preferred_element_type=jnp.float32,
        )
    return total


def project_kernel(sources, blocks, *refs):
    x_refs, w_refs = refs[:sources], refs[sources : sources + blocks]
    q_ref, k_ref, v_ref, x_all = refs[sources + blocks :]
    rows = x_refs[0].shape[0]

    @pl.when(pl.program_id(0) == 0)
    def _():
        for n in range(sources):
            x_all[n * rows : (n + 1) * rows] = x_refs[n][...]

    proj = product(x_all, w_refs)
    for h in range(q_ref.shape[0]):
        query, key, value = (proj[:, (3 * h + i) * HD : (3 * h + i + 1) * HD] for i in range(3))
        q_ref[h] = root_norm(query)
        k_ref[h] = root_norm(key)
        v_ref[h] = value.astype(jnp.bfloat16)


def project(sources, blocks):
    rows, width = sources[0].shape
    length = rows * len(sources)
    total = blocks[0].shape[1]
    heads = total // (3 * HD)
    many = 2 if heads % 2 == 0 else 1
    out = jax.ShapeDtypeStruct((heads, length, HD), jnp.bfloat16)
    return pl.pallas_call(
        functools.partial(project_kernel, len(sources), len(blocks)),
        grid=(heads // many,),
        in_specs=[pl.BlockSpec((rows, width), lambda h: (0, 0))] * len(sources)
        + [pl.BlockSpec((width // len(blocks), many * 3 * HD), lambda h: (0, h))] * len(blocks),
        out_specs=[pl.BlockSpec((many, length, HD), lambda h: (h, 0, 0))] * 3,
        out_shape=[out] * 3,
        scratch_shapes=[pltpu.VMEM((length, width), jnp.bfloat16)],
        compiler_params=pltpu.CompilerParams(vmem_limit_bytes=60 * MIB),
        cost_estimate=pl.CostEstimate(
            flops=2 * length * width * total,
            bytes_accessed=2 * (length * width + width * total * 2),
            transcendentals=0,
        ),
        name="project",
    )(*sources, *blocks)


def attend_kernel(blocks, devices, place_ref, x_ref, *refs):
    first, second = refs[0:3], refs[3:6]
    w_refs = refs[6 : 6 + blocks]
    outs = refs[6 + blocks : 6 + blocks + devices]
    queries, keys, values = refs[6 + blocks + devices :]
    proj = product(x_ref, w_refs)
    queries[...] = root_norm(proj[:, :HD])
    sets = (first[1].shape[1], second[1].shape[1], x_ref.shape[0])
    ends = (sets[0], sets[0] + sets[1], sum(sets))
    keys[: ends[0]] = first[1][0]
    keys[ends[0] : ends[1]] = second[1][0]
    keys[ends[1] :] = root_norm(proj[:, HD : 2 * HD])
    values[: ends[0], :HD] = first[2][0]
    values[ends[0] : ends[1], :HD] = second[2][0]
    values[ends[1] :, :HD] = proj[:, 2 * HD :].astype(jnp.bfloat16)
    values[:, HD:] = jnp.ones((ends[2], HD), jnp.bfloat16)
    rows = [count // devices for count in sets]
    for turn in range(devices):
        dest = lax.rem(place_ref[0] + turn, devices)
        slot = (devices - turn) % devices
        query = jnp.concatenate(
            [
                first[0][0, pl.ds(pl.multiple_of(dest * rows[0], rows[0]), rows[0])],
                second[0][0, slot * rows[1] : (slot + 1) * rows[1]],
                queries[pl.ds(pl.multiple_of(dest * rows[2], rows[2]), rows[2])],
            ],
            axis=0,
        )
        scores = lax.dot_general(
            query, keys[...], (((1,), (1,)), ((), ())), preferred_element_type=jnp.float32
        )
        expo = jnp.exp(scores * (1.0 / math.sqrt(HD))).astype(jnp.bfloat16)
        mixed = jnp.dot(expo, values[...], preferred_element_type=jnp.float32)
        outs[turn][...] = (mixed[:, :HD] / mixed[:, HD:]).astype(jnp.bfloat16)


def attend(place, devices, x, first, second, blocks, start, heads):
    last, width = x.shape
    length = last + first[0].shape[1] + second[0].shape[1]
    rows = length // devices
    head = lambda value: pl.BlockSpec((1, value.shape[1], HD), lambda h: (start + h, 0, 0))
    out = jax.ShapeDtypeStruct((rows, heads * HD), jnp.bfloat16)
    return pl.pallas_call(
        functools.partial(attend_kernel, len(blocks), devices),
        grid=(heads,),
        in_specs=[
            pl.BlockSpec(memory_space=pltpu.SMEM),
            pl.BlockSpec((last, width), lambda h: (0, 0)),
        ]
        + [head(value) for value in first + second]
        + [pl.BlockSpec((width // len(blocks), 3 * HD), lambda h: (0, start + h))] * len(blocks),
        out_specs=[pl.BlockSpec((rows, HD), lambda h: (0, h))] * devices,
        out_shape=[out] * devices,
        scratch_shapes=[
            pltpu.VMEM((last, HD), jnp.bfloat16),
            pltpu.VMEM((length, HD), jnp.bfloat16),
            pltpu.VMEM((length, 2 * HD), jnp.bfloat16),
        ],
        compiler_params=pltpu.CompilerParams(vmem_limit_bytes=60 * MIB),
        cost_estimate=pl.CostEstimate(
            flops=4 * length * length * heads * HD + 2 * last * width * 3 * HD * heads,
            bytes_accessed=2 * heads * HD * (4 * length + 3 * width),
            transcendentals=length * length * heads,
        ),
        name="attend",
    )(place.reshape(1), x, *first, *second, *blocks)


def multiply(parts, offsets, starts_ref, sources, weights, sems, wide, store):
    depth = [part.shape[1] for part in parts]
    width = weights.shape[2]
    copies = []
    for p, source in enumerate(sources):
        copies.append([])
        for n, offset in enumerate(offsets):
            to = sum(depth[:n])
            copies[p].append(
                pltpu.make_async_copy(
                    source.at[pl.ds(offset, depth[n])],
                    weights.at[p, pl.ds(to, depth[n])],
                    sems.at[p, n],
                )
            )
            copies[p][n].start()
    for n, part in enumerate(parts):
        wide[:, sum(depth[:n]) : sum(depth[: n + 1])] = part[...]
    for p in range(len(sources)):
        for copy in copies[p]:
            copy.wait()
        cols = pl.ds(pl.multiple_of(starts_ref[p], HD), width)
        store(p, cols, jnp.dot(wide[...], weights[p], preferred_element_type=jnp.float32))


def add_kernel(offsets, count, starts_ref, *refs):
    parts = refs[: len(offsets)]
    sources = refs[len(offsets) : len(offsets) + count]
    before_ref, mod_ref, out_ref, weights, wide, sems = refs[len(offsets) + count :]

    def store(p, cols, summed):
        out_ref[:, cols] = before_ref[:, cols].astype(jnp.float32) + mod_ref[2:3, cols] * summed

    multiply(parts, offsets, starts_ref, sources, weights, sems, wide, store)


def finish_kernel(offsets, count, starts_ref, coef_ref, *refs):
    parts = refs[: len(offsets)]
    sources = refs[len(offsets) : len(offsets) + count]
    before_ref, mod_ref, head_ref, latent_ref, weight_ref, out_ref, sent_ref = refs[
        len(offsets) + count : len(offsets) + count + 7
    ]
    weights, wide, sems, mixed, extra = refs[len(offsets) + count + 7 :]
    width = weights.shape[2]
    copies = []
    for p in range(count):
        cols = pl.ds(pl.multiple_of(starts_ref[p], HD), width)
        copies.append(
            pltpu.make_async_copy(before_ref.at[:, cols], mixed.at[:, cols], extra.at[p])
        )
        copies[p].start()

    def store(p, cols, summed):
        copies[p].wait()
        mixed[:, cols] += mod_ref[2:3, cols] * summed

    multiply(parts, offsets, starts_ref, sources, weights, sems, wide, store)
    normed = layer_norm(mixed[...]) * (1.0 + mod_ref[4:5, :]) + mod_ref[3:4, :]
    velocity = lax.dot_general(
        head_ref[...],
        normed.astype(jnp.bfloat16),
        (((1,), (1,)), ((), ())),
        preferred_element_type=jnp.float32,
    )
    channels = velocity.shape[0]
    base, weight = latent_ref[...], weight_ref[...]
    moved = (base + coef_ref[1] * velocity) * weight
    guess = (base - coef_ref[0] * velocity) * weight
    out_ref[:channels, :] = moved
    out_ref[channels:, :] = guess
    sent_ref[:channels, :] = moved.astype(jnp.bfloat16)
    sent_ref[channels:, :] = guess.astype(jnp.bfloat16)


def accumulate(parts, offsets, starts, pieces, before, modulation, last=None):
    rows, width = before.shape
    depth = sum(part.shape[1] for part in parts)
    count = len(pieces)
    smem = pl.BlockSpec(memory_space=pltpu.SMEM)
    vmem = pl.BlockSpec(memory_space=pltpu.VMEM)
    hbm = pl.BlockSpec(memory_space=pl.ANY)
    scratch = [
        pltpu.VMEM((count, depth, pieces[0].shape[1]), jnp.bfloat16),
        pltpu.VMEM((rows, depth), jnp.bfloat16),
        pltpu.SemaphoreType.DMA((count, len(parts))),
    ]
    params = dict(
        compiler_params=pltpu.CompilerParams(vmem_limit_bytes=60 * MIB),
        cost_estimate=pl.CostEstimate(
            flops=2 * rows * width * depth,
            bytes_accessed=2 * width * depth + 8 * rows * width,
            transcendentals=0,
        ),
    )
    if last is None:
        aliased = before.dtype == jnp.float32
        return pl.pallas_call(
            functools.partial(add_kernel, offsets, count),
            in_specs=[smem] + [vmem] * len(parts) + [hbm] * count + [vmem] * 2,
            out_specs=vmem,
            out_shape=jax.ShapeDtypeStruct((rows, width), jnp.float32),
            scratch_shapes=scratch,
            input_output_aliases={1 + len(parts) + count: 0} if aliased else {},
            name="add_parts",
            **params,
        )(starts, *parts, *pieces, before, modulation)
    coef, head, latent, weight = last
    channels = head.shape[0]
    return pl.pallas_call(
        functools.partial(finish_kernel, offsets, count),
        in_specs=[smem, smem] + [vmem] * len(parts) + [hbm] * (count + 1) + [vmem] * 4,
        out_specs=[vmem, vmem],
        out_shape=[
            jax.ShapeDtypeStruct((2 * channels, rows), jnp.float32),
            jax.ShapeDtypeStruct((2 * channels, rows), jnp.bfloat16),
        ],
        scratch_shapes=scratch
        + [pltpu.VMEM((rows, width), jnp.float32), pltpu.SemaphoreType.DMA((count,))],
        name="finish",
        **params,
    )(starts, coef, *parts, *pieces, before, modulation, head, latent, weight)


def shards(hidden, modulation, w_qkv, w_out, w_head, latent, weights_int, step_index):
    local = hidden[0]
    rows = local.shape[0]
    devices = lax.axis_size("seq")
    tiles = lax.axis_size("tile")
    groups = lax.axis_size("group")
    place, tile, group = lax.axis_index("seq"), lax.axis_index("tile"), lax.axis_index("group")
    far, near = bits_of(tiles)[:-1], bits_of(tiles)[-1]

    weight = weights_int.astype(jnp.float32)
    joins = [
        (t * devices + s, (t + 1) * devices + s - (devices - 2))
        for t in range(tiles - 1)
        for s in range(devices - 2, devices)
    ]
    joins += [
        (t * devices + s, (t - 1) * devices + s + (devices - 2))
        for t in range(1, tiles)
        for s in range(2)
    ]
    norms = weight + lax.ppermute(
        weight.astype(jnp.bfloat16), ("tile", "seq"), joins
    ).astype(jnp.float32)

    height = w_qkv.shape[0]
    blocks = {0: w_qkv}
    for bit in far + [near]:
        blocks.update({d ^ bit: swap(blocks[d], "tile", bit) for d in list(blocks)})
    arrived = dict(blocks)
    row_starts = jnp.stack([(tile ^ d) * height for d in range(tiles)]).astype(jnp.int32)
    if height % HD:
        full = jnp.zeros((tiles * height, w_qkv.shape[1]), w_qkv.dtype)
        for d in range(tiles):
            full = lax.dynamic_update_slice_in_dim(full, blocks[d], row_starts[d], axis=0)
        blocks = {0: full}
        row_starts = jnp.zeros((1,), jnp.int32)
    blocks = [blocks[d] for d in range(len(blocks))]

    counts = (rows // 2, rows // 4, rows // 4)
    normed = [
        norm_rows(local, modulation, row_starts, sum(counts[:n]), counts[n]) for n in range(3)
    ]
    gathered = lax.all_gather(normed[0], "seq", axis=0, tiled=True)

    part = w_out.shape[1] // groups
    share = lax.dynamic_slice_in_dim(w_out, group * part, part, axis=1)
    share = [share] + [turned(share, "seq", turn) for turn in range(1, devices)]
    passed = [normed[1]] + [turned(normed[1], "seq", turn) for turn in range(1, devices)]
    gathered_last = lax.all_gather(normed[2], "seq", axis=0, tiled=True)
    columns = {(0, 0): jnp.concatenate(share, axis=0)}
    if far:
        columns[far[0], 0] = swap(after(columns[0, 0], arrived[far[0]]), "tile", far[0])
    first = project([gathered], blocks)
    if far:
        columns[far[0], 0] = after(columns[far[0], 0], first[0])
    for bit in far[1:]:
        columns.update({(d ^ bit, g): swap(columns[d, g], "tile", bit) for d, g in list(columns)})
    for turn in range(1, groups):
        columns.update(
            {(d, turn): turned(columns[d, 0], "group", turn) for d, g in list(columns) if g == 0}
        )
    second = project(passed, blocks)
    heads = w_qkv.shape[1] // (3 * HD)
    halves = [(0, (heads + 1) // 2), ((heads + 1) // 2, heads // 2)]
    sent = []
    for start, count in halves:
        sent.append(
            attend(place, devices, gathered_last, first, second, blocks, start, count)
        )
    columns.update(
        {
            (d ^ near, g): swap(
                after(columns[d, g], sent[0][0]) if g else columns[d, g], "tile", near
            )
            for d, g in list(columns)
        }
    )
    order = sorted(columns)
    pieces = [columns[key] for key in order]
    starts = jnp.stack(
        [
            (tile ^ d) * (part * groups) + lax.rem(group - g + groups, groups) * part
            for d, g in order
        ]
    ).astype(jnp.int32)
    if part % HD:
        whole = jnp.zeros((w_out.shape[0] * devices, part * len(order)), w_out.dtype)
        for n, piece in enumerate(pieces):
            whole = lax.dynamic_update_slice_in_dim(whole, piece, starts[n], axis=1)
        pieces, starts = [whole], jnp.zeros((1,), jnp.int32)

    turns = sorted(range(1, devices), key=lambda turn: -min(turn, devices - turn))
    received = [
        [turned(half[turn], "seq", turn) for turn in turns] for half in sent
    ]
    features = w_out.shape[0]
    offsets = [[turn * features + start * HD for turn in turns] for start, _ in halves]
    mixed = accumulate(
        [half[0] for half in sent],
        [start * HD for start, _ in halves],
        starts,
        pieces,
        local,
        modulation,
    )
    mixed = accumulate(received[0], offsets[0], starts, pieces, mixed, modulation)
    index = step_index[0].astype(jnp.float32)
    now = noise_level(index, NSTEPS)
    later = noise_level(index + 1.0, NSTEPS)
    weighted, to_join = accumulate(
        received[1],
        offsets[1],
        starts,
        pieces,
        mixed,
        modulation,
        (jnp.stack([now, later - now]), w_head.T, latent[0].T, weight),
    )
    other = lax.ppermute(to_join, ("tile", "seq"), joins).astype(jnp.float32)
    joined = (weighted + other) / norms
    channels = w_head.shape[1]
    return (joined[:channels].T[None], joined[channels:].T[None])


def solution(mesh):
    in_specs = (
        P(("group", "tile"), "seq", None),
        P("group", None),
        P("tile", "seq"),
        P("seq", "tile"),
        P(),
        P(("group", "tile"), "seq", None),
        P(("group", "tile"), "seq"),
        P("group"),
    )
    out_specs = (P(("group", "tile"), "seq", None), P(("group", "tile"), "seq", None))
    return jax.shard_map(shards, mesh=mesh, in_specs=in_specs, out_specs=out_specs, check_vma=False)
```

```python
import functools
import math

import jax
import jax.numpy as jnp
from jax import lax
from jax.experimental import pallas as pl
from jax.experimental.pallas import tpu as pltpu
from jax.sharding import PartitionSpec as P

HD = 128
NSTEPS = 28
MIB = 1 << 20


def swap(value, axis, bit):
    count = lax.axis_size(axis)
    return lax.ppermute(value, axis, [(i, i ^ bit) for i in range(count)])


def bits_of(count):
    far = [1 << n for n in range(1, count.bit_length() - 1)]
    return far + [1]


def noise_level(index, steps):
    level = 1.0 - index / steps
    return 3.0 * level / (1.0 + 2.0 * level)


def turned(value, axis, turn):
    count = lax.axis_size(axis)
    return lax.ppermute(value, axis, [(i, (i + turn) % count) for i in range(count)])


def layer_norm(values):
    mean = jnp.mean(values, axis=-1, keepdims=True)
    centred = values - mean
    spread = jnp.mean(centred * centred, axis=-1, keepdims=True)
    return centred * lax.rsqrt(spread + 1e-06)


def root_norm(values):
    spread = jnp.mean(values * values, axis=-1, keepdims=True)
    return (values * lax.rsqrt(spread + 1e-06)).astype(jnp.bfloat16)


def norm_kernel(blocks, starts_ref, hidden_ref, mod_ref, out_ref):
    local = hidden_ref[...].astype(jnp.float32)
    mean = jnp.mean(local, axis=-1, keepdims=True)
    centred = local - mean
    spread = jnp.mean(centred * centred, axis=-1, keepdims=True)
    scaling = lax.rsqrt(spread + 1e-06)
    width = hidden_ref.shape[1] // blocks
    for n in range(blocks):
        taken = pl.ds(pl.multiple_of(starts_ref[n], HD), width)
        values = (hidden_ref[:, taken].astype(jnp.float32) - mean) * scaling
        values = values * (1.0 + mod_ref[1:2, taken]) + mod_ref[0:1, taken]
        out_ref[:, n * width : (n + 1) * width] = values.astype(jnp.bfloat16)


def norm_rows(hidden, modulation, starts, first, rows):
    width = hidden.shape[1]
    block = math.gcd(math.gcd(first, rows), 64)
    return pl.pallas_call(
        functools.partial(norm_kernel, starts.shape[0]),
        grid=(rows // block,),
        in_specs=[
            pl.BlockSpec(memory_space=pltpu.SMEM),
            pl.BlockSpec((block, width), lambda i: (first // block + i, 0)),
            pl.BlockSpec(modulation.shape, lambda i: (0, 0)),
        ],
        out_specs=pl.BlockSpec((block, width), lambda i: (i, 0)),
        out_shape=jax.ShapeDtypeStruct((rows, width), jnp.bfloat16),
        name="norm_in",
    )(starts, hidden, modulation)


def product(x_ref, blocks):
    height = x_ref.shape[1] // len(blocks)
    total = 0.0
    for n, block in enumerate(blocks):
        total += jnp.dot(
            x_ref[:, n * height : (n + 1) * height],
            block[...],
            preferred_element_type=jnp.float32,
        )
    return total


def project_kernel(sources, blocks, *refs):
    x_refs, w_refs = refs[:sources], refs[sources : sources + blocks]
    q_ref, k_ref, v_ref, x_all = refs[sources + blocks :]
    rows = x_refs[0].shape[0]

    @pl.when(pl.program_id(0) == 0)
    def _():
        for n in range(sources):
            x_all[n * rows : (n + 1) * rows] = x_refs[n][...]

    proj = product(x_all, w_refs)
    for h in range(q_ref.shape[0]):
        query, key, value = (proj[:, (3 * h + i) * HD : (3 * h + i + 1) * HD] for i in range(3))
        q_ref[h] = root_norm(query)
        k_ref[h] = root_norm(key)
        v_ref[h] = value.astype(jnp.bfloat16)


def project(sources, blocks):
    rows, width = sources[0].shape
    length = rows * len(sources)
    total = blocks[0].shape[1]
    heads = total // (3 * HD)
    many = 2 if heads % 2 == 0 else 1
    out = jax.ShapeDtypeStruct((heads, length, HD), jnp.bfloat16)
    return pl.pallas_call(
        functools.partial(project_kernel, len(sources), len(blocks)),
        grid=(heads // many,),
        in_specs=[pl.BlockSpec((rows, width), lambda h: (0, 0))] * len(sources)
        + [pl.BlockSpec((width // len(blocks), many * 3 * HD), lambda h: (0, h))] * len(blocks),
        out_specs=[pl.BlockSpec((many, length, HD), lambda h: (h, 0, 0))] * 3,
        out_shape=[out] * 3,
        scratch_shapes=[pltpu.VMEM((length, width), jnp.bfloat16)],
        compiler_params=pltpu.CompilerParams(vmem_limit_bytes=60 * MIB),
        name="project",
    )(*sources, *blocks)


def attend_kernel(blocks, devices, place_ref, gathered_ref, *refs):
    passed, first = refs[:devices], refs[devices : devices + 3]
    w_refs = refs[devices + 3 : devices + 3 + blocks]
    outs = refs[devices + 3 + blocks : 2 * devices + 3 + blocks]
    tokens, queries, keys, values, sems = refs[2 * devices + 3 + blocks :]
    sets = (first[1].shape[1], gathered_ref.shape[0], passed[0].shape[0] * devices)
    start, length = sets[0], sum(sets)
    rows = [count // devices for count in sets]

    @pl.when(pl.program_id(0) == 0)
    def _():
        copies = [pltpu.make_async_copy(gathered_ref, tokens.at[pl.ds(0, sets[1])], sems.at[0])]
        for n in range(devices):
            to = tokens.at[pl.ds(sets[1] + n * rows[2], rows[2])]
            copies.append(pltpu.make_async_copy(passed[n], to, sems.at[n + 1]))
        for copy in copies:
            copy.start()
        values[:, HD:] = jnp.ones((length, HD), jnp.bfloat16)
        for copy in copies:
            copy.wait()

    proj = product(tokens, w_refs)
    queries[...] = root_norm(proj[:, :HD])
    keys[:start] = first[1][0]
    keys[start:] = root_norm(proj[:, HD : 2 * HD])
    values[:start, :HD] = first[2][0]
    values[start:, :HD] = proj[:, 2 * HD :].astype(jnp.bfloat16)
    for turn in range(devices):
        dest = lax.rem(place_ref[0] + turn, devices)
        slot = (devices - turn) % devices
        slot_start = sets[1] + slot * rows[2]
        query = jnp.concatenate(
            [
                first[0][0, pl.ds(pl.multiple_of(dest * rows[0], rows[0]), rows[0])],
                queries[slot_start : slot_start + rows[2]],
                queries[pl.ds(pl.multiple_of(dest * rows[1], rows[1]), rows[1])],
            ],
            axis=0,
        )
        scores = lax.dot_general(
            query, keys[...], (((1,), (1,)), ((), ())), preferred_element_type=jnp.float32
        )
        expo = jnp.exp(scores * (1.0 / math.sqrt(HD))).astype(jnp.bfloat16)
        mixed = jnp.dot(expo, values[...], preferred_element_type=jnp.float32)
        outs[turn][...] = (mixed[:, :HD] / mixed[:, HD:]).astype(jnp.bfloat16)


def attend(place, gathered, passed, first, blocks, start, heads):
    devices = len(passed)
    last, width = gathered.shape
    last += passed[0].shape[0] * devices
    length = last + first[0].shape[1]
    rows = length // devices
    hbm = pl.BlockSpec(memory_space=pl.ANY)
    head = pl.BlockSpec((1, length - last, HD), lambda h: (start + h, 0, 0))
    out = jax.ShapeDtypeStruct((rows, heads * HD), jnp.bfloat16)
    return pl.pallas_call(
        functools.partial(attend_kernel, len(blocks), devices),
        grid=(heads,),
        in_specs=[pl.BlockSpec(memory_space=pltpu.SMEM), hbm]
        + [hbm] * devices
        + [head] * 3
        + [pl.BlockSpec((width // len(blocks), 3 * HD), lambda h: (0, start + h))] * len(blocks),
        out_specs=[pl.BlockSpec((rows, HD), lambda h: (0, h))] * devices,
        out_shape=[out] * devices,
        scratch_shapes=[
            pltpu.VMEM((last, width), jnp.bfloat16),
            pltpu.VMEM((last, HD), jnp.bfloat16),
            pltpu.VMEM((length, HD), jnp.bfloat16),
            pltpu.VMEM((length, 2 * HD), jnp.bfloat16),
            pltpu.SemaphoreType.DMA((devices + 1,)),
        ],
        compiler_params=pltpu.CompilerParams(vmem_limit_bytes=60 * MIB),
        name="attend",
    )(place.reshape(1), gathered, *passed, *first, *blocks)


def multiply(parts, offsets, starts_ref, sources, weights, sems, wide, store):
    depth = [part.shape[1] for part in parts]
    width = weights.shape[2]
    copies = []
    for p, source in enumerate(sources):
        copies.append([])
        for n, offset in enumerate(offsets):
            to = sum(depth[:n])
            copies[p].append(
                pltpu.make_async_copy(
                    source.at[pl.ds(offset, depth[n])],
                    weights.at[p, pl.ds(to, depth[n])],
                    sems.at[p, n],
                )
            )
            copies[p][n].start()
    for n, part in enumerate(parts):
        wide[:, sum(depth[:n]) : sum(depth[: n + 1])] = part[...]
    for p in range(len(sources)):
        for copy in copies[p]:
            copy.wait()
        cols = pl.ds(pl.multiple_of(starts_ref[p], HD), width)
        store(p, cols, jnp.dot(wide[...], weights[p], preferred_element_type=jnp.float32))


def add_kernel(offsets, count, starts_ref, *refs):
    parts = refs[: len(offsets)]
    sources = refs[len(offsets) : len(offsets) + count]
    before_ref, mod_ref, out_ref, weights, wide, sems = refs[len(offsets) + count :]

    def store(p, cols, summed):
        out_ref[:, cols] = before_ref[:, cols].astype(jnp.float32) + mod_ref[2:3, cols] * summed

    multiply(parts, offsets, starts_ref, sources, weights, sems, wide, store)


def finish_kernel(offsets, count, starts_ref, coef_ref, *refs):
    parts = refs[: len(offsets)]
    sources = refs[len(offsets) : len(offsets) + count]
    before_ref, mod_ref, head_ref, latent_ref, weight_ref, out_ref, sent_ref = refs[
        len(offsets) + count : len(offsets) + count + 7
    ]
    weights, wide, sems, mixed, extra = refs[len(offsets) + count + 7 :]
    width = weights.shape[2]
    copies = []
    for p in range(count):
        cols = pl.ds(pl.multiple_of(starts_ref[p], HD), width)
        copies.append(
            pltpu.make_async_copy(before_ref.at[:, cols], mixed.at[:, cols], extra.at[p])
        )
        copies[p].start()

    def store(p, cols, summed):
        copies[p].wait()
        mixed[:, cols] += mod_ref[2:3, cols] * summed

    multiply(parts, offsets, starts_ref, sources, weights, sems, wide, store)
    normed = layer_norm(mixed[...]) * (1.0 + mod_ref[4:5, :]) + mod_ref[3:4, :]
    velocity = lax.dot_general(
        head_ref[...],
        normed.astype(jnp.bfloat16),
        (((1,), (1,)), ((), ())),
        preferred_element_type=jnp.float32,
    )
    channels = velocity.shape[0]
    base, weight = latent_ref[...], weight_ref[...]
    moved = (base + coef_ref[1] * velocity) * weight
    guess = (base - coef_ref[0] * velocity) * weight
    out_ref[:channels, :] = moved
    out_ref[channels:, :] = guess
    sent_ref[:channels, :] = moved.astype(jnp.bfloat16)
    sent_ref[channels:, :] = guess.astype(jnp.bfloat16)


def accumulate(parts, offsets, starts, pieces, before, modulation, last=None):
    rows, width = before.shape
    depth = sum(part.shape[1] for part in parts)
    count = len(pieces)
    smem = pl.BlockSpec(memory_space=pltpu.SMEM)
    vmem = pl.BlockSpec(memory_space=pltpu.VMEM)
    hbm = pl.BlockSpec(memory_space=pl.ANY)
    scratch = [
        pltpu.VMEM((count, depth, pieces[0].shape[1]), jnp.bfloat16),
        pltpu.VMEM((rows, depth), jnp.bfloat16),
        pltpu.SemaphoreType.DMA((count, len(parts))),
    ]
    params = dict(
        compiler_params=pltpu.CompilerParams(vmem_limit_bytes=60 * MIB),
    )
    if last is None:
        aliased = before.dtype == jnp.float32
        return pl.pallas_call(
            functools.partial(add_kernel, offsets, count),
            in_specs=[smem] + [vmem] * len(parts) + [hbm] * count + [vmem] * 2,
            out_specs=vmem,
            out_shape=jax.ShapeDtypeStruct((rows, width), jnp.float32),
            scratch_shapes=scratch,
            input_output_aliases={1 + len(parts) + count: 0} if aliased else {},
            name="add_parts",
            **params,
        )(starts, *parts, *pieces, before, modulation)
    coef, head, latent, weight = last
    channels = head.shape[0]
    return pl.pallas_call(
        functools.partial(finish_kernel, offsets, count),
        in_specs=[smem, smem] + [vmem] * len(parts) + [hbm] * (count + 1) + [vmem] * 4,
        out_specs=[vmem, vmem],
        out_shape=[
            jax.ShapeDtypeStruct((2 * channels, rows), jnp.float32),
            jax.ShapeDtypeStruct((2 * channels, rows), jnp.bfloat16),
        ],
        scratch_shapes=scratch
        + [pltpu.VMEM((rows, width), jnp.float32), pltpu.SemaphoreType.DMA((count,))],
        name="finish",
        **params,
    )(starts, coef, *parts, *pieces, before, modulation, head, latent, weight)


def shards(hidden, modulation, w_qkv, w_out, w_head, latent, weights_int, step_index):
    local = hidden[0]
    rows = local.shape[0]
    devices = lax.axis_size("seq")
    tiles = lax.axis_size("tile")
    groups = lax.axis_size("group")
    place, tile, group = lax.axis_index("seq"), lax.axis_index("tile"), lax.axis_index("group")
    far, near = bits_of(tiles)[:-1], bits_of(tiles)[-1]

    weight = weights_int.astype(jnp.float32)
    joins = [
        (t * devices + s, (t + 1) * devices + s - (devices - 2))
        for t in range(tiles - 1)
        for s in range(devices - 2, devices)
    ]
    joins += [
        (t * devices + s, (t - 1) * devices + s + (devices - 2))
        for t in range(1, tiles)
        for s in range(2)
    ]
    norms = weight + lax.ppermute(
        weight.astype(jnp.bfloat16), ("tile", "seq"), joins
    ).astype(jnp.float32)

    part = w_out.shape[1] // groups
    share = lax.dynamic_slice_in_dim(w_out, group * part, part, axis=1)
    narrow = part % HD != 0
    if narrow:
        share = share.T
    share = [share] + [turned(share, "seq", turn) for turn in range(1, devices)]

    height = w_qkv.shape[0]
    row_starts = jnp.stack([(tile ^ d) * height for d in range(tiles)]).astype(jnp.int32)
    if height % HD != 0:
        row_starts = jnp.zeros((1,), jnp.int32)
    counts = (3 * rows // 8, rows // 4, 3 * rows // 8)
    normed = [
        norm_rows(local, modulation, row_starts, sum(counts[:n]), counts[n]) for n in range(3)
    ]
    gathered = lax.all_gather(normed[0], "seq", axis=0, tiled=True)

    blocks = {0: w_qkv}
    ragged = height % HD != 0
    for bit in far if not ragged else []:
        blocks.update({d ^ bit: swap(blocks[d], "tile", bit) for d in list(blocks)})
    blocks, share, gathered = lax.optimization_barrier((blocks, share, gathered))
    passed = [normed[1]] + [turned(normed[1], "seq", turn) for turn in range(1, devices)]
    gathered_last = lax.all_gather(normed[2], "seq", axis=0, tiled=True)
    if ragged:
        blocks[0] = lax.all_gather(blocks[0], "tile", axis=0, tiled=True)
    else:
        blocks.update({d ^ near: swap(blocks[d], "tile", near) for d in list(blocks)})
    blocks = [blocks[d] for d in range(len(blocks))]

    columns = {(0, 0): jnp.concatenate(share, axis=1 if narrow else 0)}
    if narrow:
        columns[0, 0] = lax.all_gather(columns[0, 0], ("tile", "group"), axis=0, tiled=True).T
    else:
        for bit in far:
            columns.update({(d ^ bit, 0): swap(columns[d, 0], "tile", bit) for d, _ in list(columns)})
        for turn in range(1, groups):
            columns[0, turn] = turned(columns[0, 0], "group", turn)
    first = project([gathered], blocks)
    passed, first, columns, gathered_last = lax.optimization_barrier(
        (passed, first, columns, gathered_last)
    )
    late = {}
    for turn in range(1, groups) if not narrow else []:
        late.update(
            {(d, turn): turned(columns[d, 0], "group", turn) for d, g in columns if d and not g}
        )
    if groups == 2 and len(far) == 1 and not narrow:
        bit, half = far[0], columns[0, 0].shape[0] // 2
        late[bit, 1] = [
            turned(columns[bit, 0][:half], "group", 1),
            swap(columns[0, 1][half:], "tile", bit),
        ]
    if not narrow:
        columns.update({(d ^ near, g): swap(columns[d, g], "tile", near) for d, g in list(columns)})
    heads = w_qkv.shape[1] // (3 * HD)
    halves = [(0, (heads + 1) // 2), ((heads + 1) // 2, heads // 2)]
    turns = sorted(range(1, devices), key=lambda turn: -min(turn, devices - turn))
    attended = attend(place, gathered_last, passed, first, blocks, *halves[0])
    attended, columns, gathered_last = lax.optimization_barrier(
        (attended, columns, gathered_last)
    )
    received = [[turned(attended[turn], "seq", turn) for turn in turns]]
    own = [attended[0]]
    attended = attend(place, gathered_last, passed, first, blocks, *halves[1])
    attended, late, received = lax.optimization_barrier((attended, late, received))
    for key, value in late.items():
        columns[key] = jnp.concatenate(value, axis=0) if isinstance(value, list) else value
    columns.update({(d ^ near, g): swap(columns[d, g], "tile", near) for d, g in late})
    received.append([turned(attended[turn], "seq", turn) for turn in turns])
    own.append(attended[0])
    order = sorted(columns)
    pieces = [columns[key] for key in order]
    starts = jnp.stack(
        [
            (tile ^ d) * (part * groups) + lax.rem(group - g + groups, groups) * part
            for d, g in order
        ]
    ).astype(jnp.int32)
    if narrow:
        starts = jnp.zeros((1,), jnp.int32)

    features = w_out.shape[0]
    offsets = [[turn * features + start * HD for turn in turns] for start, _ in halves]
    mixed = accumulate(
        own,
        [start * HD for start, _ in halves],
        starts,
        pieces,
        local,
        modulation,
    )
    mixed = accumulate(received[0], offsets[0], starts, pieces, mixed, modulation)
    index = step_index[0].astype(jnp.float32)
    now = noise_level(index, NSTEPS)
    later = noise_level(index + 1.0, NSTEPS)
    weighted, to_join = accumulate(
        received[1],
        offsets[1],
        starts,
        pieces,
        mixed,
        modulation,
        (jnp.stack([now, later - now]), w_head.T, latent[0].T, weight),
    )
    other = lax.ppermute(to_join, ("tile", "seq"), joins).astype(jnp.float32)
    joined = (weighted + other) / norms
    channels = w_head.shape[1]
    return (joined[:channels].T[None], joined[channels:].T[None])


def solution(mesh):
    in_specs = (
        P(("group", "tile"), "seq", None),
        P("group", None),
        P("tile", "seq"),
        P("seq", "tile"),
        P(),
        P(("group", "tile"), "seq", None),
        P(("group", "tile"), "seq"),
        P("group"),
    )
    out_specs = (P(("group", "tile"), "seq", None), P(("group", "tile"), "seq", None))
    return jax.shard_map(shards, mesh=mesh, in_specs=in_specs, out_specs=out_specs, check_vma=False)
```

```python
import functools
import math

import jax
import jax.numpy as jnp
from jax import lax
from jax.experimental import pallas as pl
from jax.experimental.pallas import tpu as pltpu
from jax.sharding import PartitionSpec as P

HD = 128
NSTEPS = 28
MIB = 1 << 20


def swap(value, axis, bit):
    count = lax.axis_size(axis)
    return lax.ppermute(value, axis, [(i, i ^ bit) for i in range(count)])


def bits_of(count):
    far = [1 << n for n in range(1, count.bit_length() - 1)]
    return far + [1]


def noise_level(index, steps):
    level = 1.0 - index / steps
    return 3.0 * level / (1.0 + 2.0 * level)


def turned(value, axis, turn):
    count = lax.axis_size(axis)
    return lax.ppermute(value, axis, [(i, (i + turn) % count) for i in range(count)])


def step_pairs(count, step, way):
    if way > 0:
        return [(s, s + 1) for s in range(step - 1, count - 1)]
    return [(s, s - 1) for s in range(1, count - step + 1)]


def arrivals(count):
    return [
        sorted((s - home for home in range(count) if home != s), key=lambda hop: (abs(hop), -hop))
        for s in range(count)
    ]


def layer_norm(values):
    mean = jnp.mean(values, axis=-1, keepdims=True)
    centred = values - mean
    spread = jnp.mean(centred * centred, axis=-1, keepdims=True)
    return centred * lax.rsqrt(spread + 1e-06)


def root_norm(values):
    spread = jnp.mean(values * values, axis=-1, keepdims=True)
    return (values * lax.rsqrt(spread + 1e-06)).astype(jnp.bfloat16)


def norm_kernel(blocks, starts_ref, hidden_ref, mod_ref, out_ref):
    local = hidden_ref[...].astype(jnp.float32)
    mean = jnp.mean(local, axis=-1, keepdims=True)
    centred = local - mean
    spread = jnp.mean(centred * centred, axis=-1, keepdims=True)
    scaling = lax.rsqrt(spread + 1e-06)
    width = hidden_ref.shape[1] // blocks
    for n in range(blocks):
        taken = pl.ds(pl.multiple_of(starts_ref[n], HD), width)
        values = (hidden_ref[:, taken].astype(jnp.float32) - mean) * scaling
        values = values * (1.0 + mod_ref[1:2, taken]) + mod_ref[0:1, taken]
        out_ref[:, n * width : (n + 1) * width] = values.astype(jnp.bfloat16)


def norm_rows(hidden, modulation, starts, first, rows):
    width = hidden.shape[1]
    block = math.gcd(math.gcd(first, rows), 64)
    return pl.pallas_call(
        functools.partial(norm_kernel, starts.shape[0]),
        grid=(rows // block,),
        in_specs=[
            pl.BlockSpec(memory_space=pltpu.SMEM),
            pl.BlockSpec((block, width), lambda i: (first // block + i, 0)),
            pl.BlockSpec(modulation.shape, lambda i: (0, 0)),
        ],
        out_specs=pl.BlockSpec((block, width), lambda i: (i, 0)),
        out_shape=jax.ShapeDtypeStruct((rows, width), jnp.bfloat16),
        name="norm_in",
    )(starts, hidden, modulation)


def product(x_ref, blocks):
    height = x_ref.shape[1] // len(blocks)
    total = 0.0
    for n, block in enumerate(blocks):
        total += jnp.dot(
            x_ref[:, n * height : (n + 1) * height],
            block[...],
            preferred_element_type=jnp.float32,
        )
    return total


def load(place, choices, refs, to, sem):
    for n, ref in enumerate(refs):
        wanted = functools.reduce(
            jnp.logical_or, [place == s for s in range(len(choices)) if choices[s] == n]
        )

        @pl.when(wanted)
        def _():
            pltpu.make_async_copy(ref, to, sem).start()

    return pltpu.make_async_copy(refs[0], to, sem)


def load_all(place, plan, refs, tokens, sems):
    rows = tokens.shape[0] // len(plan)
    copies, used = [], 0
    for n, choices in enumerate(plan):
        many = max(choices) + 1
        to = tokens.at[pl.ds(n * rows, rows)]
        copies.append(load(place, choices, refs[used : used + many], to, sems.at[n]))
        used += many
    for copy in copies:
        copy.wait()


def project_kernel(plan, blocks, place_ref, *refs):
    w_refs = refs[:blocks]
    sources, (q_ref, k_ref, v_ref, tokens, sems) = refs[blocks:-5], refs[-5:]

    @pl.when(pl.program_id(0) == 0)
    def _():
        load_all(place_ref[0], plan, sources, tokens, sems)

    proj = product(tokens, w_refs)
    for h in range(q_ref.shape[0]):
        query, key, value = (proj[:, (3 * h + i) * HD : (3 * h + i + 1) * HD] for i in range(3))
        q_ref[h] = root_norm(query)
        k_ref[h] = root_norm(key)
        v_ref[h] = value.astype(jnp.bfloat16)


def project(place, plan, sources, blocks):
    rows, width = sources[0].shape
    length = rows * len(plan)
    total = blocks[0].shape[1]
    heads = total // (3 * HD)
    many = 2 if heads % 2 == 0 else 1
    out = jax.ShapeDtypeStruct((heads, length, HD), jnp.bfloat16)
    return pl.pallas_call(
        functools.partial(project_kernel, plan, len(blocks)),
        grid=(heads // many,),
        in_specs=[pl.BlockSpec(memory_space=pltpu.SMEM)]
        + [pl.BlockSpec((width // len(blocks), many * 3 * HD), lambda h: (0, h))] * len(blocks)
        + [pl.BlockSpec(memory_space=pl.ANY)] * len(sources),
        out_specs=[pl.BlockSpec((many, length, HD), lambda h: (h, 0, 0))] * 3,
        out_shape=[out] * 3,
        scratch_shapes=[
            pltpu.VMEM((length, width), jnp.bfloat16),
            pltpu.SemaphoreType.DMA((len(plan),)),
        ],
        compiler_params=pltpu.CompilerParams(vmem_limit_bytes=60 * MIB),
        name="project",
    )(place, *blocks, *sources)


def attend_kernel(plan, blocks, counts, place_ref, slots_ref, *refs):
    w_refs, refs = refs[:blocks], refs[blocks:]
    known, refs = refs[: 3 * len(counts)], refs[3 * len(counts) :]
    queries, keys, values, tokens, sems = refs[-5:]
    devices = slots_ref.shape[0]
    sources, outs = refs[: -5 - devices], refs[-5 - devices : -5]
    start, rows = sum(counts), tokens.shape[0]

    @pl.when(pl.program_id(0) == 0)
    def _():
        values[:, HD:] = jnp.ones((start + rows, HD), jnp.bfloat16)
        load_all(place_ref[0], plan, sources, tokens, sems)

    proj = product(tokens, w_refs)
    at = 0
    for n, count in enumerate(counts):
        queries[at : at + count] = known[3 * n][0]
        keys[at : at + count] = known[3 * n + 1][0]
        values[at : at + count, :HD] = known[3 * n + 2][0]
        at += count
    queries[start:] = root_norm(proj[:, :HD])
    keys[start:] = root_norm(proj[:, HD : 2 * HD])
    values[start:, :HD] = proj[:, 2 * HD :].astype(jnp.bfloat16)
    for turn in range(devices):
        first = pl.multiple_of(slots_ref[turn] * rows, rows)
        scores = lax.dot_general(
            queries[pl.ds(first, rows)],
            keys[...],
            (((1,), (1,)), ((), ())),
            preferred_element_type=jnp.float32,
        )
        expo = jnp.exp(scores * (1.0 / math.sqrt(HD))).astype(jnp.bfloat16)
        mixed = jnp.dot(expo, values[...], preferred_element_type=jnp.float32)
        outs[turn][...] = (mixed[:, :HD] / mixed[:, HD:]).astype(jnp.bfloat16)


def attend(place, slots, plan, sources, known, blocks, start, heads):
    devices = slots.shape[0]
    rows, width = sources[0].shape
    counts = [three[0].shape[1] for three in known]
    length = rows + sum(counts)
    smem = pl.BlockSpec(memory_space=pltpu.SMEM)
    out = jax.ShapeDtypeStruct((rows, heads * HD), jnp.bfloat16)
    return pl.pallas_call(
        functools.partial(attend_kernel, plan, len(blocks), counts),
        grid=(heads,),
        in_specs=[smem, smem]
        + [pl.BlockSpec((width // len(blocks), 3 * HD), lambda h: (0, start + h))] * len(blocks)
        + [
            pl.BlockSpec((1, count, HD), lambda h: (start + h, 0, 0))
            for count in counts
            for _ in range(3)
        ]
        + [pl.BlockSpec(memory_space=pl.ANY)] * len(sources),
        out_specs=[pl.BlockSpec((rows, HD), lambda h: (0, h))] * devices,
        out_shape=[out] * devices,
        scratch_shapes=[
            pltpu.VMEM((length, HD), jnp.bfloat16),
            pltpu.VMEM((length, HD), jnp.bfloat16),
            pltpu.VMEM((length, 2 * HD), jnp.bfloat16),
            pltpu.VMEM((rows, width), jnp.bfloat16),
            pltpu.SemaphoreType.DMA((1,)),
        ],
        compiler_params=pltpu.CompilerParams(vmem_limit_bytes=60 * MIB),
        name="attend",
    )(place, slots, *blocks, *(value for three in known for value in three), *sources)


def multiply(parts, offsets, starts_ref, rows_ref, sources, weights, sems, wide, store):
    depth = [part.shape[1] for part in parts]
    width = weights.shape[2]
    copies = []
    for p, source in enumerate(sources):
        copies.append([])
        for n, (turn, offset) in enumerate(offsets):
            to = sum(depth[:n])
            row = pl.multiple_of(rows_ref[turn] + offset, HD)
            copies[p].append(
                pltpu.make_async_copy(
                    source.at[pl.ds(row, depth[n])],
                    weights.at[p, pl.ds(to, depth[n])],
                    sems.at[p, n],
                )
            )
            copies[p][n].start()
    for n, part in enumerate(parts):
        wide[:, sum(depth[:n]) : sum(depth[: n + 1])] = part[...]
    for p in range(len(sources)):
        for copy in copies[p]:
            copy.wait()
        cols = pl.ds(pl.multiple_of(starts_ref[p], HD), width)
        store(p, cols, jnp.dot(wide[...], weights[p], preferred_element_type=jnp.float32))


def add_kernel(offsets, count, starts_ref, rows_ref, *refs):
    parts = refs[: len(offsets)]
    sources = refs[len(offsets) : len(offsets) + count]
    before_ref, mod_ref, out_ref, weights, wide, sems = refs[len(offsets) + count :]

    def store(p, cols, summed):
        out_ref[:, cols] = before_ref[:, cols].astype(jnp.float32) + mod_ref[2:3, cols] * summed

    multiply(parts, offsets, starts_ref, rows_ref, sources, weights, sems, wide, store)


def finish_kernel(offsets, count, starts_ref, rows_ref, coef_ref, *refs):
    parts = refs[: len(offsets)]
    sources = refs[len(offsets) : len(offsets) + count]
    before_ref, mod_ref, head_ref, latent_ref, weight_ref, out_ref, sent_ref = refs[
        len(offsets) + count : len(offsets) + count + 7
    ]
    weights, wide, sems, mixed, extra = refs[len(offsets) + count + 7 :]
    width = weights.shape[2]
    copies = []
    for p in range(count):
        cols = pl.ds(pl.multiple_of(starts_ref[p], HD), width)
        copies.append(
            pltpu.make_async_copy(before_ref.at[:, cols], mixed.at[:, cols], extra.at[p])
        )
        copies[p].start()

    def store(p, cols, summed):
        copies[p].wait()
        mixed[:, cols] += mod_ref[2:3, cols] * summed

    multiply(parts, offsets, starts_ref, rows_ref, sources, weights, sems, wide, store)
    normed = layer_norm(mixed[...]) * (1.0 + mod_ref[4:5, :]) + mod_ref[3:4, :]
    velocity = lax.dot_general(
        head_ref[...],
        normed.astype(jnp.bfloat16),
        (((1,), (1,)), ((), ())),
        preferred_element_type=jnp.float32,
    )
    channels = velocity.shape[0]
    base, weight = latent_ref[...], weight_ref[...]
    moved = (base + coef_ref[1] * velocity) * weight
    guess = (base - coef_ref[0] * velocity) * weight
    out_ref[:channels, :] = moved
    out_ref[channels:, :] = guess
    sent_ref[:channels, :] = moved.astype(jnp.bfloat16)
    sent_ref[channels:, :] = guess.astype(jnp.bfloat16)


def accumulate(parts, offsets, starts, firsts, pieces, before, modulation, last=None):
    rows, width = before.shape
    depth = sum(part.shape[1] for part in parts)
    count = len(pieces)
    smem = pl.BlockSpec(memory_space=pltpu.SMEM)
    vmem = pl.BlockSpec(memory_space=pltpu.VMEM)
    hbm = pl.BlockSpec(memory_space=pl.ANY)
    scratch = [
        pltpu.VMEM((count, depth, pieces[0].shape[1]), jnp.bfloat16),
        pltpu.VMEM((rows, depth), jnp.bfloat16),
        pltpu.SemaphoreType.DMA((count, len(parts))),
    ]
    params = dict(
        compiler_params=pltpu.CompilerParams(vmem_limit_bytes=60 * MIB),
    )
    if last is None:
        aliased = before.dtype == jnp.float32
        return pl.pallas_call(
            functools.partial(add_kernel, offsets, count),
            in_specs=[smem] * 2 + [vmem] * len(parts) + [hbm] * count + [vmem] * 2,
            out_specs=vmem,
            out_shape=jax.ShapeDtypeStruct((rows, width), jnp.float32),
            scratch_shapes=scratch,
            input_output_aliases={2 + len(parts) + count: 0} if aliased else {},
            name="add_parts",
            **params,
        )(starts, firsts, *parts, *pieces, before, modulation)
    coef, head, latent, weight = last
    channels = head.shape[0]
    return pl.pallas_call(
        functools.partial(finish_kernel, offsets, count),
        in_specs=[smem] * 3 + [vmem] * len(parts) + [hbm] * (count + 1) + [vmem] * 4,
        out_specs=[vmem, vmem],
        out_shape=[
            jax.ShapeDtypeStruct((2 * channels, rows), jnp.float32),
            jax.ShapeDtypeStruct((2 * channels, rows), jnp.bfloat16),
        ],
        scratch_shapes=scratch
        + [pltpu.VMEM((rows, width), jnp.float32), pltpu.SemaphoreType.DMA((count,))],
        name="finish",
        **params,
    )(starts, firsts, coef, *parts, *pieces, before, modulation, head, latent, weight)


def shards(hidden, modulation, w_qkv, w_out, w_head, latent, weights_int, step_index):
    local = hidden[0]
    rows = local.shape[0]
    devices = lax.axis_size("seq")
    tiles = lax.axis_size("tile")
    groups = lax.axis_size("group")
    place, tile, group = lax.axis_index("seq"), lax.axis_index("tile"), lax.axis_index("group")
    far, near = bits_of(tiles)[:-1], bits_of(tiles)[-1]

    weight = weights_int.astype(jnp.float32)
    joins = [
        (t * devices + s, (t + 1) * devices + s - (devices - 2))
        for t in range(tiles - 1)
        for s in range(devices - 2, devices)
    ]
    joins += [
        (t * devices + s, (t - 1) * devices + s + (devices - 2))
        for t in range(1, tiles)
        for s in range(2)
    ]
    norms = weight + lax.ppermute(
        weight.astype(jnp.bfloat16), ("tile", "seq"), joins
    ).astype(jnp.float32)

    height = w_qkv.shape[0]
    ragged = height % HD != 0
    row_starts = jnp.stack([(tile ^ d) * height for d in range(tiles)]).astype(jnp.int32)
    if ragged:
        row_starts = jnp.zeros((1,), jnp.int32)
    normed = norm_rows(local, modulation, row_starts, 0, rows)
    hops = arrivals(devices)
    blocks_by = {0: normed}

    def hop(step):
        for way in (1, -1):
            blocks_by[way * step] = lax.ppermute(
                blocks_by[way * (step - 1)], "seq", step_pairs(devices, step, way)
            )

    def arrival(number):
        wanted = [hops[s][number] for s in range(devices)]
        names = sorted(set(wanted))
        return [names.index(name) for name in wanted], [blocks_by[name] for name in names]

    part = w_out.shape[1] // groups
    share = lax.dynamic_slice_in_dim(w_out, group * part, part, axis=1)
    narrow = part % HD != 0
    columns = {(0, 0): lax.all_gather(share, "seq", axis=0, tiled=True)}

    blocks = {0: w_qkv}
    if not ragged:
        blocks[near] = swap(w_qkv, "tile", near)
        for bit in far:
            blocks.update(
                {d ^ bit: swap(blocks[d], "tile", bit) for d in list(blocks) if d != near}
            )
    hop(1)
    blocks, columns, blocks_by = lax.optimization_barrier((blocks, columns, blocks_by))
    if ragged:
        blocks[0] = lax.all_gather(blocks[0], "tile", axis=0, tiled=True)
    else:
        blocks.update(
            {d ^ near: swap(blocks[d], "tile", near) for d in list(blocks) if d not in (0, near)}
        )
    blocks = [blocks[d] for d in range(len(blocks))]
    if narrow:
        columns[0, 0] = lax.all_gather(columns[0, 0].T, ("tile", "group"), axis=0, tiled=True).T
    else:
        for bit in far:
            columns.update({(d ^ bit, 0): swap(columns[d, 0], "tile", bit) for d, _ in list(columns)})
        for turn in range(1, groups):
            columns[0, turn] = turned(columns[0, 0], "group", turn)

    at = place.reshape(1)
    known, plan, sources = [], [[0] * devices], [normed]
    for number in range(devices - 2):
        if number + 2 < devices:
            hop(number + 2)
        choices, found = arrival(number)
        plan, sources = plan + [choices], sources + found
        known.append(project(at, plan, sources, blocks))
        plan, sources = [], []
        if number + 3 < devices:
            blocks_by, known = lax.optimization_barrier((blocks_by, known))
    if not narrow:
        mine = lax.optimization_barrier((columns[0, 0], known[0]))[0]
        columns[near, 0] = swap(mine, "tile", near)
    blocks_by, known, columns = lax.optimization_barrier((blocks_by, known, columns))
    late = {}
    for turn in range(1, groups) if not narrow else []:
        late.update(
            {
                (d, turn): turned(columns[d, 0], "group", turn)
                for d, g in columns
                if d not in (0, near) and not g
            }
        )
    if groups == 2 and len(far) == 1 and not narrow:
        bit, half = far[0], columns[0, 0].shape[0] // 2
        late[bit, 1] = [
            turned(columns[bit, 0][:half], "group", 1),
            swap(columns[0, 1][half:], "tile", bit),
        ]
    if not narrow:
        columns.update(
            {
                (d ^ near, g): swap(columns[d, g], "tile", near)
                for d, g in list(columns)
                if (d ^ near, g) not in columns
            }
        )

    table = [
        [([s] + [s - hop for hop in hops[s]]).index((s + turn) % devices) for turn in range(devices)]
        for s in range(devices)
    ]
    slots = jnp.asarray(table, jnp.int32)[place]
    heads = w_qkv.shape[1] // (3 * HD)
    halves = [(0, (heads + 1) // 2), ((heads + 1) // 2, heads // 2)]
    turns = sorted(range(1, devices), key=lambda turn: -min(turn, devices - turn))
    choices, found = arrival(devices - 2)
    attended = attend(at, slots, [choices], found, known, blocks, *halves[0])
    attended, columns, found = lax.optimization_barrier((attended, columns, found))
    received = [[turned(attended[turn], "seq", turn) for turn in turns]]
    own = [attended[0]]
    attended = attend(at, slots, [choices], found, known, blocks, *halves[1])
    attended, late, received = lax.optimization_barrier((attended, late, received))
    for key, value in late.items():
        columns[key] = jnp.concatenate(value, axis=0) if isinstance(value, list) else value
    columns.update({(d ^ near, g): swap(columns[d, g], "tile", near) for d, g in late})
    received.append([turned(attended[turn], "seq", turn) for turn in turns])
    own.append(attended[0])
    order = sorted(columns)
    pieces = [columns[key] for key in order]
    starts = jnp.stack(
        [
            (tile ^ d) * (part * groups) + lax.rem(group - g + groups, groups) * part
            for d, g in order
        ]
    ).astype(jnp.int32)
    if narrow:
        starts = jnp.zeros((1,), jnp.int32)

    features = w_out.shape[0]
    firsts = jnp.stack(
        [lax.rem(place - turn + devices, devices) * features for turn in range(devices)]
    ).astype(jnp.int32)
    offsets = [[(turn, start * HD) for turn in turns] for start, _ in halves]
    mixed = accumulate(
        own + received[0],
        [(0, start * HD) for start, _ in halves] + offsets[0],
        starts,
        firsts,
        pieces,
        local,
        modulation,
    )
    index = step_index[0].astype(jnp.float32)
    now = noise_level(index, NSTEPS)
    later = noise_level(index + 1.0, NSTEPS)
    weighted, to_join = accumulate(
        received[1],
        offsets[1],
        starts,
        firsts,
        pieces,
        mixed,
        modulation,
        (jnp.stack([now, later - now]), w_head.T, latent[0].T, weight),
    )
    other = lax.ppermute(to_join, ("tile", "seq"), joins).astype(jnp.float32)
    joined = (weighted + other) / norms
    channels = w_head.shape[1]
    return (joined[:channels].T[None], joined[channels:].T[None])


def solution(mesh):
    in_specs = (
        P(("group", "tile"), "seq", None),
        P("group", None),
        P("tile", "seq"),
        P("seq", "tile"),
        P(),
        P(("group", "tile"), "seq", None),
        P(("group", "tile"), "seq"),
        P("group"),
    )
    out_specs = (P(("group", "tile"), "seq", None), P(("group", "tile"), "seq", None))
    return jax.shard_map(shards, mesh=mesh, in_specs=in_specs, out_specs=out_specs, check_vma=False)
```

```python
import functools
import math

import jax
import jax.numpy as jnp
from jax import lax
from jax.experimental import pallas as pl
from jax.experimental.pallas import tpu as pltpu
from jax.sharding import PartitionSpec as P

HD = 128
NSTEPS = 28
MIB = 1 << 20


def swap(value, axis, bit):
    count = lax.axis_size(axis)
    return lax.ppermute(value, axis, [(i, i ^ bit) for i in range(count)])


def bits_of(count):
    far = [1 << n for n in range(1, count.bit_length() - 1)]
    return far + [1]


def noise_level(index, steps):
    level = 1.0 - index / steps
    return 3.0 * level / (1.0 + 2.0 * level)


def turned(value, axis, turn):
    count = lax.axis_size(axis)
    return lax.ppermute(value, axis, [(i, (i + turn) % count) for i in range(count)])


def step_pairs(count, step, way):
    if way > 0:
        return [(s, s + 1) for s in range(step - 1, count - 1)]
    return [(s, s - 1) for s in range(1, count - step + 1)]


def arrivals(count):
    return [
        sorted((s - home for home in range(count) if home != s), key=lambda hop: (abs(hop), -hop))
        for s in range(count)
    ]


def layer_norm(values):
    mean = jnp.mean(values, axis=-1, keepdims=True)
    centred = values - mean
    spread = jnp.mean(centred * centred, axis=-1, keepdims=True)
    return centred * lax.rsqrt(spread + 1e-06)


def root_norm(values):
    spread = jnp.mean(values * values, axis=-1, keepdims=True)
    return (values * lax.rsqrt(spread + 1e-06)).astype(jnp.bfloat16)


def norm_kernel(blocks, starts_ref, hidden_ref, mod_ref, out_ref):
    local = hidden_ref[...].astype(jnp.float32)
    mean = jnp.mean(local, axis=-1, keepdims=True)
    centred = local - mean
    spread = jnp.mean(centred * centred, axis=-1, keepdims=True)
    scaling = lax.rsqrt(spread + 1e-06)
    width = hidden_ref.shape[1] // blocks
    for n in range(blocks):
        taken = pl.ds(pl.multiple_of(starts_ref[n], HD), width)
        values = (hidden_ref[:, taken].astype(jnp.float32) - mean) * scaling
        values = values * (1.0 + mod_ref[1:2, taken]) + mod_ref[0:1, taken]
        out_ref[:, n * width : (n + 1) * width] = values.astype(jnp.bfloat16)


def norm_rows(hidden, modulation, starts, first, rows):
    width = hidden.shape[1]
    block = math.gcd(math.gcd(first, rows), 64)
    return pl.pallas_call(
        functools.partial(norm_kernel, starts.shape[0]),
        grid=(rows // block,),
        in_specs=[
            pl.BlockSpec(memory_space=pltpu.SMEM),
            pl.BlockSpec((block, width), lambda i: (first // block + i, 0)),
            pl.BlockSpec(modulation.shape, lambda i: (0, 0)),
        ],
        out_specs=pl.BlockSpec((block, width), lambda i: (i, 0)),
        out_shape=jax.ShapeDtypeStruct((rows, width), jnp.bfloat16),
        name="norm_in",
    )(starts, hidden, modulation)


def product(x_ref, blocks):
    height = x_ref.shape[1] // len(blocks)
    total = 0.0
    for n, block in enumerate(blocks):
        total += jnp.dot(
            x_ref[:, n * height : (n + 1) * height],
            block[...],
            preferred_element_type=jnp.float32,
        )
    return total


def load(place, choices, refs, to, sem):
    for n, ref in enumerate(refs):
        wanted = functools.reduce(
            jnp.logical_or, [place == s for s in range(len(choices)) if choices[s] == n]
        )

        @pl.when(wanted)
        def _():
            pltpu.make_async_copy(ref, to, sem).start()

    return pltpu.make_async_copy(refs[0], to, sem)


def load_all(place, plan, refs, tokens, sems):
    rows = tokens.shape[0] // len(plan)
    copies, used = [], 0
    for n, choices in enumerate(plan):
        many = max(choices) + 1
        to = tokens.at[pl.ds(n * rows, rows)]
        copies.append(load(place, choices, refs[used : used + many], to, sems.at[n]))
        used += many
    for copy in copies:
        copy.wait()


def project_kernel(plan, blocks, place_ref, *refs):
    w_refs = refs[:blocks]
    sources, (q_ref, k_ref, v_ref, tokens, sems) = refs[blocks:-5], refs[-5:]

    @pl.when(pl.program_id(0) == 0)
    def _():
        load_all(place_ref[0], plan, sources, tokens, sems)

    proj = product(tokens, w_refs)
    for h in range(q_ref.shape[0]):
        query, key, value = (proj[:, (3 * h + i) * HD : (3 * h + i + 1) * HD] for i in range(3))
        q_ref[h] = root_norm(query)
        k_ref[h] = root_norm(key)
        v_ref[h] = value.astype(jnp.bfloat16)


def project(place, plan, sources, blocks):
    rows, width = sources[0].shape
    length = rows * len(plan)
    total = blocks[0].shape[1]
    heads = total // (3 * HD)
    many = 2 if heads % 2 == 0 else 1
    out = jax.ShapeDtypeStruct((heads, length, HD), jnp.bfloat16)
    return pl.pallas_call(
        functools.partial(project_kernel, plan, len(blocks)),
        grid=(heads // many,),
        in_specs=[pl.BlockSpec(memory_space=pltpu.SMEM)]
        + [pl.BlockSpec((width // len(blocks), many * 3 * HD), lambda h: (0, h))] * len(blocks)
        + [pl.BlockSpec(memory_space=pl.ANY)] * len(sources),
        out_specs=[pl.BlockSpec((many, length, HD), lambda h: (h, 0, 0))] * 3,
        out_shape=[out] * 3,
        scratch_shapes=[
            pltpu.VMEM((length, width), jnp.bfloat16),
            pltpu.SemaphoreType.DMA((len(plan),)),
        ],
        compiler_params=pltpu.CompilerParams(vmem_limit_bytes=28 * MIB),
        name="project",
    )(place, *blocks, *sources)


def attend_kernel(plan, blocks, counts, place_ref, slots_ref, *refs):
    w_refs, refs = refs[:blocks], refs[blocks:]
    known, refs = refs[: 3 * len(counts)], refs[3 * len(counts) :]
    queries, keys, values, tokens, sems = refs[-5:]
    devices = slots_ref.shape[0]
    sources, outs = refs[: -5 - devices], refs[-5 - devices : -5]
    start, rows = sum(counts), tokens.shape[0]

    @pl.when(pl.program_id(0) == 0)
    def _():
        values[:, HD:] = jnp.ones((start + rows, HD), jnp.bfloat16)
        load_all(place_ref[0], plan, sources, tokens, sems)

    proj = product(tokens, w_refs)
    at = 0
    for n, count in enumerate(counts):
        queries[at : at + count] = known[3 * n][0]
        keys[at : at + count] = known[3 * n + 1][0]
        values[at : at + count, :HD] = known[3 * n + 2][0]
        at += count
    queries[start:] = root_norm(proj[:, :HD])
    keys[start:] = root_norm(proj[:, HD : 2 * HD])
    values[start:, :HD] = proj[:, 2 * HD :].astype(jnp.bfloat16)
    for turn in range(devices):
        first = pl.multiple_of(slots_ref[turn] * rows, rows)
        scores = lax.dot_general(
            queries[pl.ds(first, rows)],
            keys[...],
            (((1,), (1,)), ((), ())),
            preferred_element_type=jnp.float32,
        )
        expo = jnp.exp(scores * (1.0 / math.sqrt(HD))).astype(jnp.bfloat16)
        mixed = jnp.dot(expo, values[...], preferred_element_type=jnp.float32)
        outs[turn][...] = (mixed[:, :HD] / mixed[:, HD:]).astype(jnp.bfloat16)


def attend(place, slots, plan, sources, known, blocks, start, heads):
    devices = slots.shape[0]
    rows, width = sources[0].shape
    counts = [three[0].shape[1] for three in known]
    length = rows + sum(counts)
    smem = pl.BlockSpec(memory_space=pltpu.SMEM)
    out = jax.ShapeDtypeStruct((rows, heads * HD), jnp.bfloat16)
    return pl.pallas_call(
        functools.partial(attend_kernel, plan, len(blocks), counts),
        grid=(heads,),
        in_specs=[smem, smem]
        + [pl.BlockSpec((width // len(blocks), 3 * HD), lambda h: (0, start + h))] * len(blocks)
        + [
            pl.BlockSpec((1, count, HD), lambda h: (start + h, 0, 0))
            for count in counts
            for _ in range(3)
        ]
        + [pl.BlockSpec(memory_space=pl.ANY)] * len(sources),
        out_specs=[pl.BlockSpec((rows, HD), lambda h: (0, h))] * devices,
        out_shape=[out] * devices,
        scratch_shapes=[
            pltpu.VMEM((length, HD), jnp.bfloat16),
            pltpu.VMEM((length, HD), jnp.bfloat16),
            pltpu.VMEM((length, 2 * HD), jnp.bfloat16),
            pltpu.VMEM((rows, width), jnp.bfloat16),
            pltpu.SemaphoreType.DMA((1,)),
        ],
        compiler_params=pltpu.CompilerParams(vmem_limit_bytes=28 * MIB),
        name="attend",
    )(place, slots, *blocks, *(value for three in known for value in three), *sources)


def multiply(parts, offsets, starts_ref, rows_ref, sources, weights, sems, wide, store):
    depth = [part.shape[1] for part in parts]
    width = weights.shape[2]
    copies = []
    for p, split in enumerate(sources):
        copies.append([])
        for n, (turn, offset) in enumerate(offsets):
            to = weights.at[p, pl.ds(sum(depth[:n]), depth[n])]
            row = rows_ref[turn] + offset
            size = split[0].shape[0]
            for i, source in enumerate(split):
                if len(split) == 1:
                    rows = source.at[pl.ds(pl.multiple_of(row, HD), depth[n])]
                    pltpu.make_async_copy(rows, to, sems.at[p, n]).start()
                    continue

                @pl.when(jnp.logical_and(row >= i * size, row < (i + 1) * size))
                def _():
                    rows = source.at[pl.ds(pl.multiple_of(row - i * size, HD), depth[n])]
                    pltpu.make_async_copy(rows, to, sems.at[p, n]).start()

            rows = split[0].at[pl.ds(0, depth[n])]
            copies[p].append(pltpu.make_async_copy(rows, to, sems.at[p, n]))
    for n, part in enumerate(parts):
        wide[:, sum(depth[:n]) : sum(depth[: n + 1])] = part[...]
    for p in range(len(sources)):
        for copy in copies[p]:
            copy.wait()
        cols = pl.ds(pl.multiple_of(starts_ref[p], HD), width)
        store(p, cols, jnp.dot(wide[...], weights[p], preferred_element_type=jnp.float32))


def split_refs(refs, splits):
    grouped = []
    for split in splits:
        grouped.append(refs[:split])
        refs = refs[split:]
    return grouped, refs


def add_kernel(offsets, splits, starts_ref, rows_ref, *refs):
    parts = refs[: len(offsets)]
    sources, refs = split_refs(refs[len(offsets) :], splits)
    before_ref, mod_ref, out_ref, weights, wide, sems = refs

    def store(p, cols, summed):
        out_ref[:, cols] = before_ref[:, cols].astype(jnp.float32) + mod_ref[2:3, cols] * summed

    multiply(parts, offsets, starts_ref, rows_ref, sources, weights, sems, wide, store)


def finish_kernel(offsets, splits, starts_ref, rows_ref, coef_ref, *refs):
    parts = refs[: len(offsets)]
    sources, refs = split_refs(refs[len(offsets) :], splits)
    before_ref, mod_ref, head_ref, latent_ref, weight_ref, out_ref, sent_ref = refs[:7]
    weights, wide, sems, mixed, extra = refs[7:]
    count = len(splits)
    width = weights.shape[2]
    copies = []
    for p in range(count):
        cols = pl.ds(pl.multiple_of(starts_ref[p], HD), width)
        copies.append(
            pltpu.make_async_copy(before_ref.at[:, cols], mixed.at[:, cols], extra.at[p])
        )
        copies[p].start()

    def store(p, cols, summed):
        copies[p].wait()
        mixed[:, cols] += mod_ref[2:3, cols] * summed

    multiply(parts, offsets, starts_ref, rows_ref, sources, weights, sems, wide, store)
    normed = layer_norm(mixed[...]) * (1.0 + mod_ref[4:5, :]) + mod_ref[3:4, :]
    velocity = lax.dot_general(
        head_ref[...],
        normed.astype(jnp.bfloat16),
        (((1,), (1,)), ((), ())),
        preferred_element_type=jnp.float32,
    )
    channels = velocity.shape[0]
    base, weight = latent_ref[...], weight_ref[...]
    moved = (base + coef_ref[1] * velocity) * weight
    guess = (base - coef_ref[0] * velocity) * weight
    out_ref[:channels, :] = moved
    out_ref[channels:, :] = guess
    sent_ref[:channels, :] = moved.astype(jnp.bfloat16)
    sent_ref[channels:, :] = guess.astype(jnp.bfloat16)


def accumulate(parts, offsets, starts, firsts, pieces, before, modulation, last=None):
    rows, width = before.shape
    depth = sum(part.shape[1] for part in parts)
    count = len(pieces)
    splits = [len(piece) for piece in pieces]
    pieces = [array for piece in pieces for array in piece]
    smem = pl.BlockSpec(memory_space=pltpu.SMEM)
    vmem = pl.BlockSpec(memory_space=pltpu.VMEM)
    hbm = pl.BlockSpec(memory_space=pl.ANY)
    scratch = [
        pltpu.VMEM((count, depth, pieces[0].shape[1]), jnp.bfloat16),
        pltpu.VMEM((rows, depth), jnp.bfloat16),
        pltpu.SemaphoreType.DMA((count, len(parts))),
    ]
    params = dict(
        compiler_params=pltpu.CompilerParams(vmem_limit_bytes=36 * MIB),
    )
    if last is None:
        aliased = before.dtype == jnp.float32
        return pl.pallas_call(
            functools.partial(add_kernel, offsets, splits),
            in_specs=[smem] * 2 + [vmem] * len(parts) + [hbm] * len(pieces) + [vmem] * 2,
            out_specs=vmem,
            out_shape=jax.ShapeDtypeStruct((rows, width), jnp.float32),
            scratch_shapes=scratch,
            input_output_aliases={2 + len(parts) + len(pieces): 0} if aliased else {},
            name="add_parts",
            **params,
        )(starts, firsts, *parts, *pieces, before, modulation)
    coef, head, latent, weight = last
    channels = head.shape[0]
    return pl.pallas_call(
        functools.partial(finish_kernel, offsets, splits),
        in_specs=[smem] * 3 + [vmem] * len(parts) + [hbm] * (len(pieces) + 1) + [vmem] * 4,
        out_specs=[vmem, vmem],
        out_shape=[
            jax.ShapeDtypeStruct((2 * channels, rows), jnp.float32),
            jax.ShapeDtypeStruct((2 * channels, rows), jnp.bfloat16),
        ],
        scratch_shapes=scratch
        + [pltpu.VMEM((rows, width), jnp.float32), pltpu.SemaphoreType.DMA((count,))],
        name="finish",
        **params,
    )(starts, firsts, coef, *parts, *pieces, before, modulation, head, latent, weight)


def shards(hidden, modulation, w_qkv, w_out, w_head, latent, weights_int, step_index):
    local = hidden[0]
    rows = local.shape[0]
    devices = lax.axis_size("seq")
    tiles = lax.axis_size("tile")
    groups = lax.axis_size("group")
    place, tile, group = lax.axis_index("seq"), lax.axis_index("tile"), lax.axis_index("group")
    far, near = bits_of(tiles)[:-1], bits_of(tiles)[-1]

    weight = weights_int.astype(jnp.float32)
    joins = [
        (t * devices + s, (t + 1) * devices + s - (devices - 2))
        for t in range(tiles - 1)
        for s in range(devices - 2, devices)
    ]
    joins += [
        (t * devices + s, (t - 1) * devices + s + (devices - 2))
        for t in range(1, tiles)
        for s in range(2)
    ]
    norms = weight + lax.ppermute(
        weight.astype(jnp.bfloat16), ("tile", "seq"), joins
    ).astype(jnp.float32)

    height = w_qkv.shape[0]
    ragged = height % HD != 0
    row_starts = jnp.stack([(tile ^ d) * height for d in range(tiles)]).astype(jnp.int32)
    if ragged:
        row_starts = jnp.zeros((1,), jnp.int32)
    normed = norm_rows(local, modulation, row_starts, 0, rows)
    hops = arrivals(devices)
    blocks_by = {0: normed}

    def hop(step):
        for way in (1, -1):
            blocks_by[way * step] = lax.ppermute(
                blocks_by[way * (step - 1)], "seq", step_pairs(devices, step, way)
            )

    def arrival(number):
        wanted = [hops[s][number] for s in range(devices)]
        names = sorted(set(wanted))
        return [names.index(name) for name in wanted], [blocks_by[name] for name in names]

    part = w_out.shape[1] // groups
    share = lax.dynamic_slice_in_dim(w_out, group * part, part, axis=1)
    narrow = part % HD != 0
    columns = {(0, 0): lax.all_gather(share, "seq", axis=0, tiled=True)}

    blocks = {0: w_qkv}
    if not ragged:
        blocks[near] = swap(w_qkv, "tile", near)
        for bit in far:
            blocks.update(
                {d ^ bit: swap(blocks[d], "tile", bit) for d in list(blocks) if d != near}
            )
    hop(1)

    table = [
        [([s] + [s - hop for hop in hops[s]]).index((s + turn) % devices) for turn in range(devices)]
        for s in range(devices)
    ]
    slots = jnp.asarray(table, jnp.int32)[place]
    order = [(d, g) for d in range(tiles) for g in range(groups)]
    starts = jnp.stack(
        [
            (tile ^ d) * (part * groups) + lax.rem(group - g + groups, groups) * part
            for d, g in order
        ]
    ).astype(jnp.int32)
    if narrow:
        order, starts = [(0, 0)], jnp.zeros((1,), jnp.int32)
    features = w_out.shape[0]
    firsts = jnp.stack(
        [lax.rem(place - turn + devices, devices) * features for turn in range(devices)]
    ).astype(jnp.int32)
    index = step_index[0].astype(jnp.float32)
    now = noise_level(index, NSTEPS)
    coef = jnp.stack([now, noise_level(index + 1.0, NSTEPS) - now])
    blocks, columns, blocks_by, slots, starts, firsts, coef, norms = lax.optimization_barrier(
        (blocks, columns, blocks_by, slots, starts, firsts, coef, norms)
    )
    if ragged:
        blocks[0] = lax.all_gather(blocks[0], "tile", axis=0, tiled=True)
    else:
        blocks.update(
            {d ^ near: swap(blocks[d], "tile", near) for d in list(blocks) if d not in (0, near)}
        )
    blocks = [blocks[d] for d in range(len(blocks))]
    if narrow:
        columns[0, 0] = lax.all_gather(columns[0, 0].T, ("tile", "group"), axis=0, tiled=True).T
    else:
        for bit in far:
            columns.update({(d ^ bit, 0): swap(columns[d, 0], "tile", bit) for d, _ in list(columns)})
        for turn in range(1, groups):
            columns[0, turn] = turned(columns[0, 0], "group", turn)

    at = place.reshape(1)
    known, plan, sources = [], [[0] * devices], [normed]
    for number in range(devices - 2):
        if number + 2 < devices:
            hop(number + 2)
        choices, found = arrival(number)
        plan, sources = plan + [choices], sources + found
        known.append(project(at, plan, sources, blocks))
        plan, sources = [], []
        if number + 3 < devices:
            blocks_by, known = lax.optimization_barrier((blocks_by, known))
    if not narrow:
        mine = lax.optimization_barrier((columns[0, 0], known[0]))[0]
        columns[near, 0] = swap(mine, "tile", near)
    columns = {key: [value] for key, value in columns.items()}
    for turn in range(1, groups) if not narrow else []:
        columns.update(
            {
                (d, turn): [turned(columns[d, 0][0], "group", turn)]
                for d in range(1, tiles)
                if d & near == 0 and (groups != 2 or len(far) != 1)
            }
        )
    if groups == 2 and len(far) == 1 and not narrow:
        bit, half = far[0], columns[0, 0][0].shape[0] // 2
        columns[bit, 1] = [
            turned(columns[bit, 0][0][:half], "group", 1),
            swap(columns[0, 1][0][half:], "tile", bit),
        ]
    blocks_by, known, columns = lax.optimization_barrier((blocks_by, known, columns))
    if not narrow:
        columns.update(
            {
                (d ^ near, g): [swap(array, "tile", near) for array in columns[d, g]]
                for d, g in list(columns)
                if (d ^ near, g) not in columns
            }
        )
    heads = w_qkv.shape[1] // (3 * HD)
    many = heads - heads // 3
    halves = [(0, many), (many, heads - many)]
    turns = sorted(range(1, devices), key=lambda turn: -min(turn, devices - turn))
    choices, found = arrival(devices - 2)
    attended = attend(at, slots, [choices], found, known, blocks, *halves[0])
    attended, columns, found = lax.optimization_barrier((attended, columns, found))
    received = [[turned(attended[turn], "seq", turn) for turn in turns]]
    own = [attended[0]]
    attended = attend(at, slots, [choices], found, known, blocks, *halves[1])
    attended, received = lax.optimization_barrier((attended, received))
    received.append([turned(attended[turn], "seq", turn) for turn in turns])
    own.append(attended[0])
    pieces = [columns[key] for key in order]
    offsets = [[(turn, start * HD) for turn in turns] for start, _ in halves]
    mixed = accumulate(
        own + received[0],
        [(0, start * HD) for start, _ in halves] + offsets[0],
        starts,
        firsts,
        pieces,
        local,
        modulation,
    )
    weighted, to_join = accumulate(
        received[1],
        offsets[1],
        starts,
        firsts,
        pieces,
        mixed,
        modulation,
        (coef, w_head.T, latent[0].T, weight),
    )
    other = lax.ppermute(to_join, ("tile", "seq"), joins).astype(jnp.float32)
    joined = (weighted + other) / norms
    channels = w_head.shape[1]
    return (joined[:channels].T[None], joined[channels:].T[None])


def solution(mesh):
    in_specs = (
        P(("group", "tile"), "seq", None),
        P("group", None),
        P("tile", "seq"),
        P("seq", "tile"),
        P(),
        P(("group", "tile"), "seq", None),
        P(("group", "tile"), "seq"),
        P("group"),
    )
    out_specs = (P(("group", "tile"), "seq", None), P(("group", "tile"), "seq", None))
    return jax.shard_map(shards, mesh=mesh, in_specs=in_specs, out_specs=out_specs, check_vma=False)
```

```python
import functools
import math

import jax
import jax.numpy as jnp
from jax import lax
from jax.experimental import pallas as pl
from jax.experimental.pallas import tpu as pltpu
from jax.sharding import PartitionSpec as P

HD = 128
NSTEPS = 28
MIB = 1 << 20


def swap(value, axis, bit):
    count = lax.axis_size(axis)
    return lax.ppermute(value, axis, [(i, i ^ bit) for i in range(count)])


def bits_of(count):
    far = [1 << n for n in range(1, count.bit_length() - 1)]
    return far + [1]


def noise_level(index, steps):
    level = 1.0 - index / steps
    return 3.0 * level / (1.0 + 2.0 * level)


def turned(value, axis, turn):
    count = lax.axis_size(axis)
    return lax.ppermute(value, axis, [(i, (i + turn) % count) for i in range(count)])


def step_pairs(count, step, way):
    if way > 0:
        return [(s, s + 1) for s in range(step - 1, count - 1)]
    return [(s, s - 1) for s in range(1, count - step + 1)]


def arrivals(count):
    return [
        sorted((s - home for home in range(count) if home != s), key=lambda hop: (abs(hop), -hop))
        for s in range(count)
    ]


def layer_norm(values):
    mean = jnp.mean(values, axis=-1, keepdims=True)
    centred = values - mean
    spread = jnp.mean(centred * centred, axis=-1, keepdims=True)
    return centred * lax.rsqrt(spread + 1e-06)


def root_norm(values):
    spread = jnp.mean(values * values, axis=-1, keepdims=True)
    return (values * lax.rsqrt(spread + 1e-06)).astype(jnp.bfloat16)


def norm_kernel(blocks, starts_ref, hidden_ref, mod_ref, out_ref):
    local = hidden_ref[...].astype(jnp.float32)
    mean = jnp.mean(local, axis=-1, keepdims=True)
    centred = local - mean
    spread = jnp.mean(centred * centred, axis=-1, keepdims=True)
    scaling = lax.rsqrt(spread + 1e-06)
    width = hidden_ref.shape[1] // blocks
    for n in range(blocks):
        taken = pl.ds(pl.multiple_of(starts_ref[n], HD), width)
        values = (hidden_ref[:, taken].astype(jnp.float32) - mean) * scaling
        values = values * (1.0 + mod_ref[1:2, taken]) + mod_ref[0:1, taken]
        out_ref[:, n * width : (n + 1) * width] = values.astype(jnp.bfloat16)


def norm_rows(hidden, modulation, starts, first, rows):
    width = hidden.shape[1]
    block = math.gcd(math.gcd(first, rows), 64)
    return pl.pallas_call(
        functools.partial(norm_kernel, starts.shape[0]),
        grid=(rows // block,),
        in_specs=[
            pl.BlockSpec(memory_space=pltpu.SMEM),
            pl.BlockSpec((block, width), lambda i: (first // block + i, 0)),
            pl.BlockSpec(modulation.shape, lambda i: (0, 0)),
        ],
        out_specs=pl.BlockSpec((block, width), lambda i: (i, 0)),
        out_shape=jax.ShapeDtypeStruct((rows, width), jnp.bfloat16),
        name="norm_in",
    )(starts, hidden, modulation)


def product(x_ref, blocks):
    height = x_ref.shape[1] // len(blocks)
    total = 0.0
    for n, block in enumerate(blocks):
        total += jnp.dot(
            x_ref[:, n * height : (n + 1) * height],
            block[...],
            preferred_element_type=jnp.float32,
        )
    return total


def load(place, choices, refs, to, sem):
    for n, ref in enumerate(refs):
        wanted = functools.reduce(
            jnp.logical_or, [place == s for s in range(len(choices)) if choices[s] == n]
        )

        @pl.when(wanted)
        def _():
            pltpu.make_async_copy(ref, to, sem).start()

    return pltpu.make_async_copy(refs[0], to, sem)


def load_all(place, plan, refs, tokens, sems):
    rows = tokens.shape[0] // len(plan)
    copies, used = [], 0
    for n, choices in enumerate(plan):
        many = max(choices) + 1
        to = tokens.at[pl.ds(n * rows, rows)]
        copies.append(load(place, choices, refs[used : used + many], to, sems.at[n]))
        used += many
    for copy in copies:
        copy.wait()


def project_kernel(plan, blocks, place_ref, *refs):
    w_refs = refs[:blocks]
    sources, (q_ref, k_ref, v_ref, tokens, sems) = refs[blocks:-5], refs[-5:]

    @pl.when(pl.program_id(0) == 0)
    def _():
        load_all(place_ref[0], plan, sources, tokens, sems)

    proj = product(tokens, w_refs)
    for h in range(q_ref.shape[0]):
        query, key, value = (proj[:, (3 * h + i) * HD : (3 * h + i + 1) * HD] for i in range(3))
        q_ref[h] = root_norm(query)
        k_ref[h] = root_norm(key)
        v_ref[h] = value.astype(jnp.bfloat16)


def project(place, plan, sources, blocks):
    rows, width = sources[0].shape
    length = rows * len(plan)
    total = blocks[0].shape[1]
    heads = total // (3 * HD)
    many = 2 if heads % 2 == 0 else 1
    out = jax.ShapeDtypeStruct((heads, length, HD), jnp.bfloat16)
    return pl.pallas_call(
        functools.partial(project_kernel, plan, len(blocks)),
        grid=(heads // many,),
        in_specs=[pl.BlockSpec(memory_space=pltpu.SMEM)]
        + [pl.BlockSpec((width // len(blocks), many * 3 * HD), lambda h: (0, h))] * len(blocks)
        + [pl.BlockSpec(memory_space=pl.ANY)] * len(sources),
        out_specs=[pl.BlockSpec((many, length, HD), lambda h: (h, 0, 0))] * 3,
        out_shape=[out] * 3,
        scratch_shapes=[
            pltpu.VMEM((length, width), jnp.bfloat16),
            pltpu.SemaphoreType.DMA((len(plan),)),
        ],
        compiler_params=pltpu.CompilerParams(vmem_limit_bytes=42 * MIB),
        name="project",
    )(place, *blocks, *sources)


def weigh(query, key, values):
    scores = lax.dot_general(
        query, key, (((1,), (1,)), ((), ())), preferred_element_type=jnp.float32
    )
    expo = jnp.exp(scores * (1.0 / math.sqrt(HD))).astype(jnp.bfloat16)
    return jnp.dot(expo, values, preferred_element_type=jnp.float32)


def gather_known(known, counts, queries, keys, values):
    at = 0
    for n, count in enumerate(counts):
        queries[at : at + count] = known[3 * n][0]
        keys[at : at + count] = known[3 * n + 1][0]
        values[at : at + count, :HD] = known[3 * n + 2][0]
        at += count


def early_kernel(counts, rows, *refs):
    known, (out_ref, queries, keys, values) = refs[:-4], refs[-4:]

    @pl.when(pl.program_id(0) == 0)
    def _():
        values[:, HD:] = jnp.ones((sum(counts), HD), jnp.bfloat16)

    gather_known(known, counts, queries, keys, values)
    for first in range(0, sum(counts), rows):
        part = slice(first, first + rows)
        out_ref[0, part] = weigh(queries[part], keys[...], values[...])


def early(known, rows):
    counts = [three[0].shape[1] for three in known]
    heads, length = known[0][0].shape[0], sum(counts)
    return pl.pallas_call(
        functools.partial(early_kernel, counts, rows),
        grid=(heads,),
        in_specs=[
            pl.BlockSpec((1, count, HD), lambda h: (h, 0, 0)) for count in counts for _ in range(3)
        ],
        out_specs=pl.BlockSpec((1, length, 2 * HD), lambda h: (h, 0, 0)),
        out_shape=jax.ShapeDtypeStruct((heads, length, 2 * HD), jnp.float32),
        scratch_shapes=[
            pltpu.VMEM((length, HD), jnp.bfloat16),
            pltpu.VMEM((length, HD), jnp.bfloat16),
            pltpu.VMEM((length, 2 * HD), jnp.bfloat16),
        ],
        compiler_params=pltpu.CompilerParams(vmem_limit_bytes=42 * MIB),
        name="early",
    )(*(value for three in known for value in three))


def attend_kernel(plan, blocks, counts, place_ref, slots_ref, *refs):
    w_refs, before_ref, refs = refs[:blocks], refs[blocks], refs[blocks + 1 :]
    known, refs = refs[: 3 * len(counts)], refs[3 * len(counts) :]
    queries, keys, values, sums, tokens, sems = refs[-6:]
    devices = slots_ref.shape[0]
    sources, outs = refs[: -6 - devices], refs[-6 - devices : -6]
    start, rows = sum(counts), tokens.shape[0]

    @pl.when(pl.program_id(0) == 0)
    def _():
        values[:, HD:] = jnp.ones((start + rows, HD), jnp.bfloat16)
        load_all(place_ref[0], plan, sources, tokens, sems)

    proj = product(tokens, w_refs)
    gather_known(known, counts, queries, keys, values)
    queries[start:] = root_norm(proj[:, :HD])
    keys[start:] = root_norm(proj[:, HD : 2 * HD])
    values[start:, :HD] = proj[:, 2 * HD :].astype(jnp.bfloat16)
    sums[:start] = before_ref[0]
    sums[start:] = weigh(queries[start:], keys[:start], values[:start])
    for turn in range(devices):
        part = pl.ds(pl.multiple_of(slots_ref[turn] * rows, rows), rows)
        mixed = sums[part] + weigh(queries[part], keys[start:], values[start:])
        outs[turn][...] = (mixed[:, :HD] / mixed[:, HD:]).astype(jnp.bfloat16)


def attend(place, slots, plan, sources, known, before, blocks, start, heads):
    devices = slots.shape[0]
    rows, width = sources[0].shape
    counts = [three[0].shape[1] for three in known]
    length = rows + sum(counts)
    smem = pl.BlockSpec(memory_space=pltpu.SMEM)
    out = jax.ShapeDtypeStruct((rows, heads * HD), jnp.bfloat16)
    return pl.pallas_call(
        functools.partial(attend_kernel, plan, len(blocks), counts),
        grid=(heads,),
        in_specs=[smem, smem]
        + [pl.BlockSpec((width // len(blocks), 3 * HD), lambda h: (0, start + h))] * len(blocks)
        + [pl.BlockSpec((1, length - rows, 2 * HD), lambda h: (start + h, 0, 0))]
        + [
            pl.BlockSpec((1, count, HD), lambda h: (start + h, 0, 0))
            for count in counts
            for _ in range(3)
        ]
        + [pl.BlockSpec(memory_space=pl.ANY)] * len(sources),
        out_specs=[pl.BlockSpec((rows, HD), lambda h: (0, h))] * devices,
        out_shape=[out] * devices,
        scratch_shapes=[
            pltpu.VMEM((length, HD), jnp.bfloat16),
            pltpu.VMEM((length, HD), jnp.bfloat16),
            pltpu.VMEM((length, 2 * HD), jnp.bfloat16),
            pltpu.VMEM((length, 2 * HD), jnp.float32),
            pltpu.VMEM((rows, width), jnp.bfloat16),
            pltpu.SemaphoreType.DMA((1,)),
        ],
        compiler_params=pltpu.CompilerParams(vmem_limit_bytes=42 * MIB),
        name="attend",
    )(place, slots, *blocks, before, *(value for three in known for value in three), *sources)


def multiply(parts, offsets, starts_ref, rows_ref, sources, weights, sems, wide, store):
    depth = [part.shape[1] for part in parts]
    width = weights.shape[2]
    copies = []
    for p, split in enumerate(sources):
        copies.append([])
        for n, (turn, offset) in enumerate(offsets):
            to = weights.at[p, pl.ds(sum(depth[:n]), depth[n])]
            row = rows_ref[turn] + offset
            size = split[0].shape[0]
            for i, source in enumerate(split):
                if len(split) == 1:
                    rows = source.at[pl.ds(pl.multiple_of(row, HD), depth[n])]
                    pltpu.make_async_copy(rows, to, sems.at[p, n]).start()
                    continue

                @pl.when(jnp.logical_and(row >= i * size, row < (i + 1) * size))
                def _():
                    rows = source.at[pl.ds(pl.multiple_of(row - i * size, HD), depth[n])]
                    pltpu.make_async_copy(rows, to, sems.at[p, n]).start()

            rows = split[0].at[pl.ds(0, depth[n])]
            copies[p].append(pltpu.make_async_copy(rows, to, sems.at[p, n]))
    for n, part in enumerate(parts):
        wide[:, sum(depth[:n]) : sum(depth[: n + 1])] = part[...]
    for p in range(len(sources)):
        for copy in copies[p]:
            copy.wait()
        cols = pl.ds(pl.multiple_of(starts_ref[p], HD), width)
        store(p, cols, jnp.dot(wide[...], weights[p], preferred_element_type=jnp.float32))


def split_refs(refs, splits):
    grouped = []
    for split in splits:
        grouped.append(refs[:split])
        refs = refs[split:]
    return grouped, refs


def add_kernel(offsets, splits, starts_ref, rows_ref, *refs):
    parts = refs[: len(offsets)]
    sources, refs = split_refs(refs[len(offsets) :], splits)
    before_ref, mod_ref, out_ref, weights, wide, sems = refs

    def store(p, cols, summed):
        out_ref[:, cols] = before_ref[:, cols].astype(jnp.float32) + mod_ref[2:3, cols] * summed

    multiply(parts, offsets, starts_ref, rows_ref, sources, weights, sems, wide, store)


def finish_kernel(offsets, splits, starts_ref, rows_ref, coef_ref, *refs):
    parts = refs[: len(offsets)]
    sources, refs = split_refs(refs[len(offsets) :], splits)
    before_ref, mod_ref, head_ref, latent_ref, weight_ref, out_ref, sent_ref = refs[:7]
    weights, wide, sems, mixed, extra = refs[7:]
    count = len(splits)
    width = weights.shape[2]
    copies = []
    for p in range(count):
        cols = pl.ds(pl.multiple_of(starts_ref[p], HD), width)
        copies.append(
            pltpu.make_async_copy(before_ref.at[:, cols], mixed.at[:, cols], extra.at[p])
        )
        copies[p].start()

    def store(p, cols, summed):
        copies[p].wait()
        mixed[:, cols] += mod_ref[2:3, cols] * summed

    multiply(parts, offsets, starts_ref, rows_ref, sources, weights, sems, wide, store)
    normed = layer_norm(mixed[...]) * (1.0 + mod_ref[4:5, :]) + mod_ref[3:4, :]
    velocity = lax.dot_general(
        normed.astype(jnp.bfloat16),
        head_ref[...],
        (((1,), (1,)), ((), ())),
        preferred_element_type=jnp.float32,
    ).T
    channels = velocity.shape[0]
    base, weight = latent_ref[...], weight_ref[...]
    moved = (base + coef_ref[1] * velocity) * weight
    guess = (base - coef_ref[0] * velocity) * weight
    out_ref[:channels, :] = moved
    out_ref[channels:, :] = guess
    sent_ref[:channels, :] = moved.astype(jnp.bfloat16)
    sent_ref[channels:, :] = guess.astype(jnp.bfloat16)


def accumulate(parts, offsets, starts, firsts, pieces, before, modulation, last=None):
    rows, width = before.shape
    depth = sum(part.shape[1] for part in parts)
    count = len(pieces)
    splits = [len(piece) for piece in pieces]
    pieces = [array for piece in pieces for array in piece]
    smem = pl.BlockSpec(memory_space=pltpu.SMEM)
    vmem = pl.BlockSpec(memory_space=pltpu.VMEM)
    hbm = pl.BlockSpec(memory_space=pl.ANY)
    scratch = [
        pltpu.VMEM((count, depth, pieces[0].shape[1]), jnp.bfloat16),
        pltpu.VMEM((rows, depth), jnp.bfloat16),
        pltpu.SemaphoreType.DMA((count, len(parts))),
    ]
    params = dict(
        compiler_params=pltpu.CompilerParams(vmem_limit_bytes=60 * MIB),
    )
    if last is None:
        aliased = before.dtype == jnp.float32
        return pl.pallas_call(
            functools.partial(add_kernel, offsets, splits),
            in_specs=[smem] * 2 + [vmem] * len(parts) + [hbm] * len(pieces) + [vmem] * 2,
            out_specs=vmem,
            out_shape=jax.ShapeDtypeStruct((rows, width), jnp.float32),
            scratch_shapes=scratch,
            input_output_aliases={2 + len(parts) + len(pieces): 0} if aliased else {},
            name="add_parts",
            **params,
        )(starts, firsts, *parts, *pieces, before, modulation)
    coef, head, latent, weight = last
    channels = head.shape[0]
    return pl.pallas_call(
        functools.partial(finish_kernel, offsets, splits),
        in_specs=[smem] * 3 + [vmem] * len(parts) + [hbm] * (len(pieces) + 1) + [vmem] * 4,
        out_specs=[vmem, vmem],
        out_shape=[
            jax.ShapeDtypeStruct((2 * channels, rows), jnp.float32),
            jax.ShapeDtypeStruct((2 * channels, rows), jnp.bfloat16),
        ],
        scratch_shapes=scratch
        + [pltpu.VMEM((rows, width), jnp.float32), pltpu.SemaphoreType.DMA((count,))],
        name="finish",
        **params,
    )(starts, firsts, coef, *parts, *pieces, before, modulation, head, latent, weight)


def shards(hidden, modulation, w_qkv, w_out, w_head, latent, weights_int, step_index):
    local = hidden[0]
    rows = local.shape[0]
    devices = lax.axis_size("seq")
    tiles = lax.axis_size("tile")
    groups = lax.axis_size("group")
    place, tile, group = lax.axis_index("seq"), lax.axis_index("tile"), lax.axis_index("group")
    far, near = bits_of(tiles)[:-1], bits_of(tiles)[-1]

    weight = weights_int.astype(jnp.float32)
    joins = [
        (t * devices + s, (t + 1) * devices + s - (devices - 2))
        for t in range(tiles - 1)
        for s in range(devices - 2, devices)
    ]
    joins += [
        (t * devices + s, (t - 1) * devices + s + (devices - 2))
        for t in range(1, tiles)
        for s in range(2)
    ]
    norms = weight + lax.ppermute(
        weight.astype(jnp.bfloat16), ("tile", "seq"), joins
    ).astype(jnp.float32)

    height = w_qkv.shape[0]
    ragged = height % HD != 0
    row_starts = jnp.stack([(tile ^ d) * height for d in range(tiles)]).astype(jnp.int32)
    if ragged:
        row_starts = jnp.zeros((1,), jnp.int32)
    normed = norm_rows(local, modulation, row_starts, 0, rows)
    hops = arrivals(devices)
    blocks_by = {0: normed}

    def hop(step):
        for way in (1, -1):
            blocks_by[way * step] = lax.ppermute(
                blocks_by[way * (step - 1)], "seq", step_pairs(devices, step, way)
            )

    def arrival(number):
        wanted = [hops[s][number] for s in range(devices)]
        names = sorted(set(wanted))
        return [names.index(name) for name in wanted], [blocks_by[name] for name in names]

    part = w_out.shape[1] // groups
    share = lax.dynamic_slice_in_dim(w_out, group * part, part, axis=1)
    narrow = part % HD != 0
    columns = {(0, 0): lax.all_gather(share, "seq", axis=0, tiled=True)}

    blocks = {0: w_qkv}
    if not ragged:
        blocks[near] = swap(w_qkv, "tile", near)
        for bit in far:
            blocks.update(
                {d ^ bit: swap(blocks[d], "tile", bit) for d in list(blocks) if d != near}
            )
    hop(1)

    table = [
        [([s] + [s - hop for hop in hops[s]]).index((s + turn) % devices) for turn in range(devices)]
        for s in range(devices)
    ]
    slots = jnp.asarray(table, jnp.int32)[place]
    order = [(d, g) for d in range(tiles) for g in range(groups)]
    starts = jnp.stack(
        [
            (tile ^ d) * (part * groups) + lax.rem(group - g + groups, groups) * part
            for d, g in order
        ]
    ).astype(jnp.int32)
    if narrow:
        order, starts = [(0, 0)], jnp.zeros((1,), jnp.int32)
    features = w_out.shape[0]
    firsts = jnp.stack(
        [lax.rem(place - turn + devices, devices) * features for turn in range(devices)]
    ).astype(jnp.int32)
    index = step_index[0].astype(jnp.float32)
    now = noise_level(index, NSTEPS)
    coef = jnp.stack([now, noise_level(index + 1.0, NSTEPS) - now])
    blocks, columns, blocks_by, slots, starts, firsts, coef, norms = lax.optimization_barrier(
        (blocks, columns, blocks_by, slots, starts, firsts, coef, norms)
    )
    if ragged:
        blocks[0] = lax.all_gather(blocks[0], "tile", axis=0, tiled=True)
    else:
        blocks.update(
            {d ^ near: swap(blocks[d], "tile", near) for d in list(blocks) if d not in (0, near)}
        )
    blocks = [blocks[d] for d in range(len(blocks))]
    if narrow:
        columns[0, 0] = lax.all_gather(columns[0, 0].T, ("tile", "group"), axis=0, tiled=True).T
    else:
        for bit in far:
            columns.update({(d ^ bit, 0): swap(columns[d, 0], "tile", bit) for d, _ in list(columns)})
        for turn in range(1, groups):
            columns[0, turn] = turned(columns[0, 0], "group", turn)

    at = place.reshape(1)
    known, plan, sources = [], [[0] * devices], [normed]
    for number in range(devices - 2):
        if number + 2 < devices:
            hop(number + 2)
        choices, found = arrival(number)
        plan, sources = plan + [choices], sources + found
        known.append(project(at, plan, sources, blocks))
        plan, sources = [], []
        if number + 3 < devices:
            blocks_by, known = lax.optimization_barrier((blocks_by, known))
    if not narrow:
        mine = lax.optimization_barrier((columns[0, 0], known[0]))[0]
        columns[near, 0] = swap(mine, "tile", near)
    before = early(known, rows)
    columns = {key: [value] for key, value in columns.items()}
    diagonal = groups == 2 and len(far) == 1 and not narrow
    crossing = ()
    if diagonal:
        bit, half = far[0], columns[0, 0][0].shape[0] // 2
        crossing = (columns[bit, 0][0][:half], columns[0, 1][0][half:])
    blocks_by, known, before, columns, crossing = lax.optimization_barrier(
        (blocks_by, known, before, columns, crossing)
    )
    late = {}
    if diagonal:
        late[bit, 1] = [turned(crossing[0], "group", 1), swap(crossing[1], "tile", bit)]
    elif not narrow:
        for turn in range(1, groups):
            for d in range(1, tiles):
                if d & near == 0:
                    late[d, turn] = [turned(columns[d, 0][0], "group", turn)]
    if not narrow:
        columns.update(
            {
                (d ^ near, g): [swap(array, "tile", near) for array in columns[d, g]]
                for d, g in list(columns)
                if (d ^ near, g) not in columns
            }
        )
    heads = w_qkv.shape[1] // (3 * HD)
    many = heads - heads // 2
    halves = [(0, many), (many, heads - many)]
    turns = sorted(range(1, devices), key=lambda turn: -min(turn, devices - turn))
    choices, found = arrival(devices - 2)
    attended = attend(at, slots, [choices], found, known, before, blocks, *halves[0])
    attended, columns, found = lax.optimization_barrier((attended, columns, found))
    received = [[turned(attended[turn], "seq", turn) for turn in turns]]
    own = [attended[0]]
    attended = attend(at, slots, [choices], found, known, before, blocks, *halves[1])
    attended, received, late = lax.optimization_barrier((attended, received, late))
    columns.update(late)
    columns.update(
        {(d ^ near, g): [swap(array, "tile", near) for array in late[d, g]] for d, g in late}
    )
    received.append([turned(attended[turn], "seq", turn) for turn in turns])
    own.append(attended[0])
    pieces = [columns[key] for key in order]
    offsets = [[(turn, start * HD) for turn in turns] for start, _ in halves]
    mixed = accumulate(
        own + received[0],
        [(0, start * HD) for start, _ in halves] + offsets[0],
        starts,
        firsts,
        pieces,
        local,
        modulation,
    )
    weighted, to_join = accumulate(
        received[1],
        offsets[1],
        starts,
        firsts,
        pieces,
        mixed,
        modulation,
        (coef, w_head.T, latent[0].T, weight),
    )
    other = lax.ppermute(to_join, ("tile", "seq"), joins).astype(jnp.float32)
    joined = (weighted + other) / norms
    channels = w_head.shape[1]
    return (joined[:channels].T[None], joined[channels:].T[None])


def solution(mesh):
    in_specs = (
        P(("group", "tile"), "seq", None),
        P("group", None),
        P("tile", "seq"),
        P("seq", "tile"),
        P(),
        P(("group", "tile"), "seq", None),
        P(("group", "tile"), "seq"),
        P("group"),
    )
    out_specs = (P(("group", "tile"), "seq", None), P(("group", "tile"), "seq", None))
    return jax.shard_map(shards, mesh=mesh, in_specs=in_specs, out_specs=out_specs, check_vma=False)
```

```python
import functools
import math

import jax
import jax.numpy as jnp
from jax import lax
from jax.experimental import pallas as pl
from jax.experimental.pallas import tpu as pltpu
from jax.sharding import PartitionSpec as P

HD = 128
NSTEPS = 28
MIB = 1 << 20


def swap(value, axis, bit):
    count = lax.axis_size(axis)
    return lax.ppermute(value, axis, [(i, i ^ bit) for i in range(count)])


def bits_of(count):
    far = [1 << n for n in range(1, count.bit_length() - 1)]
    return far + [1]


def noise_level(index, steps):
    level = 1.0 - index / steps
    return 3.0 * level / (1.0 + 2.0 * level)


def turned(value, axis, turn):
    count = lax.axis_size(axis)
    return lax.ppermute(value, axis, [(i, (i + turn) % count) for i in range(count)])


def step_pairs(count, step, way):
    if way > 0:
        return [(s, s + 1) for s in range(step - 1, count - 1)]
    return [(s, s - 1) for s in range(1, count - step + 1)]


def arrivals(count):
    return [
        sorted((s - home for home in range(count) if home != s), key=lambda hop: (abs(hop), -hop))
        for s in range(count)
    ]


def layer_norm(values):
    mean = jnp.mean(values, axis=-1, keepdims=True)
    centred = values - mean
    spread = jnp.mean(centred * centred, axis=-1, keepdims=True)
    return centred * lax.rsqrt(spread + 1e-06)


def root_norm(values):
    spread = jnp.mean(values * values, axis=-1, keepdims=True)
    return (values * lax.rsqrt(spread + 1e-06)).astype(jnp.bfloat16)


def norm_kernel(blocks, starts_ref, hidden_ref, mod_ref, out_ref):
    local = hidden_ref[...].astype(jnp.float32)
    mean = jnp.mean(local, axis=-1, keepdims=True)
    centred = local - mean
    spread = jnp.mean(centred * centred, axis=-1, keepdims=True)
    scaling = lax.rsqrt(spread + 1e-06)
    width = hidden_ref.shape[1] // blocks
    for n in range(blocks):
        taken = pl.ds(pl.multiple_of(starts_ref[n], HD), width)
        values = (hidden_ref[:, taken].astype(jnp.float32) - mean) * scaling
        values = values * (1.0 + mod_ref[1:2, taken]) + mod_ref[0:1, taken]
        out_ref[:, n * width : (n + 1) * width] = values.astype(jnp.bfloat16)


def norm_rows(hidden, modulation, starts, first, rows):
    width = hidden.shape[1]
    block = math.gcd(math.gcd(first, rows), 64)
    return pl.pallas_call(
        functools.partial(norm_kernel, starts.shape[0]),
        grid=(rows // block,),
        in_specs=[
            pl.BlockSpec(memory_space=pltpu.SMEM),
            pl.BlockSpec((block, width), lambda i: (first // block + i, 0)),
            pl.BlockSpec(modulation.shape, lambda i: (0, 0)),
        ],
        out_specs=pl.BlockSpec((block, width), lambda i: (i, 0)),
        out_shape=jax.ShapeDtypeStruct((rows, width), jnp.bfloat16),
        name="norm_in",
    )(starts, hidden, modulation)


def product(x_ref, blocks):
    height = x_ref.shape[1] // len(blocks)
    total = 0.0
    for n, block in enumerate(blocks):
        total += jnp.dot(
            x_ref[:, n * height : (n + 1) * height],
            block[...],
            preferred_element_type=jnp.float32,
        )
    return total


def load(place, choices, refs, to, sem):
    for n, ref in enumerate(refs):
        wanted = functools.reduce(
            jnp.logical_or, [place == s for s in range(len(choices)) if choices[s] == n]
        )

        @pl.when(wanted)
        def _():
            pltpu.make_async_copy(ref, to, sem).start()

    return pltpu.make_async_copy(refs[0], to, sem)


def load_all(place, plan, refs, tokens, sems):
    rows = tokens.shape[0] // len(plan)
    copies, used = [], 0
    for n, choices in enumerate(plan):
        many = max(choices) + 1
        to = tokens.at[pl.ds(n * rows, rows)]
        copies.append(load(place, choices, refs[used : used + many], to, sems.at[n]))
        used += many
    for copy in copies:
        copy.wait()


def project_kernel(plan, blocks, place_ref, *refs):
    w_refs = refs[:blocks]
    sources, (q_ref, k_ref, v_ref, tokens, sems) = refs[blocks:-5], refs[-5:]

    @pl.when(pl.program_id(0) == 0)
    def _():
        load_all(place_ref[0], plan, sources, tokens, sems)

    proj = product(tokens, w_refs)
    for h in range(q_ref.shape[0]):
        query, key, value = (proj[:, (3 * h + i) * HD : (3 * h + i + 1) * HD] for i in range(3))
        q_ref[h] = root_norm(query)
        k_ref[h] = root_norm(key)
        v_ref[h] = value.astype(jnp.bfloat16)


def project(place, plan, sources, blocks):
    rows, width = sources[0].shape
    length = rows * len(plan)
    total = blocks[0].shape[1]
    heads = total // (3 * HD)
    many = 2 if heads % 2 == 0 else 1
    out = jax.ShapeDtypeStruct((heads, length, HD), jnp.bfloat16)
    return pl.pallas_call(
        functools.partial(project_kernel, plan, len(blocks)),
        grid=(heads // many,),
        in_specs=[pl.BlockSpec(memory_space=pltpu.SMEM)]
        + [pl.BlockSpec((width // len(blocks), many * 3 * HD), lambda h: (0, h))] * len(blocks)
        + [pl.BlockSpec(memory_space=pl.ANY)] * len(sources),
        out_specs=[pl.BlockSpec((many, length, HD), lambda h: (h, 0, 0))] * 3,
        out_shape=[out] * 3,
        scratch_shapes=[
            pltpu.VMEM((length, width), jnp.bfloat16),
            pltpu.SemaphoreType.DMA((len(plan),)),
        ],
        compiler_params=pltpu.CompilerParams(vmem_limit_bytes=42 * MIB),
        name="project",
    )(place, *blocks, *sources)


def weigh(query, key, values):
    scores = lax.dot_general(
        query, key, (((1,), (1,)), ((), ())), preferred_element_type=jnp.float32
    )
    expo = jnp.exp(scores * (1.0 / math.sqrt(HD))).astype(jnp.bfloat16)
    return jnp.dot(expo, values, preferred_element_type=jnp.float32)


def gather_known(known, counts, queries, keys, values):
    at = 0
    for n, count in enumerate(counts):
        queries[at : at + count] = known[3 * n][0]
        keys[at : at + count] = known[3 * n + 1][0]
        values[at : at + count, :HD] = known[3 * n + 2][0]
        at += count


def early_kernel(counts, rows, *refs):
    known, (out_ref, queries, keys, values) = refs[:-4], refs[-4:]

    @pl.when(pl.program_id(0) == 0)
    def _():
        values[:, HD:] = jnp.ones((sum(counts), HD), jnp.bfloat16)

    gather_known(known, counts, queries, keys, values)
    for first in range(0, sum(counts), rows):
        part = slice(first, first + rows)
        out_ref[0, part] = weigh(queries[part], keys[...], values[...])


def early(known, rows):
    counts = [three[0].shape[1] for three in known]
    heads, length = known[0][0].shape[0], sum(counts)
    return pl.pallas_call(
        functools.partial(early_kernel, counts, rows),
        grid=(heads,),
        in_specs=[
            pl.BlockSpec((1, count, HD), lambda h: (h, 0, 0)) for count in counts for _ in range(3)
        ],
        out_specs=pl.BlockSpec((1, length, 2 * HD), lambda h: (h, 0, 0)),
        out_shape=jax.ShapeDtypeStruct((heads, length, 2 * HD), jnp.float32),
        scratch_shapes=[
            pltpu.VMEM((length, HD), jnp.bfloat16),
            pltpu.VMEM((length, HD), jnp.bfloat16),
            pltpu.VMEM((length, 2 * HD), jnp.bfloat16),
        ],
        compiler_params=pltpu.CompilerParams(vmem_limit_bytes=42 * MIB),
        name="early",
    )(*(value for three in known for value in three))


def attend_kernel(plan, blocks, counts, place_ref, slots_ref, *refs):
    w_refs, before_ref, refs = refs[:blocks], refs[blocks], refs[blocks + 1 :]
    known, refs = refs[: 3 * len(counts)], refs[3 * len(counts) :]
    queries, keys, values, done, tokens, sems = refs[-6:]
    devices = slots_ref.shape[0]
    sources, outs = refs[: -6 - devices], refs[-6 - devices : -6]
    start, rows = sum(counts), tokens.shape[0]

    @pl.when(pl.program_id(0) == 0)
    def _():
        values[:, HD:] = jnp.ones((start + rows, HD), jnp.bfloat16)
        load_all(place_ref[0], plan, sources, tokens, sems)

    proj = product(tokens, w_refs)
    gather_known(known, counts, queries, keys, values)
    queries[start:] = root_norm(proj[:, :HD])
    keys[start:] = root_norm(proj[:, HD : 2 * HD])
    values[start:, :HD] = proj[:, 2 * HD :].astype(jnp.bfloat16)
    mixed = before_ref[0] + weigh(queries[:start], keys[start:], values[start:])
    done[:start] = (mixed[:, :HD] / mixed[:, HD:]).astype(jnp.bfloat16)
    mixed = weigh(queries[start:], keys[...], values[...])
    done[start:] = (mixed[:, :HD] / mixed[:, HD:]).astype(jnp.bfloat16)
    for turn in range(devices):
        part = pl.ds(pl.multiple_of(slots_ref[turn] * rows, rows), rows)
        outs[turn][...] = done[part]


def attend(place, slots, plan, sources, known, before, blocks, start, heads):
    devices = slots.shape[0]
    rows, width = sources[0].shape
    counts = [three[0].shape[1] for three in known]
    length = rows + sum(counts)
    smem = pl.BlockSpec(memory_space=pltpu.SMEM)
    out = jax.ShapeDtypeStruct((rows, heads * HD), jnp.bfloat16)
    return pl.pallas_call(
        functools.partial(attend_kernel, plan, len(blocks), counts),
        grid=(heads,),
        in_specs=[smem, smem]
        + [pl.BlockSpec((width // len(blocks), 3 * HD), lambda h: (0, start + h))] * len(blocks)
        + [pl.BlockSpec((1, length - rows, 2 * HD), lambda h: (start + h, 0, 0))]
        + [
            pl.BlockSpec((1, count, HD), lambda h: (start + h, 0, 0))
            for count in counts
            for _ in range(3)
        ]
        + [pl.BlockSpec(memory_space=pl.ANY)] * len(sources),
        out_specs=[pl.BlockSpec((rows, HD), lambda h: (0, h))] * devices,
        out_shape=[out] * devices,
        scratch_shapes=[
            pltpu.VMEM((length, HD), jnp.bfloat16),
            pltpu.VMEM((length, HD), jnp.bfloat16),
            pltpu.VMEM((length, 2 * HD), jnp.bfloat16),
            pltpu.VMEM((length, HD), jnp.bfloat16),
            pltpu.VMEM((rows, width), jnp.bfloat16),
            pltpu.SemaphoreType.DMA((1,)),
        ],
        compiler_params=pltpu.CompilerParams(vmem_limit_bytes=42 * MIB),
        name="attend",
    )(place, slots, *blocks, before, *(value for three in known for value in three), *sources)


def multiply(parts, offsets, starts_ref, rows_ref, sources, weights, sems, wide, store):
    depth = [part.shape[1] for part in parts]
    width = weights.shape[2]
    copies = []
    for p, split in enumerate(sources):
        copies.append([])
        for n, (turn, offset) in enumerate(offsets):
            to = weights.at[p, pl.ds(sum(depth[:n]), depth[n])]
            row = rows_ref[turn] + offset
            size = split[0].shape[0]
            for i, source in enumerate(split):
                if len(split) == 1:
                    rows = source.at[pl.ds(pl.multiple_of(row, HD), depth[n])]
                    pltpu.make_async_copy(rows, to, sems.at[p, n]).start()
                    continue

                @pl.when(jnp.logical_and(row >= i * size, row < (i + 1) * size))
                def _():
                    rows = source.at[pl.ds(pl.multiple_of(row - i * size, HD), depth[n])]
                    pltpu.make_async_copy(rows, to, sems.at[p, n]).start()

            rows = split[0].at[pl.ds(0, depth[n])]
            copies[p].append(pltpu.make_async_copy(rows, to, sems.at[p, n]))
    for n, part in enumerate(parts):
        wide[:, sum(depth[:n]) : sum(depth[: n + 1])] = part[...]
    for p in range(len(sources)):
        for copy in copies[p]:
            copy.wait()
        cols = pl.ds(pl.multiple_of(starts_ref[p], HD), width)
        store(p, cols, jnp.dot(wide[...], weights[p], preferred_element_type=jnp.float32))


def split_refs(refs, splits):
    grouped = []
    for split in splits:
        grouped.append(refs[:split])
        refs = refs[split:]
    return grouped, refs


def add_kernel(offsets, splits, starts_ref, rows_ref, *refs):
    parts = refs[: len(offsets)]
    sources, refs = split_refs(refs[len(offsets) :], splits)
    before_ref, mod_ref, out_ref, weights, wide, sems = refs

    def store(p, cols, summed):
        out_ref[:, cols] = before_ref[:, cols].astype(jnp.float32) + mod_ref[2:3, cols] * summed

    multiply(parts, offsets, starts_ref, rows_ref, sources, weights, sems, wide, store)


def finish_kernel(offsets, splits, starts_ref, rows_ref, coef_ref, *refs):
    parts = refs[: len(offsets)]
    sources, refs = split_refs(refs[len(offsets) :], splits)
    before_ref, mod_ref, head_ref, latent_ref, weight_ref, out_ref, sent_ref = refs[:7]
    weights, wide, sems, mixed, extra = refs[7:]
    count = len(splits)
    width = weights.shape[2]
    copies = []
    for p in range(count):
        cols = pl.ds(pl.multiple_of(starts_ref[p], HD), width)
        copies.append(
            pltpu.make_async_copy(before_ref.at[:, cols], mixed.at[:, cols], extra.at[p])
        )
        copies[p].start()

    held = {}

    def store(p, cols, summed):
        copies[p].wait()
        values = mixed[:, cols] + mod_ref[2:3, cols] * summed
        mixed[:, cols] = values
        if p == 0:
            held["base"] = jnp.mean(values, axis=-1, keepdims=True)
        away = values - held["base"]
        sums = (
            jnp.sum(away, axis=-1, keepdims=True),
            jnp.sum(away * away, axis=-1, keepdims=True),
        )
        held["sums"] = [a + b for a, b in zip(held.get("sums", (0.0, 0.0)), sums)]

    multiply(parts, offsets, starts_ref, rows_ref, sources, weights, sems, wide, store)
    total = width * count
    shift = held["sums"][0] / total
    scaling = lax.rsqrt(held["sums"][1] / total - shift * shift + 1e-06)
    mean = held["base"] + shift
    velocity = 0.0
    for p in range(count):
        cols = slice(p * width, (p + 1) * width)
        normed = (mixed[:, cols] - mean) * scaling
        normed = normed * (1.0 + mod_ref[4:5, cols]) + mod_ref[3:4, cols]
        velocity += lax.dot_general(
            normed.astype(jnp.bfloat16),
            head_ref[:, cols],
            (((1,), (1,)), ((), ())),
            preferred_element_type=jnp.float32,
        )
    velocity = velocity.T
    channels = velocity.shape[0]
    base, weight = latent_ref[...], weight_ref[...]
    moved = (base + coef_ref[1] * velocity) * weight
    guess = (base - coef_ref[0] * velocity) * weight
    out_ref[:channels, :] = moved
    out_ref[channels:, :] = guess
    sent_ref[:channels, :] = moved.astype(jnp.bfloat16)
    sent_ref[channels:, :] = guess.astype(jnp.bfloat16)


def accumulate(parts, offsets, starts, firsts, pieces, before, modulation, last=None):
    rows, width = before.shape
    depth = sum(part.shape[1] for part in parts)
    count = len(pieces)
    splits = [len(piece) for piece in pieces]
    pieces = [array for piece in pieces for array in piece]
    smem = pl.BlockSpec(memory_space=pltpu.SMEM)
    vmem = pl.BlockSpec(memory_space=pltpu.VMEM)
    hbm = pl.BlockSpec(memory_space=pl.ANY)
    scratch = [
        pltpu.VMEM((count, depth, pieces[0].shape[1]), jnp.bfloat16),
        pltpu.VMEM((rows, depth), jnp.bfloat16),
        pltpu.SemaphoreType.DMA((count, len(parts))),
    ]
    params = dict(
        compiler_params=pltpu.CompilerParams(vmem_limit_bytes=60 * MIB),
    )
    if last is None:
        aliased = before.dtype == jnp.float32
        return pl.pallas_call(
            functools.partial(add_kernel, offsets, splits),
            in_specs=[smem] * 2 + [vmem] * len(parts) + [hbm] * len(pieces) + [vmem] * 2,
            out_specs=vmem,
            out_shape=jax.ShapeDtypeStruct((rows, width), jnp.float32),
            scratch_shapes=scratch,
            input_output_aliases={2 + len(parts) + len(pieces): 0} if aliased else {},
            name="add_parts",
            **params,
        )(starts, firsts, *parts, *pieces, before, modulation)
    coef, head, latent, weight = last
    channels = head.shape[0]
    return pl.pallas_call(
        functools.partial(finish_kernel, offsets, splits),
        in_specs=[smem] * 3 + [vmem] * len(parts) + [hbm] * (len(pieces) + 1) + [vmem] * 4,
        out_specs=[vmem, vmem],
        out_shape=[
            jax.ShapeDtypeStruct((2 * channels, rows), jnp.float32),
            jax.ShapeDtypeStruct((2 * channels, rows), jnp.bfloat16),
        ],
        scratch_shapes=scratch
        + [pltpu.VMEM((rows, width), jnp.float32), pltpu.SemaphoreType.DMA((count,))],
        name="finish",
        **params,
    )(starts, firsts, coef, *parts, *pieces, before, modulation, head, latent, weight)


def shards(hidden, modulation, w_qkv, w_out, w_head, latent, weights_int, step_index):
    local = hidden[0]
    rows = local.shape[0]
    devices = lax.axis_size("seq")
    tiles = lax.axis_size("tile")
    groups = lax.axis_size("group")
    place, tile, group = lax.axis_index("seq"), lax.axis_index("tile"), lax.axis_index("group")
    far, near = bits_of(tiles)[:-1], bits_of(tiles)[-1]

    weight = weights_int.astype(jnp.float32)
    joins = [
        (t * devices + s, (t + 1) * devices + s - (devices - 2))
        for t in range(tiles - 1)
        for s in range(devices - 2, devices)
    ]
    joins += [
        (t * devices + s, (t - 1) * devices + s + (devices - 2))
        for t in range(1, tiles)
        for s in range(2)
    ]
    norms = weight + lax.ppermute(
        weight.astype(jnp.bfloat16), ("tile", "seq"), joins
    ).astype(jnp.float32)

    height = w_qkv.shape[0]
    ragged = height % HD != 0
    row_starts = jnp.stack([(tile ^ d) * height for d in range(tiles)]).astype(jnp.int32)
    if ragged:
        row_starts = jnp.zeros((1,), jnp.int32)
    normed = norm_rows(local, modulation, row_starts, 0, rows)
    hops = arrivals(devices)
    blocks_by = {0: normed}

    def hop(step):
        for way in (1, -1):
            blocks_by[way * step] = lax.ppermute(
                blocks_by[way * (step - 1)], "seq", step_pairs(devices, step, way)
            )

    def arrival(number):
        wanted = [hops[s][number] for s in range(devices)]
        names = sorted(set(wanted))
        return [names.index(name) for name in wanted], [blocks_by[name] for name in names]

    part = w_out.shape[1] // groups
    share = lax.dynamic_slice_in_dim(w_out, group * part, part, axis=1)
    narrow = part % HD != 0
    columns = {(0, 0): lax.all_gather(share, "seq", axis=0, tiled=True)}

    blocks = {0: w_qkv}
    if not ragged:
        blocks[near] = swap(w_qkv, "tile", near)
        for bit in far:
            blocks.update(
                {d ^ bit: swap(blocks[d], "tile", bit) for d in list(blocks) if d != near}
            )
    hop(1)

    table = [
        [([s] + [s - hop for hop in hops[s]]).index((s + turn) % devices) for turn in range(devices)]
        for s in range(devices)
    ]
    slots = jnp.asarray(table, jnp.int32)[place]
    order = [(d, g) for d in range(tiles) for g in range(groups)]
    starts = jnp.stack(
        [
            (tile ^ d) * (part * groups) + lax.rem(group - g + groups, groups) * part
            for d, g in order
        ]
    ).astype(jnp.int32)
    if narrow:
        order, starts = [(0, 0)], jnp.zeros((1,), jnp.int32)
    features = w_out.shape[0]
    firsts = jnp.stack(
        [lax.rem(place - turn + devices, devices) * features for turn in range(devices)]
    ).astype(jnp.int32)
    index = step_index[0].astype(jnp.float32)
    now = noise_level(index, NSTEPS)
    coef = jnp.stack([now, noise_level(index + 1.0, NSTEPS) - now])
    blocks, columns, blocks_by, slots, starts, firsts, coef, norms = lax.optimization_barrier(
        (blocks, columns, blocks_by, slots, starts, firsts, coef, norms)
    )
    if ragged:
        blocks[0] = lax.all_gather(blocks[0], "tile", axis=0, tiled=True)
    else:
        blocks.update(
            {d ^ near: swap(blocks[d], "tile", near) for d in list(blocks) if d not in (0, near)}
        )
    blocks = [blocks[d] for d in range(len(blocks))]
    if narrow:
        columns[0, 0] = lax.all_gather(columns[0, 0].T, ("tile", "group"), axis=0, tiled=True).T
    else:
        for bit in far:
            columns.update({(d ^ bit, 0): swap(columns[d, 0], "tile", bit) for d, _ in list(columns)})
        for turn in range(1, groups):
            columns[0, turn] = turned(columns[0, 0], "group", turn)

    at = place.reshape(1)
    known, plan, sources = [], [[0] * devices], [normed]
    for number in range(devices - 2):
        if number + 2 < devices:
            hop(number + 2)
        choices, found = arrival(number)
        plan, sources = plan + [choices], sources + found
        known.append(project(at, plan, sources, blocks))
        plan, sources = [], []
        if number + 3 < devices:
            blocks_by, known = lax.optimization_barrier((blocks_by, known))
    if not narrow:
        mine = lax.optimization_barrier((columns[0, 0], known[0]))[0]
        columns[near, 0] = swap(mine, "tile", near)
    columns = {key: [value] for key, value in columns.items()}
    diagonal = groups == 2 and len(far) == 1 and not narrow
    crossing = ()
    if diagonal:
        bit, half = far[0], columns[0, 0][0].shape[0] // 2
        crossing = (columns[bit, 0][0][:half], columns[0, 1][0][half:])
    known, crossing = lax.optimization_barrier((known, crossing))
    late = {}
    if diagonal:
        late[bit, 1] = [turned(crossing[0], "group", 1), swap(crossing[1], "tile", bit)]
    before = early(known, rows)
    blocks_by, known, before, columns = lax.optimization_barrier(
        (blocks_by, known, before, columns)
    )
    if not narrow and not diagonal:
        for turn in range(1, groups):
            for d in range(1, tiles):
                if d & near == 0:
                    late[d, turn] = [turned(columns[d, 0][0], "group", turn)]
    if not narrow:
        columns.update(
            {
                (d ^ near, g): [swap(array, "tile", near) for array in columns[d, g]]
                for d, g in list(columns)
                if (d ^ near, g) not in columns
            }
        )
    heads = w_qkv.shape[1] // (3 * HD)
    many = heads - heads // 2
    halves = [(0, many), (many, heads - many)]
    turns = sorted(range(1, devices), key=lambda turn: -min(turn, devices - turn))
    choices, found = arrival(devices - 2)
    attended = attend(at, slots, [choices], found, known, before, blocks, *halves[0])
    attended, columns, found = lax.optimization_barrier((attended, columns, found))
    received = [[turned(attended[turn], "seq", turn) for turn in turns]]
    own = [attended[0]]
    attended = attend(at, slots, [choices], found, known, before, blocks, *halves[1])
    attended, received, late = lax.optimization_barrier((attended, received, late))
    columns.update(late)
    columns.update(
        {(d ^ near, g): [swap(array, "tile", near) for array in late[d, g]] for d, g in late}
    )
    received.append([turned(attended[turn], "seq", turn) for turn in turns])
    own.append(attended[0])
    pieces = [columns[key] for key in order]
    offsets = [[(turn, start * HD) for turn in turns] for start, _ in halves]
    mixed = accumulate(
        own + received[0],
        [(0, start * HD) for start, _ in halves] + offsets[0],
        starts,
        firsts,
        pieces,
        local,
        modulation,
    )
    weighted, to_join = accumulate(
        received[1],
        offsets[1],
        starts,
        firsts,
        pieces,
        mixed,
        modulation,
        (coef, w_head.T, latent[0].T, weight),
    )
    other = lax.ppermute(to_join, ("tile", "seq"), joins).astype(jnp.float32)
    joined = (weighted + other) / norms
    channels = w_head.shape[1]
    return (joined[:channels].T[None], joined[channels:].T[None])


def solution(mesh):
    in_specs = (
        P(("group", "tile"), "seq", None),
        P("group", None),
        P("tile", "seq"),
        P("seq", "tile"),
        P(),
        P(("group", "tile"), "seq", None),
        P(("group", "tile"), "seq"),
        P("group"),
    )
    out_specs = (P(("group", "tile"), "seq", None), P(("group", "tile"), "seq", None))
    return jax.shard_map(shards, mesh=mesh, in_specs=in_specs, out_specs=out_specs, check_vma=False)
```

```python
import functools
import math

import jax
import jax.numpy as jnp
from jax import lax
from jax.experimental import pallas as pl
from jax.experimental.pallas import tpu as pltpu
from jax.sharding import PartitionSpec as P

HD = 128
NSTEPS = 28
MIB = 1 << 20


def swap(value, axis, bit):
    count = lax.axis_size(axis)
    return lax.ppermute(value, axis, [(i, i ^ bit) for i in range(count)])


def bits_of(count):
    far = [1 << n for n in range(1, count.bit_length() - 1)]
    return far + [1]


def noise_level(index, steps):
    level = 1.0 - index / steps
    return 3.0 * level / (1.0 + 2.0 * level)


def turned(value, axis, turn):
    count = lax.axis_size(axis)
    return lax.ppermute(value, axis, [(i, (i + turn) % count) for i in range(count)])


def step_pairs(count, step, way):
    if way > 0:
        return [(s, s + 1) for s in range(step - 1, count - 1)]
    return [(s, s - 1) for s in range(1, count - step + 1)]


def arrivals(count):
    return [
        sorted((s - home for home in range(count) if home != s), key=lambda hop: (abs(hop), -hop))
        for s in range(count)
    ]


def layer_norm(values):
    mean = jnp.mean(values, axis=-1, keepdims=True)
    centred = values - mean
    spread = jnp.mean(centred * centred, axis=-1, keepdims=True)
    return centred * lax.rsqrt(spread + 1e-06)


def root_norm(values):
    spread = jnp.mean(values * values, axis=-1, keepdims=True)
    return (values * lax.rsqrt(spread + 1e-06)).astype(jnp.bfloat16)


def norm_kernel(blocks, starts_ref, hidden_ref, mod_ref, out_ref):
    local = hidden_ref[...].astype(jnp.float32)
    mean = jnp.mean(local, axis=-1, keepdims=True)
    centred = local - mean
    spread = jnp.mean(centred * centred, axis=-1, keepdims=True)
    scaling = lax.rsqrt(spread + 1e-06)
    width = hidden_ref.shape[1] // blocks
    for n in range(blocks):
        taken = pl.ds(pl.multiple_of(starts_ref[n], HD), width)
        values = (hidden_ref[:, taken].astype(jnp.float32) - mean) * scaling
        values = values * (1.0 + mod_ref[1:2, taken]) + mod_ref[0:1, taken]
        out_ref[:, n * width : (n + 1) * width] = values.astype(jnp.bfloat16)


def norm_rows(hidden, modulation, starts, first, rows):
    width = hidden.shape[1]
    block = math.gcd(math.gcd(first, rows), 64)
    return pl.pallas_call(
        functools.partial(norm_kernel, starts.shape[0]),
        grid=(rows // block,),
        in_specs=[
            pl.BlockSpec(memory_space=pltpu.SMEM),
            pl.BlockSpec((block, width), lambda i: (first // block + i, 0)),
            pl.BlockSpec(modulation.shape, lambda i: (0, 0)),
        ],
        out_specs=pl.BlockSpec((block, width), lambda i: (i, 0)),
        out_shape=jax.ShapeDtypeStruct((rows, width), jnp.bfloat16),
        name="norm_in",
    )(starts, hidden, modulation)


def product(x_ref, blocks):
    height = x_ref.shape[1] // len(blocks)
    total = 0.0
    for n, block in enumerate(blocks):
        total += jnp.dot(
            x_ref[:, n * height : (n + 1) * height],
            block[...],
            preferred_element_type=jnp.float32,
        )
    return total


def load(place, choices, refs, to, sem):
    for n, ref in enumerate(refs):
        wanted = functools.reduce(
            jnp.logical_or, [place == s for s in range(len(choices)) if choices[s] == n]
        )

        @pl.when(wanted)
        def _():
            pltpu.make_async_copy(ref, to, sem).start()

    return pltpu.make_async_copy(refs[0], to, sem)


def load_all(place, plan, refs, tokens, sems):
    rows = tokens.shape[0] // len(plan)
    copies, used = [], 0
    for n, choices in enumerate(plan):
        many = max(choices) + 1
        to = tokens.at[pl.ds(n * rows, rows)]
        copies.append(load(place, choices, refs[used : used + many], to, sems.at[n]))
        used += many
    for copy in copies:
        copy.wait()


def project_kernel(plan, blocks, place_ref, *refs):
    w_refs = refs[:blocks]
    sources, (q_ref, k_ref, v_ref, tokens, sems) = refs[blocks:-5], refs[-5:]

    @pl.when(pl.program_id(0) == 0)
    def _():
        load_all(place_ref[0], plan, sources, tokens, sems)

    proj = product(tokens, w_refs)
    for h in range(q_ref.shape[0]):
        query, key, value = (proj[:, (3 * h + i) * HD : (3 * h + i + 1) * HD] for i in range(3))
        q_ref[h] = root_norm(query)
        k_ref[h] = root_norm(key)
        v_ref[h] = value.astype(jnp.bfloat16)


def project(place, plan, sources, blocks):
    rows, width = sources[0].shape
    length = rows * len(plan)
    total = blocks[0].shape[1]
    heads = total // (3 * HD)
    many = 2 if heads % 2 == 0 else 1
    out = jax.ShapeDtypeStruct((heads, length, HD), jnp.bfloat16)
    return pl.pallas_call(
        functools.partial(project_kernel, plan, len(blocks)),
        grid=(heads // many,),
        in_specs=[pl.BlockSpec(memory_space=pltpu.SMEM)]
        + [pl.BlockSpec((width // len(blocks), many * 3 * HD), lambda h: (0, h))] * len(blocks)
        + [pl.BlockSpec(memory_space=pl.ANY)] * len(sources),
        out_specs=[pl.BlockSpec((many, length, HD), lambda h: (h, 0, 0))] * 3,
        out_shape=[out] * 3,
        scratch_shapes=[
            pltpu.VMEM((length, width), jnp.bfloat16),
            pltpu.SemaphoreType.DMA((len(plan),)),
        ],
        compiler_params=pltpu.CompilerParams(vmem_limit_bytes=42 * MIB),
        name="project",
    )(place, *blocks, *sources)


def weigh(query, key, values):
    scores = lax.dot_general(
        query, key, (((1,), (1,)), ((), ())), preferred_element_type=jnp.float32
    )
    expo = jnp.exp(scores * (1.0 / math.sqrt(HD))).astype(jnp.bfloat16)
    return jnp.dot(expo, values, preferred_element_type=jnp.float32)


def gather_known(known, counts, queries, keys, values):
    at = 0
    for n, count in enumerate(counts):
        queries[at : at + count] = known[3 * n][0]
        keys[at : at + count] = known[3 * n + 1][0]
        values[at : at + count, :HD] = known[3 * n + 2][0]
        at += count


def early_kernel(counts, rows, *refs):
    known, (out_ref, queries, keys, values) = refs[:-4], refs[-4:]

    @pl.when(pl.program_id(0) == 0)
    def _():
        values[:, HD:] = jnp.ones((sum(counts), HD), jnp.bfloat16)

    gather_known(known, counts, queries, keys, values)
    for first in range(0, sum(counts), rows):
        part = slice(first, first + rows)
        out_ref[0, part] = weigh(queries[part], keys[...], values[...])


def early(known, rows):
    counts = [three[0].shape[1] for three in known]
    heads, length = known[0][0].shape[0], sum(counts)
    return pl.pallas_call(
        functools.partial(early_kernel, counts, rows),
        grid=(heads,),
        in_specs=[
            pl.BlockSpec((1, count, HD), lambda h: (h, 0, 0)) for count in counts for _ in range(3)
        ],
        out_specs=pl.BlockSpec((1, length, 2 * HD), lambda h: (h, 0, 0)),
        out_shape=jax.ShapeDtypeStruct((heads, length, 2 * HD), jnp.float32),
        scratch_shapes=[
            pltpu.VMEM((length, HD), jnp.bfloat16),
            pltpu.VMEM((length, HD), jnp.bfloat16),
            pltpu.VMEM((length, 2 * HD), jnp.bfloat16),
        ],
        compiler_params=pltpu.CompilerParams(vmem_limit_bytes=42 * MIB),
        name="early",
    )(*(value for three in known for value in three))


def attend_kernel(plan, blocks, counts, head, heads, place_ref, slots_ref, *refs):
    w_refs, before_ref, refs = refs[:blocks], refs[blocks], refs[blocks + 1 :]
    known, refs = refs[: 3 * len(counts)], refs[3 * len(counts) :]
    queries, keys, values, done, tokens, sems = refs[-6:]
    devices = slots_ref.shape[0]
    sources, outs = refs[: -6 - devices], refs[-6 - devices : -6]
    start, rows = sum(counts), tokens.shape[0]
    values[:, HD:] = jnp.ones((start + rows, HD), jnp.bfloat16)
    load_all(place_ref[0], plan, sources, tokens, sems)
    for h in range(heads):
        cols = slice((head + h) * 3 * HD, (head + h + 1) * 3 * HD)
        proj = product(tokens, [w_ref.at[:, cols] for w_ref in w_refs])
        at = 0
        for n, count in enumerate(counts):
            queries[at : at + count] = known[3 * n][head + h]
            keys[at : at + count] = known[3 * n + 1][head + h]
            values[at : at + count, :HD] = known[3 * n + 2][head + h]
            at += count
        queries[start:] = root_norm(proj[:, :HD])
        keys[start:] = root_norm(proj[:, HD : 2 * HD])
        values[start:, :HD] = proj[:, 2 * HD :].astype(jnp.bfloat16)
        mixed = before_ref[head + h] + weigh(queries[:start], keys[start:], values[start:])
        done[:start] = (mixed[:, :HD] / mixed[:, HD:]).astype(jnp.bfloat16)
        mixed = weigh(queries[start:], keys[...], values[...])
        done[start:] = (mixed[:, :HD] / mixed[:, HD:]).astype(jnp.bfloat16)
        for turn in range(devices):
            part = pl.ds(pl.multiple_of(slots_ref[turn] * rows, rows), rows)
            outs[turn][:, h * HD : (h + 1) * HD] = done[part]


def attend(place, slots, plan, sources, known, before, blocks, start, heads):
    devices = slots.shape[0]
    rows, width = sources[0].shape
    counts = [three[0].shape[1] for three in known]
    length = rows + sum(counts)
    smem = pl.BlockSpec(memory_space=pltpu.SMEM)
    vmem = pl.BlockSpec(memory_space=pltpu.VMEM)
    out = jax.ShapeDtypeStruct((rows, heads * HD), jnp.bfloat16)
    return pl.pallas_call(
        functools.partial(attend_kernel, plan, len(blocks), counts, start, heads),
        in_specs=[smem, smem]
        + [vmem] * (len(blocks) + 1 + 3 * len(counts))
        + [pl.BlockSpec(memory_space=pl.ANY)] * len(sources),
        out_specs=[vmem] * devices,
        out_shape=[out] * devices,
        scratch_shapes=[
            pltpu.VMEM((length, HD), jnp.bfloat16),
            pltpu.VMEM((length, HD), jnp.bfloat16),
            pltpu.VMEM((length, 2 * HD), jnp.bfloat16),
            pltpu.VMEM((length, HD), jnp.bfloat16),
            pltpu.VMEM((rows, width), jnp.bfloat16),
            pltpu.SemaphoreType.DMA((1,)),
        ],
        compiler_params=pltpu.CompilerParams(vmem_limit_bytes=36 * MIB),
        name="attend",
    )(place, slots, *blocks, before, *(value for three in known for value in three), *sources)


def multiply(parts, offsets, starts_ref, rows_ref, sources, weights, sems, wide, store):
    depth = [part.shape[1] for part in parts]
    width = weights.shape[2]
    copies = []
    for p, split in enumerate(sources):
        copies.append([])
        for n, (turn, offset) in enumerate(offsets):
            to = weights.at[p, pl.ds(sum(depth[:n]), depth[n])]
            row = rows_ref[turn] + offset
            size = split[0].shape[0]
            for i, source in enumerate(split):
                if len(split) == 1:
                    rows = source.at[pl.ds(pl.multiple_of(row, HD), depth[n])]
                    pltpu.make_async_copy(rows, to, sems.at[p, n]).start()
                    continue

                @pl.when(jnp.logical_and(row >= i * size, row < (i + 1) * size))
                def _():
                    rows = source.at[pl.ds(pl.multiple_of(row - i * size, HD), depth[n])]
                    pltpu.make_async_copy(rows, to, sems.at[p, n]).start()

            rows = split[0].at[pl.ds(0, depth[n])]
            copies[p].append(pltpu.make_async_copy(rows, to, sems.at[p, n]))
    for n, part in enumerate(parts):
        wide[:, sum(depth[:n]) : sum(depth[: n + 1])] = part[...]
    for p in range(len(sources)):
        for copy in copies[p]:
            copy.wait()
        cols = pl.ds(pl.multiple_of(starts_ref[p], HD), width)
        store(p, cols, jnp.dot(wide[...], weights[p], preferred_element_type=jnp.float32))


def split_refs(refs, splits):
    grouped = []
    for split in splits:
        grouped.append(refs[:split])
        refs = refs[split:]
    return grouped, refs


def add_kernel(offsets, splits, starts_ref, rows_ref, *refs):
    parts = refs[: len(offsets)]
    sources, refs = split_refs(refs[len(offsets) :], splits)
    before_ref, mod_ref, out_ref, weights, wide, sems = refs

    def store(p, cols, summed):
        out_ref[:, cols] = before_ref[:, cols].astype(jnp.float32) + mod_ref[2:3, cols] * summed

    multiply(parts, offsets, starts_ref, rows_ref, sources, weights, sems, wide, store)


def finish_kernel(offsets, splits, starts_ref, rows_ref, coef_ref, *refs):
    parts = refs[: len(offsets)]
    sources, refs = split_refs(refs[len(offsets) :], splits)
    before_ref, mod_ref, head_ref, latent_ref, weight_ref, out_ref, sent_ref = refs[:7]
    weights, wide, sems, mixed = refs[7:]
    count = len(splits)
    width = weights.shape[2]
    held = {}

    def store(p, cols, summed):
        values = before_ref[:, cols] + mod_ref[2:3, cols] * summed
        mixed[:, cols] = values
        if p == 0:
            held["base"] = jnp.mean(values, axis=-1, keepdims=True)
        away = values - held["base"]
        sums = (
            jnp.sum(away, axis=-1, keepdims=True),
            jnp.sum(away * away, axis=-1, keepdims=True),
        )
        held["sums"] = [a + b for a, b in zip(held.get("sums", (0.0, 0.0)), sums)]

    multiply(parts, offsets, starts_ref, rows_ref, sources, weights, sems, wide, store)
    total = width * count
    shift = held["sums"][0] / total
    scaling = lax.rsqrt(held["sums"][1] / total - shift * shift + 1e-06)
    mean = held["base"] + shift
    velocity = 0.0
    for p in range(count):
        cols = slice(p * width, (p + 1) * width)
        normed = (mixed[:, cols] - mean) * scaling
        normed = normed * (1.0 + mod_ref[4:5, cols]) + mod_ref[3:4, cols]
        velocity += lax.dot_general(
            normed.astype(jnp.bfloat16),
            head_ref[:, cols],
            (((1,), (1,)), ((), ())),
            preferred_element_type=jnp.float32,
        )
    velocity = velocity.T
    channels = velocity.shape[0]
    base, weight = latent_ref[...], weight_ref[...]
    moved = (base + coef_ref[1] * velocity) * weight
    guess = (base - coef_ref[0] * velocity) * weight
    out_ref[:channels, :] = moved
    out_ref[channels:, :] = guess
    sent_ref[:channels, :] = moved.astype(jnp.bfloat16)
    sent_ref[channels:, :] = guess.astype(jnp.bfloat16)


def accumulate(parts, offsets, starts, firsts, pieces, before, modulation, last=None):
    rows, width = before.shape
    depth = sum(part.shape[1] for part in parts)
    count = len(pieces)
    splits = [len(piece) for piece in pieces]
    pieces = [array for piece in pieces for array in piece]
    smem = pl.BlockSpec(memory_space=pltpu.SMEM)
    vmem = pl.BlockSpec(memory_space=pltpu.VMEM)
    hbm = pl.BlockSpec(memory_space=pl.ANY)
    scratch = [
        pltpu.VMEM((count, depth, pieces[0].shape[1]), jnp.bfloat16),
        pltpu.VMEM((rows, depth), jnp.bfloat16),
        pltpu.SemaphoreType.DMA((count, len(parts))),
    ]
    params = dict(
        compiler_params=pltpu.CompilerParams(vmem_limit_bytes=52 * MIB),
    )
    if last is None:
        aliased = before.dtype == jnp.float32
        return pl.pallas_call(
            functools.partial(add_kernel, offsets, splits),
            in_specs=[smem] * 2 + [vmem] * len(parts) + [hbm] * len(pieces) + [vmem] * 2,
            out_specs=vmem,
            out_shape=jax.ShapeDtypeStruct((rows, width), jnp.float32),
            scratch_shapes=scratch,
            input_output_aliases={2 + len(parts) + len(pieces): 0} if aliased else {},
            name="add_parts",
            **params,
        )(starts, firsts, *parts, *pieces, before, modulation)
    coef, head, latent, weight = last
    channels = head.shape[0]
    return pl.pallas_call(
        functools.partial(finish_kernel, offsets, splits),
        in_specs=[smem] * 3 + [vmem] * len(parts) + [hbm] * len(pieces) + [vmem] * 5,
        out_specs=[vmem, vmem],
        out_shape=[
            jax.ShapeDtypeStruct((2 * channels, rows), jnp.float32),
            jax.ShapeDtypeStruct((2 * channels, rows), jnp.bfloat16),
        ],
        scratch_shapes=scratch
        + [pltpu.VMEM((rows, width), jnp.float32)],
        name="finish",
        **params,
    )(starts, firsts, coef, *parts, *pieces, before, modulation, head, latent, weight)


def shards(hidden, modulation, w_qkv, w_out, w_head, latent, weights_int, step_index):
    local = hidden[0]
    rows = local.shape[0]
    devices = lax.axis_size("seq")
    tiles = lax.axis_size("tile")
    groups = lax.axis_size("group")
    place, tile, group = lax.axis_index("seq"), lax.axis_index("tile"), lax.axis_index("group")
    far, near = bits_of(tiles)[:-1], bits_of(tiles)[-1]

    weight = weights_int.astype(jnp.float32)
    joins = [
        (t * devices + s, (t + 1) * devices + s - (devices - 2))
        for t in range(tiles - 1)
        for s in range(devices - 2, devices)
    ]
    joins += [
        (t * devices + s, (t - 1) * devices + s + (devices - 2))
        for t in range(1, tiles)
        for s in range(2)
    ]
    norms = weight + lax.ppermute(
        weight.astype(jnp.bfloat16), ("tile", "seq"), joins
    ).astype(jnp.float32)

    height = w_qkv.shape[0]
    ragged = height % HD != 0
    row_starts = jnp.stack([(tile ^ d) * height for d in range(tiles)]).astype(jnp.int32)
    if ragged:
        row_starts = jnp.zeros((1,), jnp.int32)
    normed = norm_rows(local, modulation, row_starts, 0, rows)
    hops = arrivals(devices)
    blocks_by = {0: normed}

    def hop(step):
        for way in (1, -1):
            blocks_by[way * step] = lax.ppermute(
                blocks_by[way * (step - 1)], "seq", step_pairs(devices, step, way)
            )

    def arrival(number):
        wanted = [hops[s][number] for s in range(devices)]
        names = sorted(set(wanted))
        return [names.index(name) for name in wanted], [blocks_by[name] for name in names]

    part = w_out.shape[1] // groups
    share = lax.dynamic_slice_in_dim(w_out, group * part, part, axis=1)
    narrow = part % HD != 0
    columns = {(0, 0): lax.all_gather(share, "seq", axis=0, tiled=True)}

    blocks = {0: w_qkv}
    if not ragged:
        blocks[near] = swap(w_qkv, "tile", near)
        for bit in far:
            blocks.update(
                {d ^ bit: swap(blocks[d], "tile", bit) for d in list(blocks) if d != near}
            )
    hop(1)

    table = [
        [([s] + [s - hop for hop in hops[s]]).index((s + turn) % devices) for turn in range(devices)]
        for s in range(devices)
    ]
    slots = jnp.asarray(table, jnp.int32)[place]
    order = [(d, g) for d in range(tiles) for g in range(groups)]
    starts = jnp.stack(
        [
            (tile ^ d) * (part * groups) + lax.rem(group - g + groups, groups) * part
            for d, g in order
        ]
    ).astype(jnp.int32)
    if narrow:
        order, starts = [(0, 0)], jnp.zeros((1,), jnp.int32)
    features = w_out.shape[0]
    firsts = jnp.stack(
        [lax.rem(place - turn + devices, devices) * features for turn in range(devices)]
    ).astype(jnp.int32)
    index = step_index[0].astype(jnp.float32)
    now = noise_level(index, NSTEPS)
    coef = jnp.stack([now, noise_level(index + 1.0, NSTEPS) - now])
    blocks, columns, blocks_by, slots, starts, firsts, coef, norms = lax.optimization_barrier(
        (blocks, columns, blocks_by, slots, starts, firsts, coef, norms)
    )
    if ragged:
        blocks[0] = lax.all_gather(blocks[0], "tile", axis=0, tiled=True)
    else:
        blocks.update(
            {d ^ near: swap(blocks[d], "tile", near) for d in list(blocks) if d not in (0, near)}
        )
    blocks = [blocks[d] for d in range(len(blocks))]
    if narrow:
        columns[0, 0] = lax.all_gather(columns[0, 0].T, ("tile", "group"), axis=0, tiled=True).T
    else:
        for bit in far:
            columns.update({(d ^ bit, 0): swap(columns[d, 0], "tile", bit) for d, _ in list(columns)})
        for turn in range(1, groups):
            columns[0, turn] = turned(columns[0, 0], "group", turn)

    at = place.reshape(1)
    known, plan, sources = [], [[0] * devices], [normed]
    for number in range(devices - 2):
        if number + 2 < devices:
            hop(number + 2)
        choices, found = arrival(number)
        plan, sources = plan + [choices], sources + found
        known.append(project(at, plan, sources, blocks))
        plan, sources = [], []
        if number + 3 < devices:
            blocks_by, known = lax.optimization_barrier((blocks_by, known))
    if not narrow:
        mine = lax.optimization_barrier((columns[0, 0], known[0]))[0]
        columns[near, 0] = swap(mine, "tile", near)
    columns = {key: [value] for key, value in columns.items()}
    diagonal = groups == 2 and len(far) == 1 and not narrow
    crossing = ()
    if diagonal:
        bit, half = far[0], columns[0, 0][0].shape[0] // 2
        crossing = (columns[bit, 0][0][:half], columns[0, 1][0][half:])
    known, crossing = lax.optimization_barrier((known, crossing))
    late = {}
    if diagonal:
        late[bit, 1] = [turned(crossing[0], "group", 1), swap(crossing[1], "tile", bit)]
    before = early(known, rows)
    blocks_by, known, before, columns = lax.optimization_barrier(
        (blocks_by, known, before, columns)
    )
    if not narrow and not diagonal:
        for turn in range(1, groups):
            for d in range(1, tiles):
                if d & near == 0:
                    late[d, turn] = [turned(columns[d, 0][0], "group", turn)]
    if not narrow:
        columns.update(
            {
                (d ^ near, g): [swap(array, "tile", near) for array in columns[d, g]]
                for d, g in list(columns)
                if (d ^ near, g) not in columns
            }
        )
    heads = w_qkv.shape[1] // (3 * HD)
    many = heads - heads // 2
    halves = [(0, many), (many, heads - many)]
    turns = sorted(range(1, devices), key=lambda turn: -min(turn, devices - turn))
    choices, found = arrival(devices - 2)
    attended = attend(at, slots, [choices], found, known, before, blocks, *halves[0])
    attended, columns, found = lax.optimization_barrier((attended, columns, found))
    received = [[turned(attended[turn], "seq", turn) for turn in turns]]
    own = [attended[0]]
    attended = attend(at, slots, [choices], found, known, before, blocks, *halves[1])
    attended, received, late = lax.optimization_barrier((attended, received, late))
    columns.update(late)
    columns.update(
        {(d ^ near, g): [swap(array, "tile", near) for array in late[d, g]] for d, g in late}
    )
    received.append([turned(attended[turn], "seq", turn) for turn in turns])
    own.append(attended[0])
    pieces = [columns[key] for key in order]
    offsets = [[(turn, start * HD) for turn in turns] for start, _ in halves]
    mixed = accumulate(
        own + received[0],
        [(0, start * HD) for start, _ in halves] + offsets[0],
        starts,
        firsts,
        pieces,
        local,
        modulation,
    )
    weighted, to_join = accumulate(
        received[1],
        offsets[1],
        starts,
        firsts,
        pieces,
        mixed,
        modulation,
        (coef, w_head.T, latent[0].T, weight),
    )
    other = lax.ppermute(to_join, ("tile", "seq"), joins).astype(jnp.float32)
    joined = (weighted + other) / norms
    channels = w_head.shape[1]
    return (joined[:channels].T[None], joined[channels:].T[None])


def solution(mesh):
    in_specs = (
        P(("group", "tile"), "seq", None),
        P("group", None),
        P("tile", "seq"),
        P("seq", "tile"),
        P(),
        P(("group", "tile"), "seq", None),
        P(("group", "tile"), "seq"),
        P("group"),
    )
    out_specs = (P(("group", "tile"), "seq", None), P(("group", "tile"), "seq", None))
    return jax.shard_map(shards, mesh=mesh, in_specs=in_specs, out_specs=out_specs, check_vma=False)
```

```python
import functools
import math

import jax
import jax.numpy as jnp
from jax import lax
from jax.experimental import pallas as pl
from jax.experimental.pallas import tpu as pltpu
from jax.sharding import PartitionSpec as P

HD = 128
NSTEPS = 28
MIB = 1 << 20


def swap(value, axis, bit):
    count = lax.axis_size(axis)
    return lax.ppermute(value, axis, [(i, i ^ bit) for i in range(count)])


def bits_of(count):
    far = [1 << n for n in range(1, count.bit_length() - 1)]
    return far + [1]


def noise_level(index, steps):
    level = 1.0 - index / steps
    return 3.0 * level / (1.0 + 2.0 * level)


def turned(value, axis, turn):
    count = lax.axis_size(axis)
    return lax.ppermute(value, axis, [(i, (i + turn) % count) for i in range(count)])


def step_pairs(count, step, way):
    if way > 0:
        return [(s, s + 1) for s in range(step - 1, count - 1)]
    return [(s, s - 1) for s in range(1, count - step + 1)]


def arrivals(count):
    return [
        sorted((s - home for home in range(count) if home != s), key=lambda hop: (abs(hop), -hop))
        for s in range(count)
    ]


def layer_norm(values):
    mean = jnp.mean(values, axis=-1, keepdims=True)
    centred = values - mean
    spread = jnp.mean(centred * centred, axis=-1, keepdims=True)
    return centred * lax.rsqrt(spread + 1e-06)


def root_norm(values):
    spread = jnp.mean(values * values, axis=-1, keepdims=True)
    return (values * lax.rsqrt(spread + 1e-06)).astype(jnp.bfloat16)


def norm_kernel(blocks, starts_ref, hidden_ref, mod_ref, out_ref):
    local = hidden_ref[...].astype(jnp.float32)
    mean = jnp.mean(local, axis=-1, keepdims=True)
    centred = local - mean
    spread = jnp.mean(centred * centred, axis=-1, keepdims=True)
    scaling = lax.rsqrt(spread + 1e-06)
    width = hidden_ref.shape[1] // blocks
    for n in range(blocks):
        taken = pl.ds(pl.multiple_of(starts_ref[n], HD), width)
        values = (hidden_ref[:, taken].astype(jnp.float32) - mean) * scaling
        values = values * (1.0 + mod_ref[1:2, taken]) + mod_ref[0:1, taken]
        out_ref[:, n * width : (n + 1) * width] = values.astype(jnp.bfloat16)


def norm_rows(hidden, modulation, starts, first, rows):
    width = hidden.shape[1]
    block = math.gcd(math.gcd(first, rows), 64)
    return pl.pallas_call(
        functools.partial(norm_kernel, starts.shape[0]),
        grid=(rows // block,),
        in_specs=[
            pl.BlockSpec(memory_space=pltpu.SMEM),
            pl.BlockSpec((block, width), lambda i: (first // block + i, 0)),
            pl.BlockSpec(modulation.shape, lambda i: (0, 0)),
        ],
        out_specs=pl.BlockSpec((block, width), lambda i: (i, 0)),
        out_shape=jax.ShapeDtypeStruct((rows, width), jnp.bfloat16),
        name="norm_in",
    )(starts, hidden, modulation)


def product(x_ref, blocks):
    height = x_ref.shape[1] // len(blocks)
    total = 0.0
    for n, block in enumerate(blocks):
        total += jnp.dot(
            x_ref[:, n * height : (n + 1) * height],
            block[...],
            preferred_element_type=jnp.float32,
        )
    return total


def load(place, choices, refs, to, sem):
    for n, ref in enumerate(refs):
        wanted = functools.reduce(
            jnp.logical_or, [place == s for s in range(len(choices)) if choices[s] == n]
        )

        @pl.when(wanted)
        def _():
            pltpu.make_async_copy(ref, to, sem).start()

    return pltpu.make_async_copy(refs[0], to, sem)


def load_all(place, plan, refs, tokens, sems):
    rows = tokens.shape[0] // len(plan)
    copies, used = [], 0
    for n, choices in enumerate(plan):
        many = max(choices) + 1
        to = tokens.at[pl.ds(n * rows, rows)]
        copies.append(load(place, choices, refs[used : used + many], to, sems.at[n]))
        used += many
    for copy in copies:
        copy.wait()


def project_kernel(plan, blocks, place_ref, *refs):
    w_refs = refs[:blocks]
    sources, (q_ref, k_ref, v_ref, tokens, sems) = refs[blocks:-5], refs[-5:]

    @pl.when(pl.program_id(0) == 0)
    def _():
        load_all(place_ref[0], plan, sources, tokens, sems)

    proj = product(tokens, w_refs)
    for h in range(q_ref.shape[0]):
        query, key, value = (proj[:, (3 * h + i) * HD : (3 * h + i + 1) * HD] for i in range(3))
        q_ref[h] = root_norm(query)
        k_ref[h] = root_norm(key)
        v_ref[h] = value.astype(jnp.bfloat16)


def project(place, plan, sources, blocks):
    rows, width = sources[0].shape
    length = rows * len(plan)
    total = blocks[0].shape[1]
    heads = total // (3 * HD)
    many = 2 if heads % 2 == 0 else 1
    out = jax.ShapeDtypeStruct((heads, length, HD), jnp.bfloat16)
    return pl.pallas_call(
        functools.partial(project_kernel, plan, len(blocks)),
        grid=(heads // many,),
        in_specs=[pl.BlockSpec(memory_space=pltpu.SMEM)]
        + [pl.BlockSpec((width // len(blocks), many * 3 * HD), lambda h: (0, h))] * len(blocks)
        + [pl.BlockSpec(memory_space=pl.ANY)] * len(sources),
        out_specs=[pl.BlockSpec((many, length, HD), lambda h: (h, 0, 0))] * 3,
        out_shape=[out] * 3,
        scratch_shapes=[
            pltpu.VMEM((length, width), jnp.bfloat16),
            pltpu.SemaphoreType.DMA((len(plan),)),
        ],
        compiler_params=pltpu.CompilerParams(vmem_limit_bytes=42 * MIB),
        name="project",
    )(place, *blocks, *sources)


def weigh(query, key, values):
    scores = lax.dot_general(
        query, key, (((1,), (1,)), ((), ())), preferred_element_type=jnp.float32
    )
    expo = jnp.exp(scores * (1.0 / math.sqrt(HD))).astype(jnp.bfloat16)
    return jnp.dot(expo, values, preferred_element_type=jnp.float32)


def gather_known(known, counts, queries, keys, values):
    at = 0
    for n, count in enumerate(counts):
        queries[at : at + count] = known[3 * n][0]
        keys[at : at + count] = known[3 * n + 1][0]
        values[at : at + count, :HD] = known[3 * n + 2][0]
        at += count


def early_kernel(counts, rows, *refs):
    known, (out_ref, queries, keys, values) = refs[:-4], refs[-4:]

    @pl.when(pl.program_id(0) == 0)
    def _():
        values[:, HD:] = jnp.ones((sum(counts), HD), jnp.bfloat16)

    gather_known(known, counts, queries, keys, values)
    for first in range(0, sum(counts), rows):
        part = slice(first, first + rows)
        out_ref[0, part] = weigh(queries[part], keys[...], values[...])


def early(known, rows):
    counts = [three[0].shape[1] for three in known]
    heads, length = known[0][0].shape[0], sum(counts)
    return pl.pallas_call(
        functools.partial(early_kernel, counts, rows),
        grid=(heads,),
        in_specs=[
            pl.BlockSpec((1, count, HD), lambda h: (h, 0, 0)) for count in counts for _ in range(3)
        ],
        out_specs=pl.BlockSpec((1, length, 2 * HD), lambda h: (h, 0, 0)),
        out_shape=jax.ShapeDtypeStruct((heads, length, 2 * HD), jnp.float32),
        scratch_shapes=[
            pltpu.VMEM((length, HD), jnp.bfloat16),
            pltpu.VMEM((length, HD), jnp.bfloat16),
            pltpu.VMEM((length, 2 * HD), jnp.bfloat16),
        ],
        compiler_params=pltpu.CompilerParams(vmem_limit_bytes=42 * MIB),
        name="early",
    )(*(value for three in known for value in three))


def attend_kernel(plan, blocks, counts, place_ref, slots_ref, *refs):
    w_refs, before_ref, refs = refs[:blocks], refs[blocks], refs[blocks + 1 :]
    known, refs = refs[: 3 * len(counts)], refs[3 * len(counts) :]
    queries, keys, values, done, tokens, sems = refs[-6:]
    devices = slots_ref.shape[0]
    sources, outs = refs[: -6 - devices], refs[-6 - devices : -6]
    start, rows = sum(counts), tokens.shape[0]

    @pl.when(pl.program_id(0) == 0)
    def _():
        values[:, HD:] = jnp.ones((start + rows, HD), jnp.bfloat16)
        load_all(place_ref[0], plan, sources, tokens, sems)

    proj = product(tokens, w_refs)
    gather_known(known, counts, queries, keys, values)
    queries[start:] = root_norm(proj[:, :HD])
    keys[start:] = root_norm(proj[:, HD : 2 * HD])
    values[start:, :HD] = proj[:, 2 * HD :].astype(jnp.bfloat16)
    mixed = before_ref[0] + weigh(queries[:start], keys[start:], values[start:])
    done[:start] = (mixed[:, :HD] / mixed[:, HD:]).astype(jnp.bfloat16)
    mixed = weigh(queries[start:], keys[...], values[...])
    done[start:] = (mixed[:, :HD] / mixed[:, HD:]).astype(jnp.bfloat16)
    for turn in range(devices):
        part = pl.ds(pl.multiple_of(slots_ref[turn] * rows, rows), rows)
        outs[turn][...] = done[part]


def attend(place, slots, plan, sources, known, before, blocks, start, heads):
    devices = slots.shape[0]
    rows, width = sources[0].shape
    counts = [three[0].shape[1] for three in known]
    length = rows + sum(counts)
    smem = pl.BlockSpec(memory_space=pltpu.SMEM)
    out = jax.ShapeDtypeStruct((rows, heads * HD), jnp.bfloat16)
    return pl.pallas_call(
        functools.partial(attend_kernel, plan, len(blocks), counts),
        grid=(heads,),
        in_specs=[smem, smem]
        + [pl.BlockSpec((width // len(blocks), 3 * HD), lambda h: (0, start + h))] * len(blocks)
        + [pl.BlockSpec((1, length - rows, 2 * HD), lambda h: (start + h, 0, 0))]
        + [
            pl.BlockSpec((1, count, HD), lambda h: (start + h, 0, 0))
            for count in counts
            for _ in range(3)
        ]
        + [pl.BlockSpec(memory_space=pl.ANY)] * len(sources),
        out_specs=[pl.BlockSpec((rows, HD), lambda h: (0, h))] * devices,
        out_shape=[out] * devices,
        scratch_shapes=[
            pltpu.VMEM((length, HD), jnp.bfloat16),
            pltpu.VMEM((length, HD), jnp.bfloat16),
            pltpu.VMEM((length, 2 * HD), jnp.bfloat16),
            pltpu.VMEM((length, HD), jnp.bfloat16),
            pltpu.VMEM((rows, width), jnp.bfloat16),
            pltpu.SemaphoreType.DMA((1,)),
        ],
        compiler_params=pltpu.CompilerParams(vmem_limit_bytes=42 * MIB),
        name="attend",
    )(place, slots, *blocks, before, *(value for three in known for value in three), *sources)


def multiply(parts, offsets, starts_ref, rows_ref, sources, weights, sems, wide, store):
    depth = [part.shape[1] for part in parts]
    width = weights.shape[2]
    copies = []
    for p, split in enumerate(sources):
        copies.append([])
        for n, (turn, offset) in enumerate(offsets):
            to = weights.at[p, pl.ds(sum(depth[:n]), depth[n])]
            row = rows_ref[turn] + offset
            size = split[0].shape[0]
            for i, source in enumerate(split):
                if len(split) == 1:
                    rows = source.at[pl.ds(pl.multiple_of(row, HD), depth[n])]
                    pltpu.make_async_copy(rows, to, sems.at[p, n]).start()
                    continue

                @pl.when(jnp.logical_and(row >= i * size, row < (i + 1) * size))
                def _():
                    rows = source.at[pl.ds(pl.multiple_of(row - i * size, HD), depth[n])]
                    pltpu.make_async_copy(rows, to, sems.at[p, n]).start()

            rows = split[0].at[pl.ds(0, depth[n])]
            copies[p].append(pltpu.make_async_copy(rows, to, sems.at[p, n]))
    for n, part in enumerate(parts):
        wide[:, sum(depth[:n]) : sum(depth[: n + 1])] = part[...]
    for p in range(len(sources)):
        for copy in copies[p]:
            copy.wait()
        cols = pl.ds(pl.multiple_of(starts_ref[p], HD), width)
        store(p, cols, jnp.dot(wide[...], weights[p], preferred_element_type=jnp.float32))


def split_refs(refs, splits):
    grouped = []
    for split in splits:
        grouped.append(refs[:split])
        refs = refs[split:]
    return grouped, refs


def add_kernel(offsets, splits, starts_ref, rows_ref, *refs):
    parts = refs[: len(offsets)]
    sources, refs = split_refs(refs[len(offsets) :], splits)
    before_ref, mod_ref, out_ref, weights, wide, sems = refs

    def store(p, cols, summed):
        out_ref[:, cols] = before_ref[:, cols].astype(jnp.float32) + mod_ref[2:3, cols] * summed

    multiply(parts, offsets, starts_ref, rows_ref, sources, weights, sems, wide, store)


def finish_kernel(offsets, splits, starts_ref, rows_ref, coef_ref, *refs):
    parts = refs[: len(offsets)]
    sources, refs = split_refs(refs[len(offsets) :], splits)
    before_ref, mod_ref, head_ref, latent_ref, weight_ref, out_ref, sent_ref = refs[:7]
    weights, wide, sems, mixed = refs[7:]
    count = len(splits)
    width = weights.shape[2]
    held = {}

    def store(p, cols, summed):
        values = before_ref[:, cols] + mod_ref[2:3, cols] * summed
        mixed[:, cols] = values
        if p == 0:
            held["base"] = jnp.mean(values, axis=-1, keepdims=True)
        away = values - held["base"]
        sums = (
            jnp.sum(away, axis=-1, keepdims=True),
            jnp.sum(away * away, axis=-1, keepdims=True),
        )
        held["sums"] = [a + b for a, b in zip(held.get("sums", (0.0, 0.0)), sums)]

    multiply(parts, offsets, starts_ref, rows_ref, sources, weights, sems, wide, store)
    total = width * count
    shift = held["sums"][0] / total
    scaling = lax.rsqrt(held["sums"][1] / total - shift * shift + 1e-06)
    mean = held["base"] + shift
    velocity = 0.0
    for p in range(count):
        cols = slice(p * width, (p + 1) * width)
        normed = (mixed[:, cols] - mean) * scaling
        normed = normed * (1.0 + mod_ref[4:5, cols]) + mod_ref[3:4, cols]
        velocity += lax.dot_general(
            normed.astype(jnp.bfloat16),
            head_ref[:, cols],
            (((1,), (1,)), ((), ())),
            preferred_element_type=jnp.float32,
        )
    velocity = velocity.T
    channels = velocity.shape[0]
    base, weight = latent_ref[...], weight_ref[...]
    moved = (base + coef_ref[1] * velocity) * weight
    guess = (base - coef_ref[0] * velocity) * weight
    out_ref[:channels, :] = moved
    out_ref[channels:, :] = guess
    sent_ref[:channels, :] = moved.astype(jnp.bfloat16)
    sent_ref[channels:, :] = guess.astype(jnp.bfloat16)


def accumulate(parts, offsets, starts, firsts, pieces, before, modulation, last=None):
    rows, width = before.shape
    depth = sum(part.shape[1] for part in parts)
    count = len(pieces)
    splits = [len(piece) for piece in pieces]
    pieces = [array for piece in pieces for array in piece]
    smem = pl.BlockSpec(memory_space=pltpu.SMEM)
    vmem = pl.BlockSpec(memory_space=pltpu.VMEM)
    hbm = pl.BlockSpec(memory_space=pl.ANY)
    scratch = [
        pltpu.VMEM((count, depth, pieces[0].shape[1]), jnp.bfloat16),
        pltpu.VMEM((rows, depth), jnp.bfloat16),
        pltpu.SemaphoreType.DMA((count, len(parts))),
    ]
    params = dict(
        compiler_params=pltpu.CompilerParams(vmem_limit_bytes=52 * MIB),
    )
    if last is None:
        aliased = before.dtype == jnp.float32
        return pl.pallas_call(
            functools.partial(add_kernel, offsets, splits),
            in_specs=[smem] * 2 + [vmem] * len(parts) + [hbm] * len(pieces) + [vmem] * 2,
            out_specs=vmem,
            out_shape=jax.ShapeDtypeStruct((rows, width), jnp.float32),
            scratch_shapes=scratch,
            input_output_aliases={2 + len(parts) + len(pieces): 0} if aliased else {},
            name="add_parts",
            **params,
        )(starts, firsts, *parts, *pieces, before, modulation)
    coef, head, latent, weight = last
    channels = head.shape[0]
    return pl.pallas_call(
        functools.partial(finish_kernel, offsets, splits),
        in_specs=[smem] * 3 + [vmem] * len(parts) + [hbm] * len(pieces) + [vmem] * 5,
        out_specs=[vmem, vmem],
        out_shape=[
            jax.ShapeDtypeStruct((2 * channels, rows), jnp.float32),
            jax.ShapeDtypeStruct((2 * channels, rows), jnp.bfloat16),
        ],
        scratch_shapes=scratch
        + [pltpu.VMEM((rows, width), jnp.float32)],
        name="finish",
        **params,
    )(starts, firsts, coef, *parts, *pieces, before, modulation, head, latent, weight)


def shards(hidden, modulation, w_qkv, w_out, w_head, latent, weights_int, step_index):
    local = hidden[0]
    rows = local.shape[0]
    devices = lax.axis_size("seq")
    tiles = lax.axis_size("tile")
    groups = lax.axis_size("group")
    place, tile, group = lax.axis_index("seq"), lax.axis_index("tile"), lax.axis_index("group")
    far, near = bits_of(tiles)[:-1], bits_of(tiles)[-1]

    weight = weights_int.astype(jnp.float32)
    joins = [
        (t * devices + s, (t + 1) * devices + s - (devices - 2))
        for t in range(tiles - 1)
        for s in range(devices - 2, devices)
    ]
    joins += [
        (t * devices + s, (t - 1) * devices + s + (devices - 2))
        for t in range(1, tiles)
        for s in range(2)
    ]
    norms = weight + lax.ppermute(
        weight.astype(jnp.bfloat16), ("tile", "seq"), joins
    ).astype(jnp.float32)

    height = w_qkv.shape[0]
    ragged = height % HD != 0
    row_starts = jnp.stack([(tile ^ d) * height for d in range(tiles)]).astype(jnp.int32)
    if ragged:
        row_starts = jnp.zeros((1,), jnp.int32)
    normed = norm_rows(local, modulation, row_starts, 0, rows)
    hops = arrivals(devices)
    blocks_by = {0: normed}

    def hop(step):
        for way in (1, -1):
            blocks_by[way * step] = lax.ppermute(
                blocks_by[way * (step - 1)], "seq", step_pairs(devices, step, way)
            )

    def arrival(number):
        wanted = [hops[s][number] for s in range(devices)]
        names = sorted(set(wanted))
        return [names.index(name) for name in wanted], [blocks_by[name] for name in names]

    part = w_out.shape[1] // groups
    share = lax.dynamic_slice_in_dim(w_out, group * part, part, axis=1)
    narrow = part % HD != 0
    columns = {(0, 0): lax.all_gather(share, "seq", axis=0, tiled=True)}

    blocks = {0: w_qkv}
    if not ragged:
        blocks[near] = swap(w_qkv, "tile", near)
        for bit in far:
            blocks.update(
                {d ^ bit: swap(blocks[d], "tile", bit) for d in list(blocks) if d != near}
            )
    hop(1)

    table = [
        [([s] + [s - hop for hop in hops[s]]).index((s + turn) % devices) for turn in range(devices)]
        for s in range(devices)
    ]
    slots = jnp.asarray(table, jnp.int32)[place]
    order = [(d, g) for d in range(tiles) for g in range(groups)]
    starts = jnp.stack(
        [
            (tile ^ d) * (part * groups) + lax.rem(group - g + groups, groups) * part
            for d, g in order
        ]
    ).astype(jnp.int32)
    if narrow:
        order, starts = [(0, 0)], jnp.zeros((1,), jnp.int32)
    features = w_out.shape[0]
    firsts = jnp.stack(
        [lax.rem(place - turn + devices, devices) * features for turn in range(devices)]
    ).astype(jnp.int32)
    index = step_index[0].astype(jnp.float32)
    now = noise_level(index, NSTEPS)
    coef = jnp.stack([now, noise_level(index + 1.0, NSTEPS) - now])
    blocks, columns, blocks_by, slots, starts, firsts, coef, norms = lax.optimization_barrier(
        (blocks, columns, blocks_by, slots, starts, firsts, coef, norms)
    )
    if ragged:
        blocks[0] = lax.all_gather(blocks[0], "tile", axis=0, tiled=True)
    else:
        blocks.update(
            {d ^ near: swap(blocks[d], "tile", near) for d in list(blocks) if d not in (0, near)}
        )
    blocks = [blocks[d] for d in range(len(blocks))]
    if narrow:
        columns[0, 0] = lax.all_gather(columns[0, 0].T, ("tile", "group"), axis=0, tiled=True).T
    else:
        for bit in far:
            columns.update({(d ^ bit, 0): swap(columns[d, 0], "tile", bit) for d, _ in list(columns)})
        for turn in range(1, groups):
            columns[0, turn] = turned(columns[0, 0], "group", turn)

    at = place.reshape(1)
    known, plan, sources = [], [[0] * devices], [normed]
    for number in range(devices - 2):
        if number + 2 < devices:
            hop(number + 2)
        choices, found = arrival(number)
        plan, sources = plan + [choices], sources + found
        known.append(project(at, plan, sources, blocks))
        plan, sources = [], []
        if number + 3 < devices:
            blocks_by, known = lax.optimization_barrier((blocks_by, known))
    if not narrow:
        mine = lax.optimization_barrier((columns[0, 0], known[0]))[0]
        columns[near, 0] = swap(mine, "tile", near)
    columns = {key: [value] for key, value in columns.items()}
    diagonal = groups == 2 and len(far) == 1 and not narrow
    crossing = ()
    if diagonal:
        bit, half = far[0], columns[0, 0][0].shape[0] // 2
        crossing = (columns[bit, 0][0][:half], columns[0, 1][0][half:])
    known, crossing = lax.optimization_barrier((known, crossing))
    late = {}
    if diagonal:
        late[bit, 1] = [turned(crossing[0], "group", 1), swap(crossing[1], "tile", bit)]
    before = early(known, rows)
    blocks_by, known, before, columns = lax.optimization_barrier(
        (blocks_by, known, before, columns)
    )
    if not narrow and not diagonal:
        for turn in range(1, groups):
            for d in range(1, tiles):
                if d & near == 0:
                    late[d, turn] = [turned(columns[d, 0][0], "group", turn)]
    if not narrow:
        columns.update(
            {
                (d ^ near, g): [swap(array, "tile", near) for array in columns[d, g]]
                for d, g in list(columns)
                if (d ^ near, g) not in columns
            }
        )
    heads = w_qkv.shape[1] // (3 * HD)
    many = heads - heads // 2
    halves = [(0, many), (many, heads - many)]
    turns = sorted(range(1, devices), key=lambda turn: -min(turn, devices - turn))
    choices, found = arrival(devices - 2)
    attended = attend(at, slots, [choices], found, known, before, blocks, *halves[0])
    attended, columns, found = lax.optimization_barrier((attended, columns, found))
    received = [[turned(attended[turn], "seq", turn) for turn in turns]]
    own = [attended[0]]
    attended = attend(at, slots, [choices], found, known, before, blocks, *halves[1])
    attended, received, late = lax.optimization_barrier((attended, received, late))
    columns.update(late)
    columns.update(
        {(d ^ near, g): [swap(array, "tile", near) for array in late[d, g]] for d, g in late}
    )
    received.append([turned(attended[turn], "seq", turn) for turn in turns])
    own.append(attended[0])
    pieces = [columns[key] for key in order]
    offsets = [[(turn, start * HD) for turn in turns] for start, _ in halves]
    mixed = accumulate(
        own + received[0],
        [(0, start * HD) for start, _ in halves] + offsets[0],
        starts,
        firsts,
        pieces,
        local,
        modulation,
    )
    weighted, to_join = accumulate(
        received[1],
        offsets[1],
        starts,
        firsts,
        pieces,
        mixed,
        modulation,
        (coef, w_head.T, latent[0].T, weight),
    )
    other = lax.ppermute(to_join, ("tile", "seq"), joins).astype(jnp.float32)
    joined = (weighted + other) / norms
    channels = w_head.shape[1]
    return (joined[:channels].T[None], joined[channels:].T[None])


def solution(mesh):
    in_specs = (
        P(("group", "tile"), "seq", None),
        P("group", None),
        P("tile", "seq"),
        P("seq", "tile"),
        P(),
        P(("group", "tile"), "seq", None),
        P(("group", "tile"), "seq"),
        P("group"),
    )
    out_specs = (P(("group", "tile"), "seq", None), P(("group", "tile"), "seq", None))
    return jax.shard_map(shards, mesh=mesh, in_specs=in_specs, out_specs=out_specs, check_vma=False)
```

```python
import functools
import math

import jax
import jax.numpy as jnp
from jax import lax
from jax.experimental import pallas as pl
from jax.experimental.pallas import tpu as pltpu
from jax.sharding import PartitionSpec as P

HD = 128
NSTEPS = 28
MIB = 1 << 20


def swap(value, axis, bit):
    count = lax.axis_size(axis)
    return lax.ppermute(value, axis, [(i, i ^ bit) for i in range(count)])


def bits_of(count):
    far = [1 << n for n in range(1, count.bit_length() - 1)]
    return far + [1]


def noise_level(index, steps):
    level = 1.0 - index / steps
    return 3.0 * level / (1.0 + 2.0 * level)


def turned(value, axis, turn):
    count = lax.axis_size(axis)
    return lax.ppermute(value, axis, [(i, (i + turn) % count) for i in range(count)])


def step_pairs(count, step, way):
    if way > 0:
        return [(s, s + 1) for s in range(step - 1, count - 1)]
    return [(s, s - 1) for s in range(1, count - step + 1)]


def arrivals(count):
    return [
        sorted((s - home for home in range(count) if home != s), key=lambda hop: (abs(hop), -hop))
        for s in range(count)
    ]


def layer_norm(values):
    mean = jnp.mean(values, axis=-1, keepdims=True)
    centred = values - mean
    spread = jnp.mean(centred * centred, axis=-1, keepdims=True)
    return centred * lax.rsqrt(spread + 1e-06)


def root_norm(values):
    spread = jnp.mean(values * values, axis=-1, keepdims=True)
    return (values * lax.rsqrt(spread + 1e-06)).astype(jnp.bfloat16)


def norm_kernel(blocks, starts_ref, hidden_ref, mod_ref, out_ref):
    local = hidden_ref[...].astype(jnp.float32)
    mean = jnp.mean(local, axis=-1, keepdims=True)
    centred = local - mean
    spread = jnp.mean(centred * centred, axis=-1, keepdims=True)
    scaling = lax.rsqrt(spread + 1e-06)
    width = hidden_ref.shape[1] // blocks
    for n in range(blocks):
        taken = pl.ds(pl.multiple_of(starts_ref[n], HD), width)
        values = (hidden_ref[:, taken].astype(jnp.float32) - mean) * scaling
        values = values * (1.0 + mod_ref[1:2, taken]) + mod_ref[0:1, taken]
        out_ref[:, n * width : (n + 1) * width] = values.astype(jnp.bfloat16)


def norm_rows(hidden, modulation, starts, first, rows):
    width = hidden.shape[1]
    block = math.gcd(math.gcd(first, rows), 64)
    return pl.pallas_call(
        functools.partial(norm_kernel, starts.shape[0]),
        grid=(rows // block,),
        in_specs=[
            pl.BlockSpec(memory_space=pltpu.SMEM),
            pl.BlockSpec((block, width), lambda i: (first // block + i, 0)),
            pl.BlockSpec(modulation.shape, lambda i: (0, 0)),
        ],
        out_specs=pl.BlockSpec((block, width), lambda i: (i, 0)),
        out_shape=jax.ShapeDtypeStruct((rows, width), jnp.bfloat16),
        name="norm_in",
    )(starts, hidden, modulation)


def product(x_ref, blocks):
    height = x_ref.shape[1] // len(blocks)
    total = 0.0
    for n, block in enumerate(blocks):
        total += jnp.dot(
            x_ref[:, n * height : (n + 1) * height],
            block[...],
            preferred_element_type=jnp.float32,
        )
    return total


def load(place, choices, refs, to, sem):
    for n, ref in enumerate(refs):
        wanted = functools.reduce(
            jnp.logical_or, [place == s for s in range(len(choices)) if choices[s] == n]
        )

        @pl.when(wanted)
        def _():
            pltpu.make_async_copy(ref, to, sem).start()

    return pltpu.make_async_copy(refs[0], to, sem)


def load_all(place, plan, refs, tokens, sems):
    rows = tokens.shape[0] // len(plan)
    copies, used = [], 0
    for n, choices in enumerate(plan):
        many = max(choices) + 1
        to = tokens.at[pl.ds(n * rows, rows)]
        copies.append(load(place, choices, refs[used : used + many], to, sems.at[n]))
        used += many
    for copy in copies:
        copy.wait()


def project_kernel(plan, blocks, place_ref, *refs):
    w_refs = refs[:blocks]
    sources, (q_ref, k_ref, v_ref, tokens, sems) = refs[blocks:-5], refs[-5:]

    @pl.when(pl.program_id(0) == 0)
    def _():
        load_all(place_ref[0], plan, sources, tokens, sems)

    proj = product(tokens, w_refs)
    for h in range(q_ref.shape[0]):
        query, key, value = (proj[:, (3 * h + i) * HD : (3 * h + i + 1) * HD] for i in range(3))
        q_ref[h] = root_norm(query)
        k_ref[h] = root_norm(key)
        v_ref[h] = value.astype(jnp.bfloat16)


def project(place, plan, sources, blocks):
    rows, width = sources[0].shape
    length = rows * len(plan)
    total = blocks[0].shape[1]
    heads = total // (3 * HD)
    many = 2 if heads % 2 == 0 else 1
    out = jax.ShapeDtypeStruct((heads, length, HD), jnp.bfloat16)
    return pl.pallas_call(
        functools.partial(project_kernel, plan, len(blocks)),
        grid=(heads // many,),
        in_specs=[pl.BlockSpec(memory_space=pltpu.SMEM)]
        + [pl.BlockSpec((width // len(blocks), many * 3 * HD), lambda h: (0, h))] * len(blocks)
        + [pl.BlockSpec(memory_space=pl.ANY)] * len(sources),
        out_specs=[pl.BlockSpec((many, length, HD), lambda h: (h, 0, 0))] * 3,
        out_shape=[out] * 3,
        scratch_shapes=[
            pltpu.VMEM((length, width), jnp.bfloat16),
            pltpu.SemaphoreType.DMA((len(plan),)),
        ],
        compiler_params=pltpu.CompilerParams(vmem_limit_bytes=42 * MIB),
        name="project",
    )(place, *blocks, *sources)


def weigh(query, key, values):
    scores = lax.dot_general(
        query, key, (((1,), (1,)), ((), ())), preferred_element_type=jnp.float32
    )
    expo = jnp.exp(scores * (1.0 / math.sqrt(HD))).astype(jnp.bfloat16)
    return jnp.dot(expo, values, preferred_element_type=jnp.float32)


def gather_known(known, counts, queries, keys, values):
    at = 0
    for n, count in enumerate(counts):
        queries[at : at + count] = known[3 * n][0]
        keys[at : at + count] = known[3 * n + 1][0]
        values[at : at + count, :HD] = known[3 * n + 2][0]
        at += count


def early_kernel(counts, rows, *refs):
    known, (out_ref, queries, keys, values) = refs[:-4], refs[-4:]

    @pl.when(pl.program_id(0) == 0)
    def _():
        values[:, HD:] = jnp.ones((sum(counts), HD), jnp.bfloat16)

    gather_known(known, counts, queries, keys, values)
    for first in range(0, sum(counts), rows):
        part = slice(first, first + rows)
        out_ref[0, part] = weigh(queries[part], keys[...], values[...]).astype(jnp.bfloat16)


def early(known, rows):
    counts = [three[0].shape[1] for three in known]
    heads, length = known[0][0].shape[0], sum(counts)
    return pl.pallas_call(
        functools.partial(early_kernel, counts, rows),
        grid=(heads,),
        in_specs=[
            pl.BlockSpec((1, count, HD), lambda h: (h, 0, 0)) for count in counts for _ in range(3)
        ],
        out_specs=pl.BlockSpec((1, length, 2 * HD), lambda h: (h, 0, 0)),
        out_shape=jax.ShapeDtypeStruct((heads, length, 2 * HD), jnp.bfloat16),
        scratch_shapes=[
            pltpu.VMEM((length, HD), jnp.bfloat16),
            pltpu.VMEM((length, HD), jnp.bfloat16),
            pltpu.VMEM((length, 2 * HD), jnp.bfloat16),
        ],
        compiler_params=pltpu.CompilerParams(vmem_limit_bytes=42 * MIB),
        name="early",
    )(*(value for three in known for value in three))


def attend_kernel(plan, blocks, counts, place_ref, slots_ref, *refs):
    w_refs, before_ref, refs = refs[:blocks], refs[blocks], refs[blocks + 1 :]
    known, refs = refs[: 3 * len(counts)], refs[3 * len(counts) :]
    queries, keys, values, done, tokens, sems = refs[-6:]
    devices = slots_ref.shape[0]
    sources, outs = refs[: -6 - devices], refs[-6 - devices : -6]
    start, rows = sum(counts), tokens.shape[0]

    @pl.when(pl.program_id(0) == 0)
    def _():
        values[:, HD:] = jnp.ones((start + rows, HD), jnp.bfloat16)
        load_all(place_ref[0], plan, sources, tokens, sems)

    proj = product(tokens, w_refs)
    gather_known(known, counts, queries, keys, values)
    queries[start:] = root_norm(proj[:, :HD])
    keys[start:] = root_norm(proj[:, HD : 2 * HD])
    values[start:, :HD] = proj[:, 2 * HD :].astype(jnp.bfloat16)
    mixed = before_ref[0].astype(jnp.float32)
    mixed += weigh(queries[:start], keys[start:], values[start:])
    done[:start] = (mixed[:, :HD] / mixed[:, HD:]).astype(jnp.bfloat16)
    mixed = weigh(queries[start:], keys[...], values[...])
    done[start:] = (mixed[:, :HD] / mixed[:, HD:]).astype(jnp.bfloat16)
    for turn in range(devices):
        part = pl.ds(pl.multiple_of(slots_ref[turn] * rows, rows), rows)
        outs[turn][...] = done[part]


def attend(place, slots, plan, sources, known, before, blocks, start, heads):
    devices = slots.shape[0]
    rows, width = sources[0].shape
    counts = [three[0].shape[1] for three in known]
    length = rows + sum(counts)
    smem = pl.BlockSpec(memory_space=pltpu.SMEM)
    out = jax.ShapeDtypeStruct((rows, heads * HD), jnp.bfloat16)
    return pl.pallas_call(
        functools.partial(attend_kernel, plan, len(blocks), counts),
        grid=(heads,),
        in_specs=[smem, smem]
        + [pl.BlockSpec((width // len(blocks), 3 * HD), lambda h: (0, start + h))] * len(blocks)
        + [pl.BlockSpec((1, length - rows, 2 * HD), lambda h: (start + h, 0, 0))]
        + [
            pl.BlockSpec((1, count, HD), lambda h: (start + h, 0, 0))
            for count in counts
            for _ in range(3)
        ]
        + [pl.BlockSpec(memory_space=pl.ANY)] * len(sources),
        out_specs=[pl.BlockSpec((rows, HD), lambda h: (0, h))] * devices,
        out_shape=[out] * devices,
        scratch_shapes=[
            pltpu.VMEM((length, HD), jnp.bfloat16),
            pltpu.VMEM((length, HD), jnp.bfloat16),
            pltpu.VMEM((length, 2 * HD), jnp.bfloat16),
            pltpu.VMEM((length, HD), jnp.bfloat16),
            pltpu.VMEM((rows, width), jnp.bfloat16),
            pltpu.SemaphoreType.DMA((1,)),
        ],
        compiler_params=pltpu.CompilerParams(vmem_limit_bytes=42 * MIB),
        name="attend",
    )(place, slots, *blocks, before, *(value for three in known for value in three), *sources)


def multiply(parts, offsets, starts_ref, rows_ref, sources, weights, sems, wide, store):
    depth = [part.shape[1] for part in parts]
    width = weights.shape[2]
    copies = []
    for p, split in enumerate(sources):
        copies.append([])
        for n, (turn, offset) in enumerate(offsets):
            to = weights.at[p, pl.ds(sum(depth[:n]), depth[n])]
            row = rows_ref[turn] + offset
            size = split[0].shape[0]
            for i, source in enumerate(split):
                if len(split) == 1:
                    rows = source.at[pl.ds(pl.multiple_of(row, HD), depth[n])]
                    pltpu.make_async_copy(rows, to, sems.at[p, n]).start()
                    continue

                @pl.when(jnp.logical_and(row >= i * size, row < (i + 1) * size))
                def _():
                    rows = source.at[pl.ds(pl.multiple_of(row - i * size, HD), depth[n])]
                    pltpu.make_async_copy(rows, to, sems.at[p, n]).start()

            rows = split[0].at[pl.ds(0, depth[n])]
            copies[p].append(pltpu.make_async_copy(rows, to, sems.at[p, n]))
    for n, part in enumerate(parts):
        wide[:, sum(depth[:n]) : sum(depth[: n + 1])] = part[...]
    for p in range(len(sources)):
        for copy in copies[p]:
            copy.wait()
        cols = pl.ds(pl.multiple_of(starts_ref[p], HD), width)
        store(p, cols, jnp.dot(wide[...], weights[p], preferred_element_type=jnp.float32))


def split_refs(refs, splits):
    grouped = []
    for split in splits:
        grouped.append(refs[:split])
        refs = refs[split:]
    return grouped, refs


def add_kernel(offsets, splits, starts_ref, rows_ref, *refs):
    parts = refs[: len(offsets)]
    sources, refs = split_refs(refs[len(offsets) :], splits)
    before_ref, mod_ref, out_ref, weights, wide, sems = refs

    def store(p, cols, summed):
        out_ref[:, cols] = before_ref[:, cols].astype(jnp.float32) + mod_ref[2:3, cols] * summed

    multiply(parts, offsets, starts_ref, rows_ref, sources, weights, sems, wide, store)


def finish_kernel(offsets, splits, starts_ref, rows_ref, coef_ref, *refs):
    parts = refs[: len(offsets)]
    sources, refs = split_refs(refs[len(offsets) :], splits)
    before_ref, mod_ref, head_ref, latent_ref, weight_ref = refs[:5]
    moved_ref, guess_ref, sent_ref, weights, wide, sems, mixed = refs[5:]
    count = len(splits)
    width = weights.shape[2]
    held = {}

    def store(p, cols, summed):
        values = before_ref[:, cols] + mod_ref[2:3, cols] * summed
        mixed[:, cols] = values
        if p == 0:
            held["base"] = jnp.mean(values, axis=-1, keepdims=True)
        away = values - held["base"]
        sums = (
            jnp.sum(away, axis=-1, keepdims=True),
            jnp.sum(away * away, axis=-1, keepdims=True),
        )
        held["sums"] = [a + b for a, b in zip(held.get("sums", (0.0, 0.0)), sums)]

    multiply(parts, offsets, starts_ref, rows_ref, sources, weights, sems, wide, store)
    total = width * count
    shift = held["sums"][0] / total
    scaling = lax.rsqrt(held["sums"][1] / total - shift * shift + 1e-06)
    mean = held["base"] + shift
    velocity = 0.0
    for p in range(count):
        cols = slice(p * width, (p + 1) * width)
        normed = (mixed[:, cols] - mean) * scaling
        normed = normed * (1.0 + mod_ref[4:5, cols]) + mod_ref[3:4, cols]
        velocity += lax.dot_general(
            normed.astype(jnp.bfloat16),
            head_ref[:, cols],
            (((1,), (1,)), ((), ())),
            preferred_element_type=jnp.float32,
        )
    velocity = velocity.T
    channels = velocity.shape[0]
    base, weight = latent_ref[...], weight_ref[...]
    moved = (base + coef_ref[1] * velocity) * weight
    guess = (base - coef_ref[0] * velocity) * weight
    moved_ref[...] = moved
    guess_ref[...] = guess
    sent_ref[:channels, :] = moved.astype(jnp.bfloat16)
    sent_ref[channels:, :] = guess.astype(jnp.bfloat16)


def accumulate(parts, offsets, starts, firsts, pieces, before, modulation, last=None):
    rows, width = before.shape
    depth = sum(part.shape[1] for part in parts)
    count = len(pieces)
    splits = [len(piece) for piece in pieces]
    pieces = [array for piece in pieces for array in piece]
    smem = pl.BlockSpec(memory_space=pltpu.SMEM)
    vmem = pl.BlockSpec(memory_space=pltpu.VMEM)
    hbm = pl.BlockSpec(memory_space=pl.ANY)
    scratch = [
        pltpu.VMEM((count, depth, pieces[0].shape[1]), jnp.bfloat16),
        pltpu.VMEM((rows, depth), jnp.bfloat16),
        pltpu.SemaphoreType.DMA((count, len(parts))),
    ]
    params = dict(
        compiler_params=pltpu.CompilerParams(vmem_limit_bytes=52 * MIB),
    )
    if last is None:
        aliased = before.dtype == jnp.float32
        return pl.pallas_call(
            functools.partial(add_kernel, offsets, splits),
            in_specs=[smem] * 2 + [vmem] * len(parts) + [hbm] * len(pieces) + [vmem] * 2,
            out_specs=vmem,
            out_shape=jax.ShapeDtypeStruct((rows, width), jnp.float32),
            scratch_shapes=scratch,
            input_output_aliases={2 + len(parts) + len(pieces): 0} if aliased else {},
            name="add_parts",
            **params,
        )(starts, firsts, *parts, *pieces, before, modulation)
    coef, head, latent, weight = last
    channels = head.shape[0]
    return pl.pallas_call(
        functools.partial(finish_kernel, offsets, splits),
        in_specs=[smem] * 3 + [vmem] * len(parts) + [hbm] * len(pieces) + [vmem] * 5,
        out_specs=[vmem] * 3,
        out_shape=[
            jax.ShapeDtypeStruct((channels, rows), jnp.float32),
            jax.ShapeDtypeStruct((channels, rows), jnp.float32),
            jax.ShapeDtypeStruct((2 * channels, rows), jnp.bfloat16),
        ],
        scratch_shapes=scratch
        + [pltpu.VMEM((rows, width), jnp.float32)],
        name="finish",
        **params,
    )(starts, firsts, coef, *parts, *pieces, before, modulation, head, latent, weight)


def shards(hidden, modulation, w_qkv, w_out, w_head, latent, weights_int, step_index):
    local = hidden[0]
    rows = local.shape[0]
    devices = lax.axis_size("seq")
    tiles = lax.axis_size("tile")
    groups = lax.axis_size("group")
    place, tile, group = lax.axis_index("seq"), lax.axis_index("tile"), lax.axis_index("group")
    far, near = bits_of(tiles)[:-1], bits_of(tiles)[-1]

    weight = weights_int.astype(jnp.float32)
    joins = [
        (t * devices + s, (t + 1) * devices + s - (devices - 2))
        for t in range(tiles - 1)
        for s in range(devices - 2, devices)
    ]
    joins += [
        (t * devices + s, (t - 1) * devices + s + (devices - 2))
        for t in range(1, tiles)
        for s in range(2)
    ]
    norms = weight + lax.ppermute(
        weight.astype(jnp.bfloat16), ("tile", "seq"), joins
    ).astype(jnp.float32)

    height = w_qkv.shape[0]
    ragged = height % HD != 0
    row_starts = jnp.stack([(tile ^ d) * height for d in range(tiles)]).astype(jnp.int32)
    if ragged:
        row_starts = jnp.zeros((1,), jnp.int32)
    normed = norm_rows(local, modulation, row_starts, 0, rows)
    hops = arrivals(devices)
    blocks_by = {0: normed}

    def hop(step):
        for way in (1, -1):
            blocks_by[way * step] = lax.ppermute(
                blocks_by[way * (step - 1)], "seq", step_pairs(devices, step, way)
            )

    def arrival(number):
        wanted = [hops[s][number] for s in range(devices)]
        names = sorted(set(wanted))
        return [names.index(name) for name in wanted], [blocks_by[name] for name in names]

    part = w_out.shape[1] // groups
    share = lax.dynamic_slice_in_dim(w_out, group * part, part, axis=1)
    narrow = part % HD != 0
    columns = {(0, 0): lax.all_gather(share, "seq", axis=0, tiled=True)}

    blocks = {0: w_qkv}
    if not ragged:
        blocks[near] = swap(w_qkv, "tile", near)
        for bit in far:
            blocks.update(
                {d ^ bit: swap(blocks[d], "tile", bit) for d in list(blocks) if d != near}
            )
    hop(1)

    table = [
        [([s] + [s - hop for hop in hops[s]]).index((s + turn) % devices) for turn in range(devices)]
        for s in range(devices)
    ]
    slots = jnp.asarray(table, jnp.int32)[place]
    order = [(d, g) for d in range(tiles) for g in range(groups)]
    starts = jnp.stack(
        [
            (tile ^ d) * (part * groups) + lax.rem(group - g + groups, groups) * part
            for d, g in order
        ]
    ).astype(jnp.int32)
    if narrow:
        order, starts = [(0, 0)], jnp.zeros((1,), jnp.int32)
    features = w_out.shape[0]
    firsts = jnp.stack(
        [lax.rem(place - turn + devices, devices) * features for turn in range(devices)]
    ).astype(jnp.int32)
    index = step_index[0].astype(jnp.float32)
    now = noise_level(index, NSTEPS)
    coef = jnp.stack([now, noise_level(index + 1.0, NSTEPS) - now])
    blocks, columns, blocks_by, slots, starts, firsts, coef, norms = lax.optimization_barrier(
        (blocks, columns, blocks_by, slots, starts, firsts, coef, norms)
    )
    if ragged:
        blocks[0] = lax.all_gather(blocks[0], "tile", axis=0, tiled=True)
    else:
        blocks.update(
            {d ^ near: swap(blocks[d], "tile", near) for d in list(blocks) if d not in (0, near)}
        )
    blocks = [blocks[d] for d in range(len(blocks))]
    if narrow:
        columns[0, 0] = lax.all_gather(columns[0, 0].T, ("tile", "group"), axis=0, tiled=True).T
    else:
        for bit in far:
            columns.update({(d ^ bit, 0): swap(columns[d, 0], "tile", bit) for d, _ in list(columns)})
        for turn in range(1, groups):
            columns[0, turn] = turned(columns[0, 0], "group", turn)

    at = place.reshape(1)
    known, plan, sources = [], [[0] * devices], [normed]
    for number in range(devices - 2):
        if number + 2 < devices:
            hop(number + 2)
        choices, found = arrival(number)
        plan, sources = plan + [choices], sources + found
        known.append(project(at, plan, sources, blocks))
        plan, sources = [], []
        if number + 3 < devices:
            blocks_by, known = lax.optimization_barrier((blocks_by, known))
    if not narrow:
        mine = lax.optimization_barrier((columns[0, 0], known[0]))[0]
        columns[near, 0] = swap(mine, "tile", near)
    columns = {key: [value] for key, value in columns.items()}
    diagonal = groups == 2 and len(far) == 1 and not narrow
    crossing = ()
    if diagonal:
        bit, half = far[0], columns[0, 0][0].shape[0] // 2
        crossing = (columns[bit, 0][0][:half], columns[0, 1][0][half:])
    known, crossing = lax.optimization_barrier((known, crossing))
    late = {}
    if diagonal:
        late[bit, 1] = [turned(crossing[0], "group", 1), swap(crossing[1], "tile", bit)]
    before = early(known, rows)
    blocks_by, known, before, columns = lax.optimization_barrier(
        (blocks_by, known, before, columns)
    )
    if not narrow and not diagonal:
        for turn in range(1, groups):
            for d in range(1, tiles):
                if d & near == 0:
                    late[d, turn] = [turned(columns[d, 0][0], "group", turn)]
    if not narrow:
        columns.update(
            {
                (d ^ near, g): [swap(array, "tile", near) for array in columns[d, g]]
                for d, g in list(columns)
                if (d ^ near, g) not in columns
            }
        )
    heads = w_qkv.shape[1] // (3 * HD)
    many = heads - heads // 2
    halves = [(0, many), (many, heads - many)]
    turns = sorted(range(1, devices), key=lambda turn: -min(turn, devices - turn))
    choices, found = arrival(devices - 2)
    attended = attend(at, slots, [choices], found, known, before, blocks, *halves[0])
    attended, columns, found = lax.optimization_barrier((attended, columns, found))
    received = [[turned(attended[turn], "seq", turn) for turn in turns]]
    own = [attended[0]]
    attended = attend(at, slots, [choices], found, known, before, blocks, *halves[1])
    attended, received, late = lax.optimization_barrier((attended, received, late))
    columns.update(late)
    columns.update(
        {(d ^ near, g): [swap(array, "tile", near) for array in late[d, g]] for d, g in late}
    )
    received.append([turned(attended[turn], "seq", turn) for turn in turns])
    own.append(attended[0])
    pieces = [columns[key] for key in order]
    offsets = [[(turn, start * HD) for turn in turns] for start, _ in halves]
    mixed = accumulate(
        own + received[0],
        [(0, start * HD) for start, _ in halves] + offsets[0],
        starts,
        firsts,
        pieces,
        local,
        modulation,
    )
    moved, guess, to_join = accumulate(
        received[1],
        offsets[1],
        starts,
        firsts,
        pieces,
        mixed,
        modulation,
        (coef, w_head.T, latent[0].T, weight),
    )
    other = lax.ppermute(to_join, ("tile", "seq"), joins).astype(jnp.float32)
    channels = w_head.shape[1]
    stepped = (moved + other[:channels]) / norms
    clean = (guess + other[channels:]) / norms
    return (stepped.T[None], clean.T[None])


def solution(mesh):
    in_specs = (
        P(("group", "tile"), "seq", None),
        P("group", None),
        P("tile", "seq"),
        P("seq", "tile"),
        P(),
        P(("group", "tile"), "seq", None),
        P(("group", "tile"), "seq"),
        P("group"),
    )
    out_specs = (P(("group", "tile"), "seq", None), P(("group", "tile"), "seq", None))
    return jax.shard_map(shards, mesh=mesh, in_specs=in_specs, out_specs=out_specs, check_vma=False)
```

```python
import functools
import math

import jax
import jax.numpy as jnp
from jax import lax
from jax.experimental import pallas as pl
from jax.experimental.pallas import tpu as pltpu
from jax.sharding import PartitionSpec as P

HD = 128
NSTEPS = 28
MIB = 1 << 20


def swap(value, axis, bit):
    count = lax.axis_size(axis)
    return lax.ppermute(value, axis, [(i, i ^ bit) for i in range(count)])


def bits_of(count):
    far = [1 << n for n in range(1, count.bit_length() - 1)]
    return far + [1]


def noise_level(index, steps):
    level = 1.0 - index / steps
    return 3.0 * level / (1.0 + 2.0 * level)


def turned(value, axis, turn):
    count = lax.axis_size(axis)
    return lax.ppermute(value, axis, [(i, (i + turn) % count) for i in range(count)])


def step_pairs(count, step, way):
    if way > 0:
        return [(s, s + 1) for s in range(step - 1, count - 1)]
    return [(s, s - 1) for s in range(1, count - step + 1)]


def arrivals(count):
    return [
        sorted((s - home for home in range(count) if home != s), key=lambda hop: (abs(hop), -hop))
        for s in range(count)
    ]


def layer_norm(values):
    mean = jnp.mean(values, axis=-1, keepdims=True)
    centred = values - mean
    spread = jnp.mean(centred * centred, axis=-1, keepdims=True)
    return centred * lax.rsqrt(spread + 1e-06)


def root_norm(values):
    spread = jnp.mean(values * values, axis=-1, keepdims=True)
    return (values * lax.rsqrt(spread + 1e-06)).astype(jnp.bfloat16)


def norm_kernel(blocks, starts_ref, hidden_ref, mod_ref, out_ref):
    local = hidden_ref[...].astype(jnp.float32)
    mean = jnp.mean(local, axis=-1, keepdims=True)
    centred = local - mean
    spread = jnp.mean(centred * centred, axis=-1, keepdims=True)
    scaling = lax.rsqrt(spread + 1e-06)
    width = hidden_ref.shape[1] // blocks
    for n in range(blocks):
        taken = pl.ds(pl.multiple_of(starts_ref[n], HD), width)
        values = (hidden_ref[:, taken].astype(jnp.float32) - mean) * scaling
        values = values * (1.0 + mod_ref[1:2, taken]) + mod_ref[0:1, taken]
        out_ref[:, n * width : (n + 1) * width] = values.astype(jnp.bfloat16)


def norm_rows(hidden, modulation, starts, first, rows):
    width = hidden.shape[1]
    block = math.gcd(math.gcd(first, rows), 64)
    return pl.pallas_call(
        functools.partial(norm_kernel, starts.shape[0]),
        grid=(rows // block,),
        in_specs=[
            pl.BlockSpec(memory_space=pltpu.SMEM),
            pl.BlockSpec((block, width), lambda i: (first // block + i, 0)),
            pl.BlockSpec(modulation.shape, lambda i: (0, 0)),
        ],
        out_specs=pl.BlockSpec((block, width), lambda i: (i, 0)),
        out_shape=jax.ShapeDtypeStruct((rows, width), jnp.bfloat16),
        name="norm_in",
    )(starts, hidden, modulation)


def product(x_ref, blocks):
    height = x_ref.shape[1] // len(blocks)
    total = 0.0
    for n, block in enumerate(blocks):
        total += jnp.dot(
            x_ref[:, n * height : (n + 1) * height],
            block[...],
            preferred_element_type=jnp.float32,
        )
    return total


def load(place, choices, refs, to, sem):
    for n, ref in enumerate(refs):
        wanted = functools.reduce(
            jnp.logical_or, [place == s for s in range(len(choices)) if choices[s] == n]
        )

        @pl.when(wanted)
        def _():
            pltpu.make_async_copy(ref, to, sem).start()

    return pltpu.make_async_copy(refs[0], to, sem)


def start_all(place, plan, refs, tokens, sems):
    rows = tokens.shape[0] // len(plan)
    copies, used = [], 0
    for n, choices in enumerate(plan):
        many = max(choices) + 1
        to = tokens.at[pl.ds(n * rows, rows)]
        copies.append(load(place, choices, refs[used : used + many], to, sems.at[n]))
        used += many
    return copies


def load_all(*args):
    for copy in start_all(*args):
        copy.wait()


def project_kernel(plan, blocks, place_ref, *refs):
    w_refs = refs[:blocks]
    sources, (q_ref, k_ref, v_ref, tokens, sems) = refs[blocks:-5], refs[-5:]

    @pl.when(pl.program_id(0) == 0)
    def _():
        load_all(place_ref[0], plan, sources, tokens, sems)

    proj = product(tokens, w_refs)
    for h in range(q_ref.shape[0]):
        query, key, value = (proj[:, (3 * h + i) * HD : (3 * h + i + 1) * HD] for i in range(3))
        q_ref[h] = root_norm(query)
        k_ref[h] = root_norm(key)
        v_ref[h] = value.astype(jnp.bfloat16)


def project(place, plan, sources, blocks):
    rows, width = sources[0].shape
    length = rows * len(plan)
    total = blocks[0].shape[1]
    heads = total // (3 * HD)
    many = 2 if heads % 2 == 0 else 1
    out = jax.ShapeDtypeStruct((heads, length, HD), jnp.bfloat16)
    return pl.pallas_call(
        functools.partial(project_kernel, plan, len(blocks)),
        grid=(heads // many,),
        in_specs=[pl.BlockSpec(memory_space=pltpu.SMEM)]
        + [pl.BlockSpec((width // len(blocks), many * 3 * HD), lambda h: (0, h))] * len(blocks)
        + [pl.BlockSpec(memory_space=pl.ANY)] * len(sources),
        out_specs=[pl.BlockSpec((many, length, HD), lambda h: (h, 0, 0))] * 3,
        out_shape=[out] * 3,
        scratch_shapes=[
            pltpu.VMEM((length, width), jnp.bfloat16),
            pltpu.SemaphoreType.DMA((len(plan),)),
        ],
        compiler_params=pltpu.CompilerParams(vmem_limit_bytes=42 * MIB),
        name="project",
    )(place, *blocks, *sources)


def weigh(query, key, values):
    scores = lax.dot_general(
        query, key, (((1,), (1,)), ((), ())), preferred_element_type=jnp.float32
    )
    expo = jnp.exp(scores * (1.0 / math.sqrt(HD))).astype(jnp.bfloat16)
    return jnp.dot(expo, values, preferred_element_type=jnp.float32)


def gather_known(known, counts, queries, keys, values):
    at = 0
    for n, count in enumerate(counts):
        queries[at : at + count] = known[3 * n][0]
        keys[at : at + count] = known[3 * n + 1][0]
        values[at : at + count, :HD] = known[3 * n + 2][0]
        at += count


def early_kernel(counts, rows, *refs):
    known, (out_ref, queries, keys, values) = refs[:-4], refs[-4:]

    @pl.when(pl.program_id(0) == 0)
    def _():
        values[:, HD:] = jnp.ones((sum(counts), HD), jnp.bfloat16)

    gather_known(known, counts, queries, keys, values)
    for first in range(0, sum(counts), rows):
        part = slice(first, first + rows)
        out_ref[0, part] = weigh(queries[part], keys[...], values[...]).astype(jnp.bfloat16)


def early(known, rows):
    counts = [three[0].shape[1] for three in known]
    heads, length = known[0][0].shape[0], sum(counts)
    return pl.pallas_call(
        functools.partial(early_kernel, counts, rows),
        grid=(heads,),
        in_specs=[
            pl.BlockSpec((1, count, HD), lambda h: (h, 0, 0)) for count in counts for _ in range(3)
        ],
        out_specs=pl.BlockSpec((1, length, 2 * HD), lambda h: (h, 0, 0)),
        out_shape=jax.ShapeDtypeStruct((heads, length, 2 * HD), jnp.bfloat16),
        scratch_shapes=[
            pltpu.VMEM((length, HD), jnp.bfloat16),
            pltpu.VMEM((length, HD), jnp.bfloat16),
            pltpu.VMEM((length, 2 * HD), jnp.bfloat16),
        ],
        compiler_params=pltpu.CompilerParams(vmem_limit_bytes=42 * MIB),
        name="early",
    )(*(value for three in known for value in three))


def attend_kernel(plan, blocks, counts, place_ref, slots_ref, *refs):
    w_refs, before_ref, refs = refs[:blocks], refs[blocks], refs[blocks + 1 :]
    known, refs = refs[: 3 * len(counts)], refs[3 * len(counts) :]
    queries, keys, values, done, tokens, sems = refs[-6:]
    devices = slots_ref.shape[0]
    sources, outs = refs[: -6 - devices], refs[-6 - devices : -6]
    start, rows = sum(counts), tokens.shape[0]

    @pl.when(pl.program_id(0) == 0)
    def _():
        copies = start_all(place_ref[0], plan, sources, tokens, sems)
        values[:, HD:] = jnp.ones((start + rows, HD), jnp.bfloat16)
        gather_known(known, counts, queries, keys, values)
        for copy in copies:
            copy.wait()

    @pl.when(pl.program_id(0) != 0)
    def _():
        gather_known(known, counts, queries, keys, values)

    proj = product(tokens, w_refs)
    queries[start:] = root_norm(proj[:, :HD])
    keys[start:] = root_norm(proj[:, HD : 2 * HD])
    values[start:, :HD] = proj[:, 2 * HD :].astype(jnp.bfloat16)
    mixed = before_ref[0].astype(jnp.float32)
    mixed += weigh(queries[:start], keys[start:], values[start:])
    done[:start] = (mixed[:, :HD] / mixed[:, HD:]).astype(jnp.bfloat16)
    mixed = weigh(queries[start:], keys[...], values[...])
    done[start:] = (mixed[:, :HD] / mixed[:, HD:]).astype(jnp.bfloat16)
    for turn in range(devices):
        part = pl.ds(pl.multiple_of(slots_ref[turn] * rows, rows), rows)
        outs[turn][...] = done[part]


def attend(place, slots, plan, sources, known, before, blocks, start, heads):
    devices = slots.shape[0]
    rows, width = sources[0].shape
    counts = [three[0].shape[1] for three in known]
    length = rows + sum(counts)
    smem = pl.BlockSpec(memory_space=pltpu.SMEM)
    out = jax.ShapeDtypeStruct((rows, heads * HD), jnp.bfloat16)
    return pl.pallas_call(
        functools.partial(attend_kernel, plan, len(blocks), counts),
        grid=(heads,),
        in_specs=[smem, smem]
        + [pl.BlockSpec((width // len(blocks), 3 * HD), lambda h: (0, start + h))] * len(blocks)
        + [pl.BlockSpec((1, length - rows, 2 * HD), lambda h: (start + h, 0, 0))]
        + [
            pl.BlockSpec((1, count, HD), lambda h: (start + h, 0, 0))
            for count in counts
            for _ in range(3)
        ]
        + [pl.BlockSpec(memory_space=pl.ANY)] * len(sources),
        out_specs=[pl.BlockSpec((rows, HD), lambda h: (0, h))] * devices,
        out_shape=[out] * devices,
        scratch_shapes=[
            pltpu.VMEM((length, HD), jnp.bfloat16),
            pltpu.VMEM((length, HD), jnp.bfloat16),
            pltpu.VMEM((length, 2 * HD), jnp.bfloat16),
            pltpu.VMEM((length, HD), jnp.bfloat16),
            pltpu.VMEM((rows, width), jnp.bfloat16),
            pltpu.SemaphoreType.DMA((1,)),
        ],
        compiler_params=pltpu.CompilerParams(vmem_limit_bytes=42 * MIB),
        name="attend",
    )(place, slots, *blocks, before, *(value for three in known for value in three), *sources)


def multiply(parts, offsets, starts_ref, rows_ref, sources, weights, sems, wide, store):
    depth = [part.shape[1] for part in parts]
    width = weights.shape[2]
    copies = []
    for p, split in enumerate(sources):
        copies.append([])
        for n, (turn, offset) in enumerate(offsets):
            to = weights.at[p, pl.ds(sum(depth[:n]), depth[n])]
            row = rows_ref[turn] + offset
            size = split[0].shape[0]
            for i, source in enumerate(split):
                if len(split) == 1:
                    rows = source.at[pl.ds(pl.multiple_of(row, HD), depth[n])]
                    pltpu.make_async_copy(rows, to, sems.at[p, n]).start()
                    continue

                @pl.when(jnp.logical_and(row >= i * size, row < (i + 1) * size))
                def _():
                    rows = source.at[pl.ds(pl.multiple_of(row - i * size, HD), depth[n])]
                    pltpu.make_async_copy(rows, to, sems.at[p, n]).start()

            rows = split[0].at[pl.ds(0, depth[n])]
            copies[p].append(pltpu.make_async_copy(rows, to, sems.at[p, n]))
    for n, part in enumerate(parts):
        wide[:, sum(depth[:n]) : sum(depth[: n + 1])] = part[...]
    for p in range(len(sources)):
        for copy in copies[p]:
            copy.wait()
        cols = pl.ds(pl.multiple_of(starts_ref[p], HD), width)
        store(p, cols, jnp.dot(wide[...], weights[p], preferred_element_type=jnp.float32))


def split_refs(refs, splits):
    grouped = []
    for split in splits:
        grouped.append(refs[:split])
        refs = refs[split:]
    return grouped, refs


def add_kernel(offsets, splits, starts_ref, rows_ref, *refs):
    parts = refs[: len(offsets)]
    sources, refs = split_refs(refs[len(offsets) :], splits)
    before_ref, mod_ref, out_ref, weights, wide, sems = refs

    def store(p, cols, summed):
        out_ref[:, cols] = before_ref[:, cols].astype(jnp.float32) + mod_ref[2:3, cols] * summed

    multiply(parts, offsets, starts_ref, rows_ref, sources, weights, sems, wide, store)


def finish_kernel(offsets, splits, starts_ref, rows_ref, coef_ref, *refs):
    parts = refs[: len(offsets)]
    sources, refs = split_refs(refs[len(offsets) :], splits)
    before_ref, mod_ref, head_ref, latent_ref, weight_ref = refs[:5]
    moved_ref, guess_ref, sent_ref, weights, wide, sems, mixed = refs[5:]
    count = len(splits)
    width = weights.shape[2]
    held = {}

    def store(p, cols, summed):
        values = before_ref[:, cols] + mod_ref[2:3, cols] * summed
        mixed[:, cols] = values
        if p == 0:
            held["base"] = jnp.mean(values, axis=-1, keepdims=True)
        away = values - held["base"]
        sums = (
            jnp.sum(away, axis=-1, keepdims=True),
            jnp.sum(away * away, axis=-1, keepdims=True),
        )
        held["sums"] = [a + b for a, b in zip(held.get("sums", (0.0, 0.0)), sums)]

    multiply(parts, offsets, starts_ref, rows_ref, sources, weights, sems, wide, store)
    total = width * count
    shift = held["sums"][0] / total
    scaling = lax.rsqrt(held["sums"][1] / total - shift * shift + 1e-06)
    mean = held["base"] + shift
    velocity = 0.0
    for p in range(count):
        cols = slice(p * width, (p + 1) * width)
        normed = (mixed[:, cols] - mean) * scaling
        normed = normed * (1.0 + mod_ref[4:5, cols]) + mod_ref[3:4, cols]
        velocity += lax.dot_general(
            normed.astype(jnp.bfloat16),
            head_ref[:, cols],
            (((1,), (1,)), ((), ())),
            preferred_element_type=jnp.float32,
        )
    velocity = velocity.T
    channels = velocity.shape[0]
    base, weight = latent_ref[...], weight_ref[...]
    moved = (base + coef_ref[1] * velocity) * weight
    guess = (base - coef_ref[0] * velocity) * weight
    moved_ref[...] = moved
    guess_ref[...] = guess
    sent_ref[:channels, :] = moved.astype(jnp.bfloat16)
    sent_ref[channels:, :] = guess.astype(jnp.bfloat16)


def accumulate(parts, offsets, starts, firsts, pieces, before, modulation, last=None):
    rows, width = before.shape
    depth = sum(part.shape[1] for part in parts)
    count = len(pieces)
    splits = [len(piece) for piece in pieces]
    pieces = [array for piece in pieces for array in piece]
    smem = pl.BlockSpec(memory_space=pltpu.SMEM)
    vmem = pl.BlockSpec(memory_space=pltpu.VMEM)
    hbm = pl.BlockSpec(memory_space=pl.ANY)
    scratch = [
        pltpu.VMEM((count, depth, pieces[0].shape[1]), jnp.bfloat16),
        pltpu.VMEM((rows, depth), jnp.bfloat16),
        pltpu.SemaphoreType.DMA((count, len(parts))),
    ]
    params = dict(
        compiler_params=pltpu.CompilerParams(vmem_limit_bytes=48 * MIB),
    )
    if last is None:
        aliased = before.dtype == jnp.float32
        return pl.pallas_call(
            functools.partial(add_kernel, offsets, splits),
            in_specs=[smem] * 2 + [vmem] * len(parts) + [hbm] * len(pieces) + [vmem] * 2,
            out_specs=vmem,
            out_shape=jax.ShapeDtypeStruct((rows, width), jnp.float32),
            scratch_shapes=scratch,
            input_output_aliases={2 + len(parts) + len(pieces): 0} if aliased else {},
            name="add_parts",
            **params,
        )(starts, firsts, *parts, *pieces, before, modulation)
    coef, head, latent, weight = last
    channels = head.shape[0]
    return pl.pallas_call(
        functools.partial(finish_kernel, offsets, splits),
        in_specs=[smem] * 3 + [vmem] * len(parts) + [hbm] * len(pieces) + [vmem] * 5,
        out_specs=[vmem] * 3,
        out_shape=[
            jax.ShapeDtypeStruct((channels, rows), jnp.float32),
            jax.ShapeDtypeStruct((channels, rows), jnp.float32),
            jax.ShapeDtypeStruct((2 * channels, rows), jnp.bfloat16),
        ],
        scratch_shapes=scratch
        + [pltpu.VMEM((rows, width), jnp.float32)],
        name="finish",
        **params,
    )(starts, firsts, coef, *parts, *pieces, before, modulation, head, latent, weight)


def shards(hidden, modulation, w_qkv, w_out, w_head, latent, weights_int, step_index):
    local = hidden[0]
    rows = local.shape[0]
    devices = lax.axis_size("seq")
    tiles = lax.axis_size("tile")
    groups = lax.axis_size("group")
    place, tile, group = lax.axis_index("seq"), lax.axis_index("tile"), lax.axis_index("group")
    far, near = bits_of(tiles)[:-1], bits_of(tiles)[-1]

    weight = weights_int.astype(jnp.float32)
    joins = [
        (t * devices + s, (t + 1) * devices + s - (devices - 2))
        for t in range(tiles - 1)
        for s in range(devices - 2, devices)
    ]
    joins += [
        (t * devices + s, (t - 1) * devices + s + (devices - 2))
        for t in range(1, tiles)
        for s in range(2)
    ]
    norms = weight + lax.ppermute(
        weight.astype(jnp.bfloat16), ("tile", "seq"), joins
    ).astype(jnp.float32)

    height = w_qkv.shape[0]
    ragged = height % HD != 0
    row_starts = jnp.stack([(tile ^ d) * height for d in range(tiles)]).astype(jnp.int32)
    if ragged:
        row_starts = jnp.zeros((1,), jnp.int32)
    normed = norm_rows(local, modulation, row_starts, 0, rows)
    hops = arrivals(devices)
    blocks_by = {0: normed}

    def hop(step):
        for way in (1, -1):
            blocks_by[way * step] = lax.ppermute(
                blocks_by[way * (step - 1)], "seq", step_pairs(devices, step, way)
            )

    def arrival(number):
        wanted = [hops[s][number] for s in range(devices)]
        names = sorted(set(wanted))
        return [names.index(name) for name in wanted], [blocks_by[name] for name in names]

    part = w_out.shape[1] // groups
    share = lax.dynamic_slice_in_dim(w_out, group * part, part, axis=1)
    narrow = part % HD != 0
    columns = {(0, 0): lax.all_gather(share, "seq", axis=0, tiled=True)}

    blocks = {0: w_qkv}
    if not ragged:
        blocks[near] = swap(w_qkv, "tile", near)
        for bit in far:
            blocks.update(
                {d ^ bit: swap(blocks[d], "tile", bit) for d in list(blocks) if d != near}
            )
    hop(1)

    table = [
        [([s] + [s - hop for hop in hops[s]]).index((s + turn) % devices) for turn in range(devices)]
        for s in range(devices)
    ]
    slots = jnp.asarray(table, jnp.int32)[place]
    order = [(d, g) for d in range(tiles) for g in range(groups)]
    starts = jnp.stack(
        [
            (tile ^ d) * (part * groups) + lax.rem(group - g + groups, groups) * part
            for d, g in order
        ]
    ).astype(jnp.int32)
    if narrow:
        order, starts = [(0, 0)], jnp.zeros((1,), jnp.int32)
    features = w_out.shape[0]
    firsts = jnp.stack(
        [lax.rem(place - turn + devices, devices) * features for turn in range(devices)]
    ).astype(jnp.int32)
    index = step_index[0].astype(jnp.float32)
    now = noise_level(index, NSTEPS)
    coef = jnp.stack([now, noise_level(index + 1.0, NSTEPS) - now])
    blocks, columns, blocks_by, slots, starts, firsts, coef, norms = lax.optimization_barrier(
        (blocks, columns, blocks_by, slots, starts, firsts, coef, norms)
    )
    if ragged:
        blocks[0] = lax.all_gather(blocks[0], "tile", axis=0, tiled=True)
    else:
        blocks.update(
            {d ^ near: swap(blocks[d], "tile", near) for d in list(blocks) if d not in (0, near)}
        )
    blocks = [blocks[d] for d in range(len(blocks))]
    if narrow:
        columns[0, 0] = lax.all_gather(columns[0, 0].T, ("tile", "group"), axis=0, tiled=True).T
    else:
        for bit in far:
            columns.update({(d ^ bit, 0): swap(columns[d, 0], "tile", bit) for d, _ in list(columns)})
        for turn in range(1, groups):
            columns[0, turn] = turned(columns[0, 0], "group", turn)

    at = place.reshape(1)
    known, plan, sources = [], [[0] * devices], [normed]
    for number in range(devices - 2):
        if number + 2 < devices:
            hop(number + 2)
        choices, found = arrival(number)
        plan, sources = plan + [choices], sources + found
        known.append(project(at, plan, sources, blocks))
        plan, sources = [], []
        if number + 3 < devices:
            blocks_by, known = lax.optimization_barrier((blocks_by, known))
    if not narrow:
        mine = lax.optimization_barrier((columns[0, 0], known[0]))[0]
        columns[near, 0] = swap(mine, "tile", near)
    columns = {key: [value] for key, value in columns.items()}
    diagonal = groups == 2 and len(far) == 1 and not narrow
    crossing = ()
    if diagonal:
        bit, half = far[0], columns[0, 0][0].shape[0] // 2
        crossing = (columns[bit, 0][0][:half], columns[0, 1][0][half:])
    known, crossing = lax.optimization_barrier((known, crossing))
    late = {}
    if diagonal:
        late[bit, 1] = [turned(crossing[0], "group", 1), swap(crossing[1], "tile", bit)]
    before = early(known, rows)
    blocks_by, known, before, columns = lax.optimization_barrier(
        (blocks_by, known, before, columns)
    )
    if not narrow and not diagonal:
        for turn in range(1, groups):
            for d in range(1, tiles):
                if d & near == 0:
                    late[d, turn] = [turned(columns[d, 0][0], "group", turn)]
    if not narrow:
        columns.update(
            {
                (d ^ near, g): [swap(array, "tile", near) for array in columns[d, g]]
                for d, g in list(columns)
                if (d ^ near, g) not in columns
            }
        )
    heads = w_qkv.shape[1] // (3 * HD)
    many = heads - heads // 2
    halves = [(0, many), (many, heads - many)]
    turns = sorted(range(1, devices), key=lambda turn: -min(turn, devices - turn))
    choices, found = arrival(devices - 2)
    attended = attend(at, slots, [choices], found, known, before, blocks, *halves[0])
    attended, columns, found = lax.optimization_barrier((attended, columns, found))
    received = [[turned(attended[turn], "seq", turn) for turn in turns]]
    own = [attended[0]]
    attended = attend(at, slots, [choices], found, known, before, blocks, *halves[1])
    attended, received, late = lax.optimization_barrier((attended, received, late))
    columns.update(late)
    columns.update(
        {(d ^ near, g): [swap(array, "tile", near) for array in late[d, g]] for d, g in late}
    )
    received.append([turned(attended[turn], "seq", turn) for turn in turns])
    own.append(attended[0])
    pieces = [columns[key] for key in order]
    offsets = [[(turn, start * HD) for turn in turns] for start, _ in halves]
    mixed = accumulate(
        own + received[0],
        [(0, start * HD) for start, _ in halves] + offsets[0],
        starts,
        firsts,
        pieces,
        local,
        modulation,
    )
    moved, guess, to_join = accumulate(
        received[1],
        offsets[1],
        starts,
        firsts,
        pieces,
        mixed,
        modulation,
        (coef, w_head.T, latent[0].T, weight),
    )
    other = lax.ppermute(to_join, ("tile", "seq"), joins).astype(jnp.float32)
    channels = w_head.shape[1]
    stepped = (moved + other[:channels]) / norms
    clean = (guess + other[channels:]) / norms
    return (stepped.T[None], clean.T[None])


def solution(mesh):
    in_specs = (
        P(("group", "tile"), "seq", None),
        P("group", None),
        P("tile", "seq"),
        P("seq", "tile"),
        P(),
        P(("group", "tile"), "seq", None),
        P(("group", "tile"), "seq"),
        P("group"),
    )
    out_specs = (P(("group", "tile"), "seq", None), P(("group", "tile"), "seq", None))
    return jax.shard_map(shards, mesh=mesh, in_specs=in_specs, out_specs=out_specs, check_vma=False)
```

```python
import functools
import math

import jax
import jax.numpy as jnp
from jax import lax
from jax.experimental import pallas as pl
from jax.experimental.pallas import tpu as pltpu
from jax.sharding import PartitionSpec as P

HD = 128
NSTEPS = 28
MIB = 1 << 20


def swap(value, axis, bit):
    count = lax.axis_size(axis)
    return lax.ppermute(value, axis, [(i, i ^ bit) for i in range(count)])


def bits_of(count):
    far = [1 << n for n in range(1, count.bit_length() - 1)]
    return far + [1]


def noise_level(index, steps):
    level = 1.0 - index / steps
    return 3.0 * level / (1.0 + 2.0 * level)


def turned(value, axis, turn):
    count = lax.axis_size(axis)
    return lax.ppermute(value, axis, [(i, (i + turn) % count) for i in range(count)])


def step_pairs(count, step, way):
    if way > 0:
        return [(s, s + 1) for s in range(step - 1, count - 1)]
    return [(s, s - 1) for s in range(1, count - step + 1)]


def arrivals(count):
    return [
        sorted((s - home for home in range(count) if home != s), key=lambda hop: (abs(hop), -hop))
        for s in range(count)
    ]


def layer_norm(values):
    mean = jnp.mean(values, axis=-1, keepdims=True)
    centred = values - mean
    spread = jnp.mean(centred * centred, axis=-1, keepdims=True)
    return centred * lax.rsqrt(spread + 1e-06)


def root_norm(values):
    spread = jnp.mean(values * values, axis=-1, keepdims=True)
    return (values * lax.rsqrt(spread + 1e-06)).astype(jnp.bfloat16)


def norm_kernel(blocks, starts_ref, hidden_ref, mod_ref, out_ref):
    local = hidden_ref[...].astype(jnp.float32)
    mean = jnp.mean(local, axis=-1, keepdims=True)
    centred = local - mean
    spread = jnp.mean(centred * centred, axis=-1, keepdims=True)
    scaling = lax.rsqrt(spread + 1e-06)
    width = hidden_ref.shape[1] // blocks
    for n in range(blocks):
        taken = pl.ds(pl.multiple_of(starts_ref[n], HD), width)
        values = (hidden_ref[:, taken].astype(jnp.float32) - mean) * scaling
        values = values * (1.0 + mod_ref[1:2, taken]) + mod_ref[0:1, taken]
        out_ref[:, n * width : (n + 1) * width] = values.astype(jnp.bfloat16)


def norm_rows(hidden, modulation, starts, first, rows):
    width = hidden.shape[1]
    block = math.gcd(math.gcd(first, rows), 128)
    return pl.pallas_call(
        functools.partial(norm_kernel, starts.shape[0]),
        grid=(rows // block,),
        in_specs=[
            pl.BlockSpec(memory_space=pltpu.SMEM),
            pl.BlockSpec((block, width), lambda i: (first // block + i, 0)),
            pl.BlockSpec(modulation.shape, lambda i: (0, 0)),
        ],
        out_specs=pl.BlockSpec((block, width), lambda i: (i, 0)),
        out_shape=jax.ShapeDtypeStruct((rows, width), jnp.bfloat16),
        name="norm_in",
    )(starts, hidden, modulation)


def product(x_ref, blocks):
    height = x_ref.shape[1] // len(blocks)
    total = 0.0
    for n, block in enumerate(blocks):
        total += jnp.dot(
            x_ref[:, n * height : (n + 1) * height],
            block[...],
            preferred_element_type=jnp.float32,
        )
    return total


def load(place, choices, refs, to, sem):
    for n, ref in enumerate(refs):
        wanted = functools.reduce(
            jnp.logical_or, [place == s for s in range(len(choices)) if choices[s] == n]
        )

        @pl.when(wanted)
        def _():
            pltpu.make_async_copy(ref, to, sem).start()

    return pltpu.make_async_copy(refs[0], to, sem)


def start_all(place, plan, refs, tokens, sems):
    rows = tokens.shape[0] // len(plan)
    copies, used = [], 0
    for n, choices in enumerate(plan):
        many = max(choices) + 1
        to = tokens.at[pl.ds(n * rows, rows)]
        copies.append(load(place, choices, refs[used : used + many], to, sems.at[n]))
        used += many
    return copies


def load_all(*args):
    for copy in start_all(*args):
        copy.wait()


def project_kernel(plan, blocks, place_ref, *refs):
    w_refs = refs[:blocks]
    sources, (q_ref, k_ref, v_ref, tokens, sems) = refs[blocks:-5], refs[-5:]

    @pl.when(pl.program_id(0) == 0)
    def _():
        load_all(place_ref[0], plan, sources, tokens, sems)

    proj = product(tokens, w_refs)
    for h in range(q_ref.shape[0]):
        query, key, value = (proj[:, (3 * h + i) * HD : (3 * h + i + 1) * HD] for i in range(3))
        q_ref[h] = root_norm(query)
        k_ref[h] = root_norm(key)
        v_ref[h] = value.astype(jnp.bfloat16)


def project(place, plan, sources, blocks):
    rows, width = sources[0].shape
    length = rows * len(plan)
    total = blocks[0].shape[1]
    heads = total // (3 * HD)
    many = 2 if heads % 2 == 0 else 1
    out = jax.ShapeDtypeStruct((heads, length, HD), jnp.bfloat16)
    return pl.pallas_call(
        functools.partial(project_kernel, plan, len(blocks)),
        grid=(heads // many,),
        in_specs=[pl.BlockSpec(memory_space=pltpu.SMEM)]
        + [pl.BlockSpec((width // len(blocks), many * 3 * HD), lambda h: (0, h))] * len(blocks)
        + [pl.BlockSpec(memory_space=pl.ANY)] * len(sources),
        out_specs=[pl.BlockSpec((many, length, HD), lambda h: (h, 0, 0))] * 3,
        out_shape=[out] * 3,
        scratch_shapes=[
            pltpu.VMEM((length, width), jnp.bfloat16),
            pltpu.SemaphoreType.DMA((len(plan),)),
        ],
        compiler_params=pltpu.CompilerParams(vmem_limit_bytes=42 * MIB),
        name="project",
    )(place, *blocks, *sources)


def weigh(query, key, values):
    scores = lax.dot_general(
        query, key, (((1,), (1,)), ((), ())), preferred_element_type=jnp.float32
    )
    expo = jnp.exp2(scores * (math.log2(math.e) / math.sqrt(HD))).astype(jnp.bfloat16)
    return jnp.dot(expo, values, preferred_element_type=jnp.float32)


def gather_known(known, counts, queries, keys, values):
    at = 0
    for n, count in enumerate(counts):
        queries[at : at + count] = known[3 * n][0]
        keys[at : at + count] = known[3 * n + 1][0]
        values[at : at + count, :HD] = known[3 * n + 2][0]
        at += count


def early_kernel(counts, rows, *refs):
    known, (out_ref, queries, keys, values) = refs[:-4], refs[-4:]

    @pl.when(pl.program_id(0) == 0)
    def _():
        values[:, HD:] = jnp.ones((sum(counts), HD), jnp.bfloat16)

    gather_known(known, counts, queries, keys, values)
    for first in range(0, sum(counts), rows):
        part = slice(first, first + rows)
        out_ref[0, part] = weigh(queries[part], keys[...], values[...]).astype(jnp.bfloat16)


def early(known, rows):
    counts = [three[0].shape[1] for three in known]
    heads, length = known[0][0].shape[0], sum(counts)
    return pl.pallas_call(
        functools.partial(early_kernel, counts, rows),
        grid=(heads,),
        in_specs=[
            pl.BlockSpec((1, count, HD), lambda h: (h, 0, 0)) for count in counts for _ in range(3)
        ],
        out_specs=pl.BlockSpec((1, length, 2 * HD), lambda h: (h, 0, 0)),
        out_shape=jax.ShapeDtypeStruct((heads, length, 2 * HD), jnp.bfloat16),
        scratch_shapes=[
            pltpu.VMEM((length, HD), jnp.bfloat16),
            pltpu.VMEM((length, HD), jnp.bfloat16),
            pltpu.VMEM((length, 2 * HD), jnp.bfloat16),
        ],
        compiler_params=pltpu.CompilerParams(vmem_limit_bytes=42 * MIB),
        name="early",
    )(*(value for three in known for value in three))


def attend_kernel(plan, blocks, counts, place_ref, slots_ref, *refs):
    w_refs, before_ref, refs = refs[:blocks], refs[blocks], refs[blocks + 1 :]
    known, refs = refs[: 3 * len(counts)], refs[3 * len(counts) :]
    queries, keys, values, done, tokens, sems = refs[-6:]
    devices = slots_ref.shape[0]
    sources, outs = refs[: -6 - devices], refs[-6 - devices : -6]
    start, rows = sum(counts), tokens.shape[0]

    @pl.when(pl.program_id(0) == 0)
    def _():
        copies = start_all(place_ref[0], plan, sources, tokens, sems)
        values[:, HD:] = jnp.ones((start + rows, HD), jnp.bfloat16)
        gather_known(known, counts, queries, keys, values)
        for copy in copies:
            copy.wait()

    @pl.when(pl.program_id(0) != 0)
    def _():
        gather_known(known, counts, queries, keys, values)

    proj = product(tokens, w_refs)
    queries[start:] = root_norm(proj[:, :HD])
    keys[start:] = root_norm(proj[:, HD : 2 * HD])
    values[start:, :HD] = proj[:, 2 * HD :].astype(jnp.bfloat16)
    mixed = before_ref[0].astype(jnp.float32)
    mixed += weigh(queries[:start], keys[start:], values[start:])
    done[:start] = (mixed[:, :HD] / mixed[:, HD:]).astype(jnp.bfloat16)
    mixed = weigh(queries[start:], keys[...], values[...])
    done[start:] = (mixed[:, :HD] / mixed[:, HD:]).astype(jnp.bfloat16)
    for turn in range(devices):
        part = pl.ds(pl.multiple_of(slots_ref[turn] * rows, rows), rows)
        outs[turn][...] = done[part]


def attend(place, slots, plan, sources, known, before, blocks, start, heads):
    devices = slots.shape[0]
    rows, width = sources[0].shape
    counts = [three[0].shape[1] for three in known]
    length = rows + sum(counts)
    smem = pl.BlockSpec(memory_space=pltpu.SMEM)
    out = jax.ShapeDtypeStruct((rows, heads * HD), jnp.bfloat16)
    return pl.pallas_call(
        functools.partial(attend_kernel, plan, len(blocks), counts),
        grid=(heads,),
        in_specs=[smem, smem]
        + [pl.BlockSpec((width // len(blocks), 3 * HD), lambda h: (0, start + h))] * len(blocks)
        + [pl.BlockSpec((1, length - rows, 2 * HD), lambda h: (start + h, 0, 0))]
        + [
            pl.BlockSpec((1, count, HD), lambda h: (start + h, 0, 0))
            for count in counts
            for _ in range(3)
        ]
        + [pl.BlockSpec(memory_space=pl.ANY)] * len(sources),
        out_specs=[pl.BlockSpec((rows, HD), lambda h: (0, h))] * devices,
        out_shape=[out] * devices,
        scratch_shapes=[
            pltpu.VMEM((length, HD), jnp.bfloat16),
            pltpu.VMEM((length, HD), jnp.bfloat16),
            pltpu.VMEM((length, 2 * HD), jnp.bfloat16),
            pltpu.VMEM((length, HD), jnp.bfloat16),
            pltpu.VMEM((rows, width), jnp.bfloat16),
            pltpu.SemaphoreType.DMA((1,)),
        ],
        compiler_params=pltpu.CompilerParams(vmem_limit_bytes=42 * MIB),
        name="attend",
    )(place, slots, *blocks, before, *(value for three in known for value in three), *sources)


def multiply(parts, offsets, starts_ref, rows_ref, sources, weights, sems, wide, store):
    depth = [part.shape[1] for part in parts]
    width = weights.shape[2]
    copies = []
    for p, split in enumerate(sources):
        copies.append([])
        for n, (turn, offset) in enumerate(offsets):
            to = weights.at[p, pl.ds(sum(depth[:n]), depth[n])]
            row = rows_ref[turn] + offset
            size = split[0].shape[0]
            for i, source in enumerate(split):
                if len(split) == 1:
                    rows = source.at[pl.ds(pl.multiple_of(row, HD), depth[n])]
                    pltpu.make_async_copy(rows, to, sems.at[p, n]).start()
                    continue

                @pl.when(jnp.logical_and(row >= i * size, row < (i + 1) * size))
                def _():
                    rows = source.at[pl.ds(pl.multiple_of(row - i * size, HD), depth[n])]
                    pltpu.make_async_copy(rows, to, sems.at[p, n]).start()

            rows = split[0].at[pl.ds(0, depth[n])]
            copies[p].append(pltpu.make_async_copy(rows, to, sems.at[p, n]))
    for n, part in enumerate(parts):
        wide[:, sum(depth[:n]) : sum(depth[: n + 1])] = part[...]
    for p in range(len(sources)):
        for copy in copies[p]:
            copy.wait()
        cols = pl.ds(pl.multiple_of(starts_ref[p], HD), width)
        store(p, cols, jnp.dot(wide[...], weights[p], preferred_element_type=jnp.float32))


def split_refs(refs, splits):
    grouped = []
    for split in splits:
        grouped.append(refs[:split])
        refs = refs[split:]
    return grouped, refs


def add_kernel(offsets, splits, starts_ref, rows_ref, *refs):
    parts = refs[: len(offsets)]
    sources, refs = split_refs(refs[len(offsets) :], splits)
    before_ref, mod_ref, out_ref, weights, wide, sems = refs

    def store(p, cols, summed):
        out_ref[:, cols] = before_ref[:, cols].astype(jnp.float32) + mod_ref[2:3, cols] * summed

    multiply(parts, offsets, starts_ref, rows_ref, sources, weights, sems, wide, store)


def finish_kernel(offsets, splits, starts_ref, rows_ref, coef_ref, *refs):
    parts = refs[: len(offsets)]
    sources, refs = split_refs(refs[len(offsets) :], splits)
    before_ref, mod_ref, head_ref, latent_ref, weight_ref = refs[:5]
    moved_ref, guess_ref, sent_ref, weights, wide, sems, mixed = refs[5:]
    count = len(splits)
    width = weights.shape[2]
    held = {}

    def store(p, cols, summed):
        values = before_ref[:, cols] + mod_ref[2:3, cols] * summed
        mixed[:, cols] = values
        if p == 0:
            held["base"] = jnp.mean(values, axis=-1, keepdims=True)
        away = values - held["base"]
        sums = (
            jnp.sum(away, axis=-1, keepdims=True),
            jnp.sum(away * away, axis=-1, keepdims=True),
        )
        held["sums"] = [a + b for a, b in zip(held.get("sums", (0.0, 0.0)), sums)]

    multiply(parts, offsets, starts_ref, rows_ref, sources, weights, sems, wide, store)
    total = width * count
    shift = held["sums"][0] / total
    scaling = lax.rsqrt(held["sums"][1] / total - shift * shift + 1e-06)
    mean = held["base"] + shift
    velocity = 0.0
    for p in range(count):
        cols = slice(p * width, (p + 1) * width)
        normed = (mixed[:, cols] - mean) * scaling
        normed = normed * (1.0 + mod_ref[4:5, cols]) + mod_ref[3:4, cols]
        velocity += lax.dot_general(
            normed.astype(jnp.bfloat16),
            head_ref[:, cols],
            (((1,), (1,)), ((), ())),
            preferred_element_type=jnp.float32,
        )
    velocity = velocity.T
    channels = velocity.shape[0]
    base, weight = latent_ref[...], weight_ref[...]
    moved = (base + coef_ref[1] * velocity) * weight
    guess = (base - coef_ref[0] * velocity) * weight
    moved_ref[...] = moved
    guess_ref[...] = guess
    sent_ref[:channels, :] = moved.astype(jnp.bfloat16)
    sent_ref[channels:, :] = guess.astype(jnp.bfloat16)


def accumulate(parts, offsets, starts, firsts, pieces, before, modulation, last=None):
    rows, width = before.shape
    depth = sum(part.shape[1] for part in parts)
    count = len(pieces)
    splits = [len(piece) for piece in pieces]
    pieces = [array for piece in pieces for array in piece]
    smem = pl.BlockSpec(memory_space=pltpu.SMEM)
    vmem = pl.BlockSpec(memory_space=pltpu.VMEM)
    hbm = pl.BlockSpec(memory_space=pl.ANY)
    scratch = [
        pltpu.VMEM((count, depth, pieces[0].shape[1]), jnp.bfloat16),
        pltpu.VMEM((rows, depth), jnp.bfloat16),
        pltpu.SemaphoreType.DMA((count, len(parts))),
    ]
    params = dict(
        compiler_params=pltpu.CompilerParams(vmem_limit_bytes=48 * MIB),
    )
    if last is None:
        aliased = before.dtype == jnp.float32
        return pl.pallas_call(
            functools.partial(add_kernel, offsets, splits),
            in_specs=[smem] * 2 + [vmem] * len(parts) + [hbm] * len(pieces) + [vmem] * 2,
            out_specs=vmem,
            out_shape=jax.ShapeDtypeStruct((rows, width), jnp.float32),
            scratch_shapes=scratch,
            input_output_aliases={2 + len(parts) + len(pieces): 0} if aliased else {},
            name="add_parts",
            **params,
        )(starts, firsts, *parts, *pieces, before, modulation)
    coef, head, latent, weight = last
    channels = head.shape[0]
    return pl.pallas_call(
        functools.partial(finish_kernel, offsets, splits),
        in_specs=[smem] * 3 + [vmem] * len(parts) + [hbm] * len(pieces) + [vmem] * 5,
        out_specs=[vmem] * 3,
        out_shape=[
            jax.ShapeDtypeStruct((channels, rows), jnp.float32),
            jax.ShapeDtypeStruct((channels, rows), jnp.float32),
            jax.ShapeDtypeStruct((2 * channels, rows), jnp.bfloat16),
        ],
        scratch_shapes=scratch
        + [pltpu.VMEM((rows, width), jnp.float32)],
        name="finish",
        **params,
    )(starts, firsts, coef, *parts, *pieces, before, modulation, head, latent, weight)


def shards(hidden, modulation, w_qkv, w_out, w_head, latent, weights_int, step_index):
    local = hidden[0]
    rows = local.shape[0]
    devices = lax.axis_size("seq")
    tiles = lax.axis_size("tile")
    groups = lax.axis_size("group")
    place, tile, group = lax.axis_index("seq"), lax.axis_index("tile"), lax.axis_index("group")
    far, near = bits_of(tiles)[:-1], bits_of(tiles)[-1]

    weight = weights_int.astype(jnp.float32)
    joins = [
        (t * devices + s, (t + 1) * devices + s - (devices - 2))
        for t in range(tiles - 1)
        for s in range(devices - 2, devices)
    ]
    joins += [
        (t * devices + s, (t - 1) * devices + s + (devices - 2))
        for t in range(1, tiles)
        for s in range(2)
    ]
    norms = weight + lax.ppermute(
        weight.astype(jnp.bfloat16), ("tile", "seq"), joins
    ).astype(jnp.float32)

    height = w_qkv.shape[0]
    ragged = height % HD != 0
    row_starts = jnp.stack([(tile ^ d) * height for d in range(tiles)]).astype(jnp.int32)
    if ragged:
        row_starts = jnp.zeros((1,), jnp.int32)
    normed = norm_rows(local, modulation, row_starts, 0, rows)
    hops = arrivals(devices)
    blocks_by = {0: normed}

    def hop(step):
        for way in (1, -1):
            blocks_by[way * step] = lax.ppermute(
                blocks_by[way * (step - 1)], "seq", step_pairs(devices, step, way)
            )

    def arrival(number):
        wanted = [hops[s][number] for s in range(devices)]
        names = sorted(set(wanted))
        return [names.index(name) for name in wanted], [blocks_by[name] for name in names]

    part = w_out.shape[1] // groups
    share = lax.dynamic_slice_in_dim(w_out, group * part, part, axis=1)
    narrow = part % HD != 0
    columns = {(0, 0): lax.all_gather(share, "seq", axis=0, tiled=True)}

    blocks = {0: w_qkv}
    if not ragged:
        blocks[near] = swap(w_qkv, "tile", near)
        for bit in far:
            blocks.update(
                {d ^ bit: swap(blocks[d], "tile", bit) for d in list(blocks) if d != near}
            )
    hop(1)

    table = [
        [([s] + [s - hop for hop in hops[s]]).index((s + turn) % devices) for turn in range(devices)]
        for s in range(devices)
    ]
    slots = jnp.asarray(table, jnp.int32)[place]
    order = [(d, g) for d in range(tiles) for g in range(groups)]
    starts = jnp.stack(
        [
            (tile ^ d) * (part * groups) + lax.rem(group - g + groups, groups) * part
            for d, g in order
        ]
    ).astype(jnp.int32)
    if narrow:
        order, starts = [(0, 0)], jnp.zeros((1,), jnp.int32)
    features = w_out.shape[0]
    firsts = jnp.stack(
        [lax.rem(place - turn + devices, devices) * features for turn in range(devices)]
    ).astype(jnp.int32)
    index = step_index[0].astype(jnp.float32)
    now = noise_level(index, NSTEPS)
    coef = jnp.stack([now, noise_level(index + 1.0, NSTEPS) - now])
    blocks, columns, blocks_by, slots, starts, firsts, coef, norms = lax.optimization_barrier(
        (blocks, columns, blocks_by, slots, starts, firsts, coef, norms)
    )
    if ragged:
        blocks[0] = lax.all_gather(blocks[0], "tile", axis=0, tiled=True)
    else:
        blocks.update(
            {d ^ near: swap(blocks[d], "tile", near) for d in list(blocks) if d not in (0, near)}
        )
    blocks = [blocks[d] for d in range(len(blocks))]
    if narrow:
        columns[0, 0] = lax.all_gather(columns[0, 0].T, ("tile", "group"), axis=0, tiled=True).T
    else:
        for bit in far:
            columns.update({(d ^ bit, 0): swap(columns[d, 0], "tile", bit) for d, _ in list(columns)})
        for turn in range(1, groups):
            columns[0, turn] = turned(columns[0, 0], "group", turn)

    at = place.reshape(1)
    known, plan, sources = [], [[0] * devices], [normed]
    for number in range(devices - 2):
        if number + 2 < devices:
            hop(number + 2)
        choices, found = arrival(number)
        plan, sources = plan + [choices], sources + found
        known.append(project(at, plan, sources, blocks))
        plan, sources = [], []
        if number + 3 < devices:
            blocks_by, known = lax.optimization_barrier((blocks_by, known))
    if not narrow:
        mine = lax.optimization_barrier((columns[0, 0], known[0]))[0]
        columns[near, 0] = swap(mine, "tile", near)
    columns = {key: [value] for key, value in columns.items()}
    diagonal = groups == 2 and len(far) == 1 and not narrow
    crossing = ()
    if diagonal:
        bit, half = far[0], columns[0, 0][0].shape[0] // 2
        crossing = (columns[bit, 0][0][:half], columns[0, 1][0][half:])
    known, crossing = lax.optimization_barrier((known, crossing))
    late = {}
    if diagonal:
        late[bit, 1] = [turned(crossing[0], "group", 1), swap(crossing[1], "tile", bit)]
    before = early(known, rows)
    blocks_by, known, before, columns = lax.optimization_barrier(
        (blocks_by, known, before, columns)
    )
    if not narrow and not diagonal:
        for turn in range(1, groups):
            for d in range(1, tiles):
                if d & near == 0:
                    late[d, turn] = [turned(columns[d, 0][0], "group", turn)]
    if not narrow:
        columns.update(
            {
                (d ^ near, g): [swap(array, "tile", near) for array in columns[d, g]]
                for d, g in list(columns)
                if (d ^ near, g) not in columns
            }
        )
    heads = w_qkv.shape[1] // (3 * HD)
    many = heads - heads // 2
    halves = [(0, many), (many, heads - many)]
    turns = sorted(range(1, devices), key=lambda turn: -min(turn, devices - turn))
    choices, found = arrival(devices - 2)
    attended = attend(at, slots, [choices], found, known, before, blocks, *halves[0])
    attended, columns, found = lax.optimization_barrier((attended, columns, found))
    received = [[turned(attended[turn], "seq", turn) for turn in turns]]
    own = [attended[0]]
    attended = attend(at, slots, [choices], found, known, before, blocks, *halves[1])
    attended, received, late = lax.optimization_barrier((attended, received, late))
    columns.update(late)
    columns.update(
        {(d ^ near, g): [swap(array, "tile", near) for array in late[d, g]] for d, g in late}
    )
    received.append([turned(attended[turn], "seq", turn) for turn in turns])
    own.append(attended[0])
    pieces = [columns[key] for key in order]
    offsets = [[(turn, start * HD) for turn in turns] for start, _ in halves]
    mixed = accumulate(
        own + received[0],
        [(0, start * HD) for start, _ in halves] + offsets[0],
        starts,
        firsts,
        pieces,
        local,
        modulation,
    )
    moved, guess, to_join = accumulate(
        received[1],
        offsets[1],
        starts,
        firsts,
        pieces,
        mixed,
        modulation,
        (coef, w_head.T, latent[0].T, weight),
    )
    other = lax.ppermute(to_join, ("tile", "seq"), joins).astype(jnp.float32)
    channels = w_head.shape[1]
    stepped = (moved + other[:channels]) / norms
    clean = (guess + other[channels:]) / norms
    return (stepped.T[None], clean.T[None])


def solution(mesh):
    in_specs = (
        P(("group", "tile"), "seq", None),
        P("group", None),
        P("tile", "seq"),
        P("seq", "tile"),
        P(),
        P(("group", "tile"), "seq", None),
        P(("group", "tile"), "seq"),
        P("group"),
    )
    out_specs = (P(("group", "tile"), "seq", None), P(("group", "tile"), "seq", None))
    return jax.shard_map(shards, mesh=mesh, in_specs=in_specs, out_specs=out_specs, check_vma=False)
```
